32 devices in a mesh: dp: 2 (over y), row: 4 (over z), col: 4 (over x, core).
Axes of the slice: x: 2, y: 2, z: 4, core: 2. Of those that a mesh axis runs over, the one named last changes fastest.
Arguments:
- layer_in: bfloat16 [8280, 4, 384], P(('dp', 'col'), 'row'), may hold values from -6 to 6
- grad_out: bfloat16 [8280, 4, 384], P(('dp', 'col'), 'row'), may hold values from -6 to 6
- crop_ids: int32 [16560], P(('dp', 'row')), may hold values from 0 to 239, as said below
- w_qkv: float32 [768, 3, 768], P(('row', 'dp'), None, 'col'), may hold values from -0.21875 to 0.21875
- w_out: float32 [768, 768], P(('col', 'dp'), 'row'), may hold values from -1 to 1
- w_fc1: float32 [768, 3072], P(('row', 'dp'), 'col'), may hold values from -0.21875 to 0.21875
- w_fc2: float32 [3072, 768], P(('col', 'dp'), 'row'), may hold values from -0.109375 to 0.109375
- norm_gains: float32 [1536], replicated, may hold values from 0.4 to 2
- all_biases: float32 [7680], replicated, may hold values from -1.5 to 1.5
- first_qkv: float32 [768, 3, 768], P(('row', 'dp'), None, 'col'), may hold values from -0.0022538076 to 0.0022538076
- second_qkv: float32 [768, 3, 768], P(('row', 'dp'), None, 'col'), may hold values from 7.0550676e-08 to 1.1288108e-06
- first_out: float32 [768, 768], P(('col', 'dp'), 'row'), may hold values from -0.0022538076 to 0.0022538076
- second_out: float32 [768, 768], P(('col', 'dp'), 'row'), may hold values from 7.0550676e-08 to 1.1288108e-06
- first_fc1: float32 [768, 3072], P(('row', 'dp'), 'col'), may hold values from -0.0022538076 to 0.0022538076
- second_fc1: float32 [768, 3072], P(('row', 'dp'), 'col'), may hold values from 7.0550676e-08 to 1.1288108e-06
- first_fc2: float32 [3072, 768], P(('col', 'dp'), 'row'), may hold values from -0.0022538076 to 0.0022538076
- second_fc2: float32 [3072, 768], P(('col', 'dp'), 'row'), may hold values from 7.0550676e-08 to 1.1288108e-06
- first_gains: float32 [1536], replicated, may hold values from -0.0022538076 to 0.0022538076
- second_gains: float32 [1536], replicated, may hold values from 7.0550676e-08 to 1.1288108e-06
- first_biases: float32 [7680], replicated, may hold values from -0.0022538076 to 0.0022538076
- second_biases: float32 [7680], replicated, may hold values from 7.0550676e-08 to 1.1288108e-06
Outputs:
- layer_out: float32 [8280, 4, 384], P(('dp', 'col'), 'row')
- grad_in: float32 [8280, 4, 384], P(('dp', 'col'), 'row')
- grad_norm: float32 [], replicated
- new_first_qkv: float32 [768, 3, 768], P(('row', 'dp'), None, 'col')
- new_second_qkv: float32 [768, 3, 768], P(('row', 'dp'), None, 'col')
- new_w_qkv: float32 [768, 3, 768], P(('row', 'dp'), None, 'col')
- half_w_qkv: bfloat16 [768, 3, 768], P(('row', 'dp'), None, 'col')
- new_first_out: float32 [768, 768], P(('col', 'dp'), 'row')
- new_second_out: float32 [768, 768], P(('col', 'dp'), 'row')
- new_w_out: float32 [768, 768], P(('col', 'dp'), 'row')
- half_w_out: bfloat16 [768, 768], P(('col', 'dp'), 'row')
- new_first_fc1: float32 [768, 3072], P(('row', 'dp'), 'col')
- new_second_fc1: float32 [768, 3072], P(('row', 'dp'), 'col')
- new_w_fc1: float32 [768, 3072], P(('row', 'dp'), 'col')
- half_w_fc1: bfloat16 [768, 3072], P(('row', 'dp'), 'col')
- new_first_fc2: float32 [3072, 768], P(('col', 'dp'), 'row')
- new_second_fc2: float32 [3072, 768], P(('col', 'dp'), 'row')
- new_w_fc2: float32 [3072, 768], P(('col', 'dp'), 'row')
- half_w_fc2: bfloat16 [3072, 768], P(('col', 'dp'), 'row')
- new_first_gains: float32 [1536], replicated
- new_second_gains: float32 [1536], replicated
- new_gains: float32 [1536], replicated
- half_gains: bfloat16 [1536], replicated
- new_first_biases: float32 [7680], replicated
- new_second_biases: float32 [7680], replicated
- new_biases: float32 [7680], replicated
- half_biases: bfloat16 [7680], replicated
The draws below stay inside these ranges and needn't reach their ends.
Inputs may be any that keep to these rules, and one draw needn't show every extreme that they name: `crop_ids`: tokens come in images of 690 consecutive positions starting at multiples of 690; each image holds 2 crops of 197 tokens and 8 crops of 37 tokens, each crop's tokens consecutive, in an order that varies from image to image; a token's value is its image's index times 10 plus its crop's place within the image.
All inputs are finite; a program needn't handle non-finite values.
Results may differ from the reference program's by a relative error of at most 0.019.
Values may be sent and summed in bfloat16 or wider, within the bound.
A program may use at most 256 MiB of HBM per device.

```python
import math
import jax
import jax.numpy as jnp
from jax import lax

HEADS = 12
HEAD_DIM = 64
FF = 3072
D = 768
BIG_CROP = 197
SMALL_CROP = 37
BIG_COUNT = 2
IMAGE_LEN = 690
CROPS = 10
STEP = 5
TOKENS = 16560
N_ROW = 4


def draw_crop_ids(key, part):
    images = TOKENS // IMAGE_LEN
    image_keys = jax.random.split(jax.random.fold_in(key, 17), images)
    orders = jax.vmap(lambda one_key: jax.random.permutation(one_key, CROPS))(image_keys)
    lengths = jnp.where(orders < BIG_COUNT, BIG_CROP, SMALL_CROP).astype(jnp.int32)
    ends = jnp.cumsum(lengths, axis=1).astype(jnp.int32)
    places = jnp.arange(IMAGE_LEN, dtype=jnp.int32)
    within = jnp.sum((places[None, :, None] >= ends[:, None, :]).astype(jnp.int32), axis=2).astype(jnp.int32)
    image_base = (jnp.arange(images, dtype=jnp.int32) * CROPS)[:, None]
    return (within + image_base).reshape(TOKENS).astype(jnp.int32)


def level_of(rng, shape, cuts, least, largest):
    level, own = 1.0, jax.random.fold_in(rng, 6)
    for axis_at, parts in cuts:
        steps = jnp.exp(jax.random.uniform(jax.random.fold_in(own, axis_at), (parts,), jnp.float32, least / len(cuts), largest / len(cuts)))
        level = level * jnp.repeat(steps, shape[axis_at] // parts).reshape([-1 if axis == axis_at else 1 for axis in range(len(shape))])
    return level


def normal_values(own_key, shape, scale, reach, shards=(), held_as=jnp.bfloat16):
    array = jax.random.normal(own_key, shape, jnp.float32) * scale
    if len(shards) > 0:
        array = level_of(own_key, shape, shards, -0.22, 0.18) * array
    return jnp.clip(array, min=-reach, max=reach).astype(held_as)


def setup_inputs(seed: int = 0) -> dict:
    key_of = jax.random.split(jax.random.key(seed), 22)
    layer_in = normal_values(key_of[0], (TOKENS // 2, N_ROW, 2 * D // N_ROW), 1.0, 6.0, ((0, 8), (1, 4)))
    grad_out = normal_values(key_of[1], (TOKENS // 2, N_ROW, 2 * D // N_ROW), 1.0, 6.0, ((0, 8), (1, 4)))
    crop_ids = draw_crop_ids(jax.random.fold_in(key_of[21], 71), 0)
    w_qkv = normal_values(key_of[3], (D, 3, D), D ** -0.5, 0.21875, ((0, 8), (2, 4)), jnp.float32)
    w_out = normal_values(key_of[4], (D, D), (D // 24) ** -0.5, 1.0, ((0, 8), (1, 4)), jnp.float32)
    w_fc1 = normal_values(key_of[5], (D, FF), D ** -0.5, 0.21875, ((0, 8), (1, 4)), jnp.float32)
    w_fc2 = normal_values(key_of[6], (FF, D), FF ** -0.5, 0.109375, ((0, 8), (1, 4)), jnp.float32)
    norm_gains = jnp.clip(jnp.exp(jax.random.uniform(key_of[7], (2 * D,), jnp.float32, math.log(0.4), math.log(2.0))), 0.4, 2.0)
    all_biases = normal_values(key_of[8], (6 * D + FF,), 0.3, 1.5, (), jnp.float32)
    first_qkv = normal_values(key_of[9], (D, 3, D), ((4 * D * D + 2 * D * FF + 8 * D + FF) ** -0.5), 0.0022538076, ((0, 8), (2, 4)), jnp.float32)
    second_qkv = jnp.clip(jnp.exp(math.log(1.1288108225926408e-06) - 2.7725887 * jax.random.uniform(key_of[10], (D, 3, D), jnp.float32) ** level_of(key_of[10], (D, 3, D), ((0, 8), (2, 4)), -0.2, 0.2)), 7.055067641204005e-08, 1.1288108225926408e-06)
    first_out = normal_values(key_of[11], (D, D), ((4 * D * D + 2 * D * FF + 8 * D + FF) ** -0.5), 0.0022538076, ((0, 8), (1, 4)), jnp.float32)
    second_out = jnp.clip(jnp.exp(math.log(1.1288108225926408e-06) - 2.7725887 * jax.random.uniform(key_of[12], (D, D), jnp.float32) ** level_of(key_of[12], (D, D), ((0, 8), (1, 4)), -0.2, 0.2)), 7.055067641204005e-08, 1.1288108225926408e-06)
    first_fc1 = normal_values(key_of[13], (D, FF), ((4 * D * D + 2 * D * FF + 8 * D + FF) ** -0.5), 0.0022538076, ((0, 8), (1, 4)), jnp.float32)
    second_fc1 = jnp.clip(jnp.exp(math.log(1.1288108225926408e-06) - 2.7725887 * jax.random.uniform(key_of[14], (D, FF), jnp.float32) ** level_of(key_of[14], (D, FF), ((0, 8), (1, 4)), -0.2, 0.2)), 7.055067641204005e-08, 1.1288108225926408e-06)
    first_fc2 = normal_values(key_of[15], (FF, D), ((4 * D * D + 2 * D * FF + 8 * D + FF) ** -0.5), 0.0022538076, ((0, 8), (1, 4)), jnp.float32)
    second_fc2 = jnp.clip(jnp.exp(math.log(1.1288108225926408e-06) - 2.7725887 * jax.random.uniform(key_of[16], (FF, D), jnp.float32) ** level_of(key_of[16], (FF, D), ((0, 8), (1, 4)), -0.2, 0.2)), 7.055067641204005e-08, 1.1288108225926408e-06)
    first_gains = normal_values(key_of[17], (2 * D,), ((4 * D * D + 2 * D * FF + 8 * D + FF) ** -0.5), 0.0022538076, (), jnp.float32)
    second_gains = jnp.clip(jnp.exp(jax.random.uniform(key_of[18], (2 * D,), jnp.float32, math.log(7.055067641204005e-08), math.log(1.1288108225926408e-06))), 7.055067641204005e-08, 1.1288108225926408e-06)
    first_biases = normal_values(key_of[19], (6 * D + FF,), ((4 * D * D + 2 * D * FF + 8 * D + FF) ** -0.5), 0.0022538076, (), jnp.float32)
    second_biases = jnp.clip(jnp.exp(jax.random.uniform(key_of[20], (6 * D + FF,), jnp.float32, math.log(7.055067641204005e-08), math.log(1.1288108225926408e-06))), 7.055067641204005e-08, 1.1288108225926408e-06)
    return dict(layer_in=layer_in, grad_out=grad_out, crop_ids=crop_ids, w_qkv=w_qkv, w_out=w_out, w_fc1=w_fc1, w_fc2=w_fc2, norm_gains=norm_gains, all_biases=all_biases, first_qkv=first_qkv, second_qkv=second_qkv, first_out=first_out, second_out=second_out, first_fc1=first_fc1, second_fc1=second_fc1, first_fc2=first_fc2, second_fc2=second_fc2, first_gains=first_gains, second_gains=second_gains, first_biases=first_biases, second_biases=second_biases)


NORM_EPS = 1e-06
CLIP_NORM = 1.0
BETA_ONE = 0.5
BETA_TWO = 0.5
ADAM_EPS = 1e-08
DECAY = 0.05
MASKED = -1e+30

@jax.custom_vjp
def low(v):
    return lax.optimization_barrier(v.astype(jnp.bfloat16)).astype(jnp.float32)

@jax.custom_vjp
def low_back(v):
    return v

def low_keep(v):
    return (low(v), None)

def low_pass(kept, grad):
    return (grad,)

def back_keep(v):
    return (v, None)

def back_low(kept, grad):
    return (low(grad),)
low.defvjp(low_keep, low_pass)
low_back.defvjp(back_keep, back_low)

def unpack_rows(value):
    return value.reshape(TOKENS // 2, N_ROW, 2, D // N_ROW).transpose(0, 2, 1, 3).reshape(TOKENS, D)

def pack_rows(value):
    return value.reshape(TOKENS // 2, 2, N_ROW, D // N_ROW).transpose(0, 2, 1, 3).reshape(TOKENS // 2, N_ROW, 2 * D // N_ROW)

def matmul(left, right):
    return jnp.dot(left, right, precision=lax.Precision.HIGHEST, preferred_element_type=jnp.float32)

def layer_norm(value, gain, shift):
    centre = lax.optimization_barrier(jnp.mean(value, axis=-1, keepdims=True))
    centred = value - centre
    spread = lax.optimization_barrier(jnp.mean(centred * centred, axis=-1, keepdims=True))
    return centred * lax.rsqrt(spread + NORM_EPS) * gain + shift

def attend_image(pieces):
    queries, keys, values, labels = pieces
    scores = jnp.einsum('qhd,khd->hqk', queries, keys, precision=lax.Precision.HIGHEST) * HEAD_DIM ** (-0.5)
    scores = low_back(scores)
    same_crop = (labels[:, None] == labels[None, :])[None]
    scores = jnp.where(same_crop, scores, MASKED)
    probs = jax.nn.softmax(scores, axis=2)
    return jnp.einsum('hqk,khd->qhd', low(probs), values, precision=lax.Precision.HIGHEST)

def forward(layer_in, w_qkv, w_out, w_fc1, w_fc2, norm_gains, all_biases, crop_ids):
    images = layer_in.shape[0] // IMAGE_LEN
    gain_one = norm_gains[:D]
    gain_two = norm_gains[D:]
    shift_one = all_biases[:D]
    shift_two = all_biases[D:2 * D]
    bias_query = all_biases[2 * D:3 * D]
    bias_value = all_biases[3 * D:4 * D]
    bias_out = all_biases[4 * D:5 * D]
    bias_fc2 = all_biases[5 * D:6 * D]
    bias_fc1 = all_biases[6 * D:]
    act_one = low(layer_norm(layer_in, gain_one, shift_one))
    qkv = matmul(act_one, w_qkv.reshape(D, 3 * D)).reshape(-1, 3, D)
    qkv = low(low_back(qkv + jnp.stack([bias_query, jnp.zeros_like(bias_query), bias_value])))
    queries = qkv[:, 0].reshape(images, IMAGE_LEN, HEADS, HEAD_DIM)
    keys = qkv[:, 1].reshape(images, IMAGE_LEN, HEADS, HEAD_DIM)
    values = qkv[:, 2].reshape(images, IMAGE_LEN, HEADS, HEAD_DIM)
    labels = crop_ids.reshape(images, IMAGE_LEN)
    mixed = lax.map(jax.checkpoint(attend_image), (queries, keys, values, labels))
    mixed = low(low_back(mixed.reshape(-1, D)))
    branch_one = low_back(matmul(mixed, w_out) + bias_out)
    middle = layer_in + branch_one
    act_two = low(layer_norm(middle, gain_two, shift_two))
    hidden = low_back(matmul(act_two, w_fc1) + bias_fc1)
    active = low(jax.nn.gelu(hidden, approximate=False))
    branch_two = low_back(matmul(active, w_fc2) + bias_fc2)
    return middle + branch_two

def adam_step(weight, grad, first, second, rate, factor):
    clipped = grad * factor
    new_first = BETA_ONE * first + (1.0 - BETA_ONE) * clipped
    new_second = BETA_TWO * second + (1.0 - BETA_TWO) * clipped * clipped
    unbiased_first = new_first / (1.0 - BETA_ONE ** STEP)
    unbiased_second = new_second / (1.0 - BETA_TWO ** STEP)
    new_weight = weight - rate * (unbiased_first / (jnp.sqrt(unbiased_second) + ADAM_EPS) + DECAY * weight)
    return (new_first, new_second, new_weight, new_weight.astype(jnp.bfloat16))

def reference(layer_in, grad_out, crop_ids, w_qkv, w_out, w_fc1, w_fc2, norm_gains, all_biases, first_qkv, second_qkv, first_out, second_out, first_fc1, second_fc1, first_fc2, second_fc2, first_gains, second_gains, first_biases, second_biases):
    inputs = unpack_rows(layer_in.astype(jnp.float32))
    cotangent = unpack_rows(grad_out.astype(jnp.float32))
    half_qkv = w_qkv.astype(jnp.bfloat16).astype(jnp.float32)
    half_out = w_out.astype(jnp.bfloat16).astype(jnp.float32)
    half_fc1 = w_fc1.astype(jnp.bfloat16).astype(jnp.float32)
    half_fc2 = w_fc2.astype(jnp.bfloat16).astype(jnp.float32)

    def layer(inputs_in, wq, wo, wa, wb, gains_in, biases_in):
        return forward(inputs_in, wq, wo, wa, wb, gains_in, biases_in, crop_ids)
    layer_out, pullback = jax.vjp(layer, inputs, half_qkv, half_out, half_fc1, half_fc2, norm_gains, all_biases)
    grad_in, g_qkv, g_out, g_fc1, g_fc2, g_gains, g_biases = pullback(cotangent)
    squares = jnp.sum(g_qkv * g_qkv) + jnp.sum(g_out * g_out) + jnp.sum(g_fc1 * g_fc1)
    squares = squares + jnp.sum(g_fc2 * g_fc2) + jnp.sum(g_gains * g_gains) + jnp.sum(g_biases * g_biases)
    grad_norm = jnp.sqrt(squares)
    factor = jnp.minimum(1.0, CLIP_NORM / grad_norm)
    upd_qkv = adam_step(w_qkv, g_qkv, first_qkv, second_qkv, D ** (-0.5), factor)
    upd_out = adam_step(w_out, g_out, first_out, second_out, (D // 24) ** (-0.5), factor)
    upd_fc1 = adam_step(w_fc1, g_fc1, first_fc1, second_fc1, D ** (-0.5), factor)
    upd_fc2 = adam_step(w_fc2, g_fc2, first_fc2, second_fc2, FF ** (-0.5), factor)
    upd_gains = adam_step(norm_gains, g_gains, first_gains, second_gains, 0.3, factor)
    upd_biases = adam_step(all_biases, g_biases, first_biases, second_biases, 0.3, factor)
    return (pack_rows(layer_out), pack_rows(grad_in), grad_norm, upd_qkv[0], upd_qkv[1], upd_qkv[2], upd_qkv[3], upd_out[0], upd_out[1], upd_out[2], upd_out[3], upd_fc1[0], upd_fc1[1], upd_fc1[2], upd_fc1[3], upd_fc2[0], upd_fc2[1], upd_fc2[2], upd_fc2[3], upd_gains[0], upd_gains[1], upd_gains[2], upd_gains[3], upd_biases[0], upd_biases[1], upd_biases[2], upd_biases[3])
```

```python
import jax
import jax.numpy as jnp
from jax import lax
from jax.sharding import PartitionSpec as P

HEADS = 12
HEAD_DIM = 64
FF = 3072
D = 768
BIG_CROP = 197
SMALL_CROP = 37
IMAGE_LEN = 690
CROPS = 10
STEP = 5

NORM_EPS = 1e-06
CLIP_NORM = 1.0
BETA_ONE = 0.5
BETA_TWO = 0.5
ADAM_EPS = 1e-08
DECAY = 0.05
MASKED = -1e30

SLOTS = 544
BIG_SLOTS = 208
TRIO_SLOTS = 112
TRIO = 3 * SMALL_CROP
BF = jnp.bfloat16
F32 = jnp.float32


def crop_starts(labels):
    images = labels.shape[0] // IMAGE_LEN
    places = labels.reshape(images, IMAGE_LEN) % CROPS
    order = jnp.arange(CROPS, dtype=jnp.int32)
    sizes = jnp.sum((places[:, :, None] == order).astype(jnp.int32), axis=1)
    starts = jnp.sum((places[:, :, None] < order).astype(jnp.int32), axis=1)
    starts = starts + IMAGE_LEN * jnp.arange(images, dtype=jnp.int32)[:, None]
    big = (sizes == BIG_CROP).astype(jnp.int32)
    earlier = (order[:, None] < order[None, :]).astype(jnp.int32)
    big_rank = jnp.sum(big[:, :, None] * earlier, axis=1)
    small_rank = jnp.sum((1 - big)[:, :, None] * earlier, axis=1)

    def ranked(flag, rank, count):
        hit = flag[:, :, None] * (rank[:, :, None] == jnp.arange(count, dtype=jnp.int32)).astype(jnp.int32)
        return jnp.sum(hit * starts[:, :, None], axis=1).reshape(-1)

    return ranked(big, big_rank, 2), ranked(1 - big, small_rank, CROPS - 2)


def slot_segments(kind):
    if kind == 0:
        bigs, trios = 2, 1
    else:
        bigs, trios = 1, 3
    parts = []
    at = 0
    for b in range(bigs):
        parts.append((at, BIG_CROP, True, b))
        at += BIG_SLOTS
    for s in range(3 * trios):
        parts.append((at + s // 3 * TRIO_SLOTS + s % 3 * SMALL_CROP, SMALL_CROP, False, s))
    return parts


def slot_sources(labels):
    big, small = crop_starts(labels)
    rows = []
    for row in range(4):
        kind = row // 2
        at_big = (0, 2, 4, 5)[row]
        at_small = (0, 3, 6, 15)[row]
        out = []
        filled = 0
        for first, length, is_big, index in slot_segments(kind):
            if first > filled:
                out.append(jnp.full((first - filled,), -1, jnp.int32))
            start = big[at_big + index] if is_big else small[at_small + index]
            out.append(start + jnp.arange(length, dtype=jnp.int32))
            filled = first + length
        if filled < SLOTS:
            out.append(jnp.full((SLOTS - filled,), -1, jnp.int32))
        rows.append(jnp.concatenate(out))
    return jnp.stack(rows)


def slot_crops(kind):
    slot = jnp.arange(SLOTS, dtype=jnp.int32)
    crop = jnp.full((SLOTS,), -1, jnp.int32)
    for number, (first, length, _, _) in enumerate(slot_segments(kind)):
        crop = jnp.where((slot >= first) & (slot < first + length), number, crop)
    return crop


def dot(a, b):
    return jnp.dot(a, b, preferred_element_type=F32)


def dot_nt(a, b):
    return lax.dot_general(a, b, (((1,), (1,)), ((), ())), preferred_element_type=F32)


def dot_tn(a, b):
    return lax.dot_general(a, b, (((0,), (0,)), ((), ())), preferred_element_type=F32)


def norm_stats(value):
    centre = jnp.mean(value, axis=1, keepdims=True)
    centred = value - centre
    spread = jnp.mean(centred * centred, axis=1, keepdims=True)
    inverse = lax.rsqrt(spread + NORM_EPS)
    return centred * inverse, inverse


def norm_back(grad, normed, inverse, gain):
    weighted = grad * gain
    first = jnp.mean(weighted, axis=1, keepdims=True)
    second = jnp.mean(weighted * normed, axis=1, keepdims=True)
    return inverse * (weighted - first - normed * second)


def layer(x, cot, crops, w_qkv, w_out, w_fc1, w_fc2, gains, biases):
    inputs = x.astype(F32)
    cotf = cot.astype(F32)
    normed_one, inverse_one = norm_stats(inputs)
    act_one = (normed_one * gains[:D] + biases[:D]).astype(BF)
    qkv_bias = jnp.concatenate([biases[2 * D : 3 * D], jnp.zeros((D,), F32), biases[3 * D : 4 * D]])
    qkv = (dot(act_one, w_qkv) + qkv_bias).astype(BF)
    heads = qkv.reshape(SLOTS, 3, HEADS, HEAD_DIM)
    q, k, v = heads[:, 0], heads[:, 1], heads[:, 2]
    scores = jnp.einsum("qhd,khd->hqk", q, k, preferred_element_type=F32) * HEAD_DIM ** (-0.5)
    scores = jnp.where((crops[:, None] == crops[None, :])[None], scores, MASKED)
    probs = jax.nn.softmax(scores, axis=2)
    half_probs = probs.astype(BF)
    mixed = jnp.einsum("hqk,khd->qhd", half_probs, v, preferred_element_type=F32)
    mixed = mixed.reshape(SLOTS, D).astype(BF)
    middle = inputs + dot(mixed, w_out) + biases[4 * D : 5 * D]
    normed_two, inverse_two = norm_stats(middle)
    act_two = (normed_two * gains[D:] + biases[D : 2 * D]).astype(BF)
    hidden = dot(act_two, w_fc1) + biases[6 * D :]
    active, gelu_pull = jax.vjp(lambda h: jax.nn.gelu(h, approximate=False), hidden)
    active = active.astype(BF)
    out = middle + dot(active, w_fc2) + biases[5 * D : 6 * D]

    g_fc2 = dot_tn(active, cot)
    grad_hidden = gelu_pull(dot_nt(cot, w_fc2))[0].astype(BF)
    g_fc1 = dot_tn(act_two, grad_hidden)
    grad_two = dot_nt(grad_hidden, w_fc1)
    grad_middle = cotf + norm_back(grad_two, normed_two, inverse_two, gains[D:])
    branch = grad_middle.astype(BF)
    g_out = dot_tn(mixed, branch)
    grad_mixed = dot_nt(branch, w_out).astype(BF).reshape(SLOTS, HEADS, HEAD_DIM)
    grad_probs = jnp.einsum("qhd,khd->hqk", grad_mixed, v, preferred_element_type=F32)
    grad_scores = (probs * (grad_probs - jnp.sum(probs * grad_probs, axis=2, keepdims=True))).astype(BF)
    scale = HEAD_DIM ** (-0.5)
    grad_q = jnp.einsum("hqk,khd->qhd", grad_scores, k, preferred_element_type=F32) * scale
    grad_k = jnp.einsum("hqk,qhd->khd", grad_scores, q, preferred_element_type=F32) * scale
    grad_v = jnp.einsum("hqk,qhd->khd", half_probs, grad_mixed, preferred_element_type=F32)
    grad_qkv = jnp.stack([grad_q, grad_k, grad_v], axis=1).astype(BF).reshape(SLOTS, 3 * D)
    g_qkv = dot_tn(act_one, grad_qkv)
    grad_one = dot_nt(grad_qkv, w_qkv)
    grad_in = grad_middle + norm_back(grad_one, normed_one, inverse_one, gains[:D])

    g_gains = jnp.concatenate([jnp.sum(grad_one * normed_one, axis=0), jnp.sum(grad_two * normed_two, axis=0)])
    qkv_sums = jnp.sum(grad_qkv.astype(F32), axis=0)
    g_biases = jnp.concatenate([
        jnp.sum(grad_one, axis=0),
        jnp.sum(grad_two, axis=0),
        qkv_sums[:D],
        qkv_sums[2 * D :],
        jnp.sum(branch.astype(F32), axis=0),
        jnp.sum(cotf, axis=0),
        jnp.sum(grad_hidden.astype(F32), axis=0),
    ])
    return out, grad_in, g_qkv, g_out, g_fc1, g_fc2, g_gains, g_biases


def adam_step(weight, grad, first, second, rate, factor):
    clipped = grad * factor
    new_first = BETA_ONE * first + (1.0 - BETA_ONE) * clipped
    new_second = BETA_TWO * second + (1.0 - BETA_TWO) * clipped * clipped
    unbiased_first = new_first / (1.0 - BETA_ONE**STEP)
    unbiased_second = new_second / (1.0 - BETA_TWO**STEP)
    new_weight = weight - rate * (
        unbiased_first / (jnp.sqrt(unbiased_second) + ADAM_EPS) + DECAY * weight
    )
    return (new_first, new_second, new_weight, new_weight.astype(BF))


def gather(value, axes):
    for name, dim in axes:
        value = lax.all_gather(value, name, axis=dim, tiled=True)
    return value


def scatter(value, axes):
    for name, dim in axes:
        value = lax.psum_scatter(value, name, scatter_dimension=dim, tiled=True)
    return value.astype(F32)


def local(
    layer_in, grad_out, crop_ids, w_qkv, w_out, w_fc1, w_fc2, norm_gains, all_biases,
    first_qkv, second_qkv, first_out, second_out, first_fc1, second_fc1, first_fc2, second_fc2,
    first_gains, second_gains, first_biases, second_biases,
):
    row = lax.axis_index("row")
    n_row, n_col = lax.axis_size("row"), lax.axis_size("col")
    feat = D // n_row
    pairs = layer_in.shape[0]
    labels = lax.ppermute(
        crop_ids, ("row", "col"), [(r * n_col + c, c * n_row + r) for r in range(n_row) for c in range(n_col)]
    )
    sources = slot_sources(labels).reshape(-1)
    place = jnp.where(sources < 0, -1, (sources % 2) * pairs + sources // 2)
    pick = (place[:, None] == jnp.arange(2 * pairs, dtype=jnp.int32)[None, :]).astype(BF)

    def to_slots(value):
        halves = jnp.concatenate([value[:, 0, :feat], value[:, 0, feat:]], axis=0)
        sent = dot(pick, halves).astype(BF)
        got = lax.all_to_all(sent, "row", 0, 0, tiled=True)
        return got.reshape(n_row, SLOTS, feat).transpose(1, 0, 2).reshape(SLOTS, D)

    def to_tokens(value):
        sent = value.astype(BF).reshape(SLOTS, n_row, feat).transpose(1, 0, 2).reshape(n_row * SLOTS, feat)
        got = lax.all_to_all(sent, "row", 0, 0, tiled=True)
        halves = dot_tn(pick, got)
        return jnp.concatenate([halves[:pairs], halves[pairs:]], axis=1).reshape(pairs, 1, 2 * feat)

    full_qkv = gather(w_qkv.astype(BF), (("dp", 0), ("row", 0), ("col", 2))).reshape(D, 3 * D)
    full_out = gather(w_out.astype(BF), (("dp", 0), ("col", 0), ("row", 1)))
    full_fc1 = gather(w_fc1.astype(BF), (("dp", 0), ("row", 0), ("col", 1)))
    full_fc2 = gather(w_fc2.astype(BF), (("dp", 0), ("col", 0), ("row", 1)))
    crops = jnp.where(row < 2, slot_crops(0), slot_crops(1))
    out, grad_in, g_qkv, g_out, g_fc1, g_fc2, g_gains, g_biases = layer(
        to_slots(layer_in), to_slots(grad_out), crops, full_qkv, full_out, full_fc1, full_fc2, norm_gains, all_biases
    )
    owned_qkv = scatter(g_qkv.astype(BF).reshape(D, 3, D), (("col", 2), ("row", 0), ("dp", 0)))
    owned_out = scatter(g_out.astype(BF), (("row", 1), ("col", 0), ("dp", 0)))
    owned_fc1 = scatter(g_fc1.astype(BF), (("col", 1), ("row", 0), ("dp", 0)))
    owned_fc2 = scatter(g_fc2.astype(BF), (("row", 1), ("col", 0), ("dp", 0)))
    local_squares = (
        jnp.sum(owned_qkv * owned_qkv)
        + jnp.sum(owned_out * owned_out)
        + jnp.sum(owned_fc1 * owned_fc1)
        + jnp.sum(owned_fc2 * owned_fc2)
    )
    grad_gains, grad_biases, weight_squares = lax.psum((g_gains, g_biases, local_squares), ("dp", "row", "col"))
    grad_norm = jnp.sqrt(weight_squares + jnp.sum(grad_gains * grad_gains) + jnp.sum(grad_biases * grad_biases))
    factor = jnp.minimum(1.0, CLIP_NORM / grad_norm)
    upd_qkv = adam_step(w_qkv, owned_qkv, first_qkv, second_qkv, D ** (-0.5), factor)
    upd_out = adam_step(w_out, owned_out, first_out, second_out, (D // 24) ** (-0.5), factor)
    upd_fc1 = adam_step(w_fc1, owned_fc1, first_fc1, second_fc1, D ** (-0.5), factor)
    upd_fc2 = adam_step(w_fc2, owned_fc2, first_fc2, second_fc2, FF ** (-0.5), factor)
    upd_gains = adam_step(norm_gains, grad_gains, first_gains, second_gains, 0.3, factor)
    upd_biases = adam_step(all_biases, grad_biases, first_biases, second_biases, 0.3, factor)
    return (
        to_tokens(out), to_tokens(grad_in), grad_norm,
        *upd_qkv, *upd_out, *upd_fc1, *upd_fc2, *upd_gains, *upd_biases,
    )


def solution(mesh):
    tokens = P(("dp", "col"), "row", None)
    qkv = P(("row", "dp"), None, "col")
    out = P(("col", "dp"), "row")
    fc1 = P(("row", "dp"), "col")
    whole = P()
    return jax.shard_map(
        local,
        mesh=mesh,
        in_specs=(
            tokens, tokens, P(("dp", "row")), qkv, out, fc1, out, whole, whole,
            qkv, qkv, out, out, fc1, fc1, out, out, whole, whole, whole, whole,
        ),
        out_specs=(tokens, tokens, whole) + (qkv,) * 4 + (out,) * 4 + (fc1,) * 4 + (out,) * 4 + (whole,) * 8,
        check_vma=False,
    )
```

```python
import jax
import jax.numpy as jnp
from jax import lax
from jax.experimental import pallas as pl
from jax.experimental.pallas import tpu as pltpu
from jax.sharding import PartitionSpec as P

HEADS = 12
HEAD_DIM = 64
FF = 3072
D = 768
BIG_CROP = 197
SMALL_CROP = 37
IMAGE_LEN = 690
CROPS = 10
STEP = 5

NORM_EPS = 1e-06
CLIP_NORM = 1.0
BETA_ONE = 0.5
BETA_TWO = 0.5
ADAM_EPS = 1e-08
DECAY = 0.05
MASKED = -1e30

SLOTS = 544
BIG_SLOTS = 208
TRIO_SLOTS = 112
TRIO = 3 * SMALL_CROP
BF = jnp.bfloat16
F32 = jnp.float32


def crop_starts(labels):
    images = labels.shape[0] // IMAGE_LEN
    places = labels.reshape(images, IMAGE_LEN) % CROPS
    order = jnp.arange(CROPS, dtype=jnp.int32)
    sizes = jnp.sum((places[:, :, None] == order).astype(jnp.int32), axis=1)
    starts = jnp.sum((places[:, :, None] < order).astype(jnp.int32), axis=1)
    starts = starts + IMAGE_LEN * jnp.arange(images, dtype=jnp.int32)[:, None]
    big = (sizes == BIG_CROP).astype(jnp.int32)
    earlier = (order[:, None] < order[None, :]).astype(jnp.int32)
    big_rank = jnp.sum(big[:, :, None] * earlier, axis=1)
    small_rank = jnp.sum((1 - big)[:, :, None] * earlier, axis=1)

    def ranked(flag, rank, count):
        hit = flag[:, :, None] * (rank[:, :, None] == jnp.arange(count, dtype=jnp.int32)).astype(jnp.int32)
        return jnp.sum(hit * starts[:, :, None], axis=1).reshape(-1)

    return ranked(big, big_rank, 2), ranked(1 - big, small_rank, CROPS - 2)


def slot_segments(kind):
    if kind == 0:
        bigs, trios = 2, 1
    else:
        bigs, trios = 1, 3
    parts = []
    at = 0
    for b in range(bigs):
        parts.append((at, BIG_CROP, True, b))
        at += BIG_SLOTS
    for s in range(3 * trios):
        parts.append((at + s // 3 * TRIO_SLOTS + s % 3 * SMALL_CROP, SMALL_CROP, False, s))
    return parts


def slot_sources(labels):
    big, small = crop_starts(labels)
    rows = []
    for row in range(4):
        kind = row // 2
        at_big = (0, 2, 4, 5)[row]
        at_small = (0, 3, 6, 15)[row]
        out = []
        filled = 0
        for first, length, is_big, index in slot_segments(kind):
            if first > filled:
                out.append(jnp.full((first - filled,), -1, jnp.int32))
            start = big[at_big + index] if is_big else small[at_small + index]
            out.append(start + jnp.arange(length, dtype=jnp.int32))
            filled = first + length
        if filled < SLOTS:
            out.append(jnp.full((SLOTS - filled,), -1, jnp.int32))
        rows.append(jnp.concatenate(out))
    return jnp.stack(rows)


def slot_crops(kind):
    slot = jnp.arange(SLOTS, dtype=jnp.int32)
    crop = jnp.full((SLOTS,), -1, jnp.int32)
    for number, (first, length, _, _) in enumerate(slot_segments(kind)):
        crop = jnp.where((slot >= first) & (slot < first + length), number, crop)
    return crop


MESH = pl.DeviceIdType.MESH
HALF = 64
QW = 640
TOK = 1040
CHUNK = 32
WQ, WO, W1, W2 = 0, 1, 2, 3
VMEM_LIMIT = 60 * 2**20


def mm(a, b):
    return lax.dot_general(a, b, (((1,), (0,)), ((), ())), preferred_element_type=F32)


def mm_nt(a, b):
    return lax.dot_general(a, b, (((1,), (1,)), ((), ())), preferred_element_type=F32)


def mm_tn(a, b):
    return lax.dot_general(a, b, (((0,), (0,)), ((), ())), preferred_element_type=F32)


class Place:
    def __init__(self):
        self.y = lax.axis_index("dp")
        self.z = lax.axis_index("row")
        self.c = lax.axis_index("col")
        self.core = lax.rem(self.c, 2)
        self.x = lax.div(self.c, 2)
        self.cx = lax.rem(self.c + 2, 4)
        self.cs = self.c + 1 - 2 * self.core
        self.xn = (self.y, self.z, self.cx)
        self.yn = (1 - self.y, self.z, self.c)
        self.cn = (self.y, self.z, self.cs)
        self.low = self.z < 2
        self.mid = jnp.logical_or(self.z == 1, self.z == 2)
        self.step = jnp.where(self.low, 1, -1)

    def zth(self, z):
        return (self.y, z, self.c)

    def other(self, j):
        return lax.rem(self.z + self.step * j + 4, 4)

    def enter(self):
        barrier = pltpu.get_barrier_semaphore()
        peers = [self.zth(lax.rem(self.z + k, 4)) for k in (1, 2, 3)] + [self.xn, self.yn, self.cn]
        for peer in peers:
            pl.semaphore_signal(barrier, inc=1, device_id=peer, device_id_type=MESH)
        pl.semaphore_wait(barrier, len(peers))


def shard_of(refs, p, c, s, y):
    ref = refs[p]
    if p == WO:
        return ref.at[s, c, pl.ds(pl.multiple_of(y * 96, 32), 96), :]
    if p == W2:
        return ref.at[c, s, :, pl.ds(pl.multiple_of(y * 384, 128), 384)]
    return ref.at[c, s, y]


def group_of(refs, p, c, y):
    ref = refs[p]
    if p == WO:
        return ref.at[:, c, pl.ds(pl.multiple_of(y * 96, 32), 96), :]
    if p == W2:
        return ref.at[c, :, :, pl.ds(pl.multiple_of(y * 384, 128), 384)]
    return ref.at[c, :, y]


class Sends:
    def __init__(self):
        self.left = []

    def start(self, src, dst, send_sem, recv_sem, peer, when=None):
        copy = pltpu.make_async_remote_copy(
            src_ref=src, dst_ref=dst, send_sem=send_sem, recv_sem=recv_sem, device_id=peer, device_id_type=MESH
        )
        if when is None:
            copy.start()
        else:
            pl.when(when)(copy.start)
        self.left.append((copy, when))

    def drain(self):
        for copy, when in self.left:
            if when is None:
                copy.wait_send()
            else:
                pl.when(when)(copy.wait_send)
        self.left = []


def arrived(ref, sem, me):
    pltpu.make_async_remote_copy(
        src_ref=ref, dst_ref=ref, send_sem=sem, recv_sem=sem, device_id=me, device_id_type=MESH
    ).wait_recv()


class Gather:
    def __init__(self, at, refs, sends, zs, zr, xs, xr, ys, yr, ds, dr, cs, cr):
        self.at, self.refs, self.sends = at, refs, sends
        self.zs, self.zr, self.xs, self.xr = zs, zr, xs, xr
        self.ys, self.yr, self.ds, self.dr, self.cs, self.cr = ys, yr, ds, dr, cs, cr

    def across(self, p, s):
        at = self.at
        own = shard_of(self.refs, p, at.c, s, at.y)
        self.sends.start(own, own, self.xs.at[p, s], self.xr.at[p, s], at.xn)
        self.sends.start(own, own, self.ys.at[p, s], self.yr.at[p, s], at.yn)

    def own_across(self, p):
        self.across(p, self.at.z)

    def own_along(self, p):
        at = self.at
        own = shard_of(self.refs, p, at.c, at.z, at.y)
        second = jnp.where(at.mid, at.z - at.step, at.z + 2 * at.step)
        self.sends.start(own, own, self.zs.at[p, 0], self.zr.at[p, at.z], at.zth(at.z + at.step))
        self.sends.start(own, own, self.zs.at[p, 1], self.zr.at[p, at.z], at.zth(second))

    def to_core(self, p, g, c, y):
        ref = group_of(self.refs, p, c, y)
        self.sends.start(ref, ref, self.cs.at[p, g], self.cr.at[p, g], self.at.cn)

    def along(self, p):
        at = self.at
        for j in (1, 2, 3):
            s = at.other(j)
            ref = shard_of(self.refs, p, at.c, s, at.y)
            arrived(ref, self.zr.at[p, s], at.yn)
            if j < 3:
                self.sends.start(ref, ref, self.zs.at[p, 1 + j], self.zr.at[p, s], at.zth(at.z - at.step), when=at.mid)
            self.across(p, s)
        self.to_core(p, 0, at.c, at.y)

    def cross(self, p):
        at = self.at
        for j in (0, 1, 2, 3):
            s = at.other(j)
            from_x = shard_of(self.refs, p, at.cx, s, at.y)
            from_y = shard_of(self.refs, p, at.c, s, 1 - at.y)
            arrived(from_x, self.xr.at[p, s], at.yn)
            arrived(from_y, self.yr.at[p, s], at.yn)
            if j < 2:
                self.sends.start(from_x, from_x, self.ds.at[p, j], self.dr.at[p, s], at.yn)
            else:
                self.sends.start(from_y, from_y, self.ds.at[p, j], self.dr.at[p, s], at.xn)
        self.to_core(p, 1, at.cx, at.y)
        self.to_core(p, 2, at.c, 1 - at.y)

    def corner(self, p):
        at = self.at
        for j in (0, 1, 2, 3):
            s = at.other(j)
            arrived(shard_of(self.refs, p, at.cx, s, 1 - at.y), self.dr.at[p, s], at.yn)
        self.to_core(p, 3, at.cx, 1 - at.y)

    def ready(self, p):
        at = self.at
        other_x = at.cs + 2 - 4 * at.x
        for g, (c, y) in enumerate(((at.cs, at.y), (other_x, at.y), (at.cs, 1 - at.y), (other_x, 1 - at.y))):
            arrived(group_of(self.refs, p, c, y), self.cr.at[p, g], at.yn)


def exchange_start(at, sends, blocks, landing, send_sems, recv_sems):
    for k in (1, 2, 3):
        to = lax.rem(at.z + k, 4)
        sends.start(blocks.at[to], landing.at[at.z], send_sems.at[k - 1], recv_sems.at[at.z], at.zth(to))


def exchange_wait(at, landing, recv_sems):
    for k in (1, 2, 3):
        s = lax.rem(at.z + k, 4)
        arrived(landing.at[s], recv_sems.at[s], at.yn)


def row_stats(value):
    centre = jnp.sum(value, axis=1, keepdims=True) * (1.0 / D)
    centred = value - centre
    spread = jnp.sum(centred * centred, axis=1, keepdims=True) * (1.0 / D)
    inverse = lax.rsqrt(spread + NORM_EPS)
    return centred * inverse, inverse


def chunks(body):
    def step(i, carry):
        body(pl.ds(pl.multiple_of(i * CHUNK, CHUNK), CHUNK))
        return carry

    lax.fori_loop(0, SLOTS // CHUNK, step, 0)


def loop(count, body):
    def step(i, carry):
        body(i)
        return carry

    lax.fori_loop(0, count, step, 0)


def lane_low(rows):
    return lax.broadcasted_iota(jnp.int32, (rows, 2 * HALF), 1) < HALF


def swap_halves(value):
    return jnp.concatenate([value[:, HALF:], value[:, :HALF]], axis=1)


def segments(kind):
    if kind == 0:
        return ((0, BIG_SLOTS, True, 0), (BIG_SLOTS, BIG_SLOTS, True, 1), (2 * BIG_SLOTS, 128, False, 0))
    return ((0, BIG_SLOTS, True, 0),) + tuple((BIG_SLOTS + t * TRIO_SLOTS, TRIO_SLOTS, False, t) for t in range(3))


def key_mask(size, is_big):
    key = lax.broadcasted_iota(jnp.int32, (size, size), 1)
    if is_big:
        return key < BIG_CROP
    query = lax.broadcasted_iota(jnp.int32, (size, size), 0)

    def crop(v):
        return (v >= SMALL_CROP).astype(jnp.int32) + (v >= 2 * SMALL_CROP).astype(jnp.int32) + (v >= TRIO).astype(jnp.int32)

    return jnp.logical_and(crop(query) == crop(key), key < TRIO)


def attend_segment(c, segment, qkv, mixed, pbig, ptrio):
    first, size, is_big, index = segment
    rows = pl.ds(first, size)
    q01 = qkv[c, rows, 0:128]
    k01 = qkv[c, rows, 128:256]
    v01 = qkv[c, rows, 256:384]
    qk2 = qkv[c, rows, 384:512]
    v2 = qkv[c, rows, 512:640]
    low = lane_low(size)
    none = jnp.zeros((size, 128), BF)
    mask = key_mask(size, is_big)
    outs = []
    for h, (q, k, v) in enumerate((
        (jnp.where(low, q01, none), k01, v01),
        (jnp.where(low, none, q01), k01, v01),
        (jnp.where(low, qk2, none), swap_halves(qk2), v2),
    )):
        scores = jnp.where(mask, mm_nt(q, k) * HEAD_DIM**-0.5, MASKED)
        weights = jnp.exp(scores - jnp.max(scores, axis=1, keepdims=True))
        total = jnp.sum(weights, axis=1, keepdims=True)
        weights = (weights * (1.0 / total)).astype(BF)
        if is_big:
            pbig[c, h, index] = weights
        else:
            ptrio[c, h, index, 0:size, 0:size] = weights
        outs.append(mm(weights, v))
    mixed[rows, pl.ds(pl.multiple_of(c * 256, 256), 128)] = jnp.where(low, outs[0], outs[1]).astype(BF)
    mixed[rows, pl.ds(pl.multiple_of(c * 256 + 128, 128), 128)] = outs[2].astype(BF)


def attend(at, c, qkv, mixed, pbig, ptrio):
    for kind in (0, 1):

        @pl.when(at.low if kind == 0 else jnp.logical_not(at.low))
        def _():
            for segment in segments(kind):
                attend_segment(c, segment, qkv, mixed, pbig, ptrio)


def transpose_into(dst, src, tiles):
    def body(j):
        lanes = pl.ds(pl.multiple_of(j * 128, 128), 128)
        dst[lanes, :] = src[:, lanes].T

    loop(tiles, body)


def forward_kernel(
    x_in, g_in, place, wq_in, wo_in, w1_in, w2_in, gains, biases, qkv_bias,
    wq_h, wo_h, w1_h, w2_h, x_h, mid_h, a1t_h, a2t_h, mixt_h, qkv_h, pbig_h, ptrio_h, act_h, slope_h, cot_h, cott_h, out_h,
    wq, wo, w1, w2, tok, send_x, send_g, land_x, land_g, x, mid, midb, a1, a1t, a2t, mixed, mixt, qkv, pbig, ptrio,
    act, slope, cot, cott, out,
    zs, zr, xs, xr, ys, yr, ds, dr, cs, cr, exs, exr, egs, egr, hs,
):
    at = Place()
    refs = (wq, wo, w1, w2)
    sends = Sends()
    gather = Gather(at, refs, sends, zs, zr, xs, xr, ys, yr, ds, dr, cs, cr)
    at.enter()
    stores = []

    def keep(src, dst):
        copy = pltpu.make_async_copy(src, dst, hs.at[len(stores)])
        copy.start()
        stores.append(copy)

    wq[at.c, at.z, at.y] = wq_in[...].astype(BF)
    gather.own_along(WQ)
    gather.own_across(WQ)
    wo[at.z, at.c, pl.ds(pl.multiple_of(at.y * 96, 32), 96), :] = wo_in[...].astype(BF)
    w1[at.c, at.z, at.y] = w1_in[...].astype(BF)
    gather.own_across(WO)
    gather.own_across(W1)
    w2[at.c, at.z, :, pl.ds(pl.multiple_of(at.y * 384, 128), 384)] = w2_in[...].T.astype(BF)
    gather.own_across(W2)

    pairs = x_in.shape[0]
    for n, ref in enumerate((x_in, g_in)):
        for half in (0, 1):
            tok[n, half * TOK + TOK - 16 : half * TOK + TOK, :] = jnp.zeros((16, 192), BF)
            tok[n, half * TOK : half * TOK + pairs, :] = ref[:, half * 192 : half * 192 + 192]

    def pick(r):
        at_slot = place[pl.ds(pl.multiple_of(r * SLOTS, SLOTS), SLOTS), :]
        one = (lax.broadcasted_iota(jnp.int32, (SLOTS, 2 * TOK), 1) == at_slot).astype(F32).astype(BF)
        send_x[r] = mm(one, tok[0]).astype(BF)
        send_g[r] = mm(one, tok[1]).astype(BF)

    loop(4, pick)
    exchange_start(at, sends, send_x, land_x, exs, exr)
    land_x[at.z] = send_x[at.z]
    land_g[at.z] = send_g[at.z]
    gather.own_along(WO)
    gather.own_along(W1)
    gather.along(WQ)
    wo[:, :, 192:256, :] = jnp.zeros((4, 4, 64, 192), BF)
    exchange_wait(at, land_x, exr)

    def norm_one(rows):
        value = jnp.concatenate([land_x[r, rows, :] for r in range(4)], axis=1)
        x[rows, :] = value
        normed, _ = row_stats(value.astype(F32))
        a1[rows, :] = (normed * gains[0:1, :] + biases[0:1, :]).astype(BF)

    chunks(norm_one)
    gather.along(WO)
    gather.own_along(W2)
    gather.cross(WQ)
    transpose_into(a1t, a1, 6)
    a1t[768:784, :] = jnp.ones((16, SLOTS), BF)
    keep(a1t, a1t_h)
    keep(x, x_h)
    gather.along(W1)
    exchange_start(at, sends, send_g, land_g, egs, egr)
    gather.cross(WO)
    gather.corner(WQ)
    gather.ready(WQ)
    wqv = wq.reshape(4, 768, QW)
    keep(wqv, wq_h)

    def project(c):
        for n in range(0, QW, 256):
            wide = min(256, QW - n)
            qkv[c, :, n : n + wide] = (mm(a1[...], wqv[c, :, n : n + wide]) + qkv_bias[c, :, n : n + wide]).astype(BF)

    loop(4, project)
    keep(qkv, qkv_h)
    gather.corner(WO)
    gather.cross(W1)
    loop(2, lambda c: attend(at, c, qkv, mixed, pbig, ptrio))
    gather.along(W2)
    loop(2, lambda c: attend(at, c + 2, qkv, mixed, pbig, ptrio))
    keep(pbig, pbig_h)
    keep(ptrio, ptrio_h)
    gather.ready(WO)
    gather.corner(W1)
    wov = wo.reshape(4, 1024, 192)
    keep(wov, wo_h)

    def branch(z):
        midb[z] = mm(mixed[...], wov[z])

    loop(4, branch)

    def norm_two(rows):
        value = x[rows, :].astype(F32) + jnp.concatenate([midb[r, rows, :] for r in range(4)], axis=1) + biases[4:5, :]
        mid[rows, :] = value
        normed, _ = row_stats(value)
        a1[rows, :] = (normed * gains[1:2, :] + biases[1:2, :]).astype(BF)

    chunks(norm_two)
    keep(mid, mid_h)
    gather.cross(W2)
    gather.ready(W1)
    w1v = w1.reshape(4, 768, 768)
    keep(w1v, w1_h)

    def expand(c):
        def tile(n):
            lanes = pl.ds(pl.multiple_of(n * 256, 256), 256)
            hidden = mm(a1[...], w1v[c, :, lanes]) + biases[pl.ds(6 + c, 1), lanes]
            share = 0.5 + 0.5 * lax.erf(hidden * 0.7071067811865476)
            bell = jnp.exp(hidden * hidden * -0.5) * 0.3989422804014327
            act[c, :, lanes] = (hidden * share).astype(BF)
            slope[c, :, lanes] = (share + hidden * bell).astype(BF)

        loop(3, tile)

    loop(4, expand)
    keep(act, act_h)
    keep(slope, slope_h)
    gather.corner(W2)
    transpose_into(a2t, a1, 6)
    a2t[768:784, :] = jnp.ones((16, SLOTS), BF)
    transpose_into(mixt, mixed, 8)
    mixt[192:208, :] = jnp.ones((16, SLOTS), BF)
    keep(a2t, a2t_h)
    keep(mixt, mixt_h)
    exchange_wait(at, land_g, egr)

    def join(rows):
        cot[rows, :] = jnp.concatenate([land_g[r, rows, :] for r in range(4)], axis=1)

    chunks(join)
    keep(cot, cot_h)
    transpose_into(cott, cot, 6)
    keep(cott, cott_h)
    gather.ready(W2)
    w2v = w2.reshape(4, 768, 768)
    keep(w2v, w2_h)

    def contract(n):
        rows = pl.ds(pl.multiple_of(n * 256, 256), 256)
        total = mm_nt(act[0], w2v[0, rows, :])
        for c in (1, 2, 3):
            total = total + mm_nt(act[c], w2v[c, rows, :])
        midb2 = total + biases[5:6, rows] + mid[:, rows]
        out[n] = midb2.astype(BF)

    loop(3, contract)

    def split(rows):
        value = jnp.concatenate([out[n, rows, :] for n in range(3)], axis=1)
        for r in range(4):
            land_x[r, rows, :] = value[:, r * 192 : r * 192 + 192]

    chunks(split)
    keep(land_x, out_h)
    sends.drain()
    for copy in stores:
        copy.wait()


FORWARD_OUT = (
    ((4, 768, QW), BF), ((4, 1024, 192), BF), ((4, 768, 768), BF), ((4, 768, 768), BF),
    ((SLOTS, D), BF), ((SLOTS, D), F32), ((784, SLOTS), BF), ((784, SLOTS), BF), ((1024, SLOTS), BF),
    ((4, SLOTS, QW), BF), ((4, 3, 2, BIG_SLOTS, BIG_SLOTS), BF), ((4, 3, 3, 128, 128), BF),
    ((4, SLOTS, 768), BF), ((4, SLOTS, 768), BF), ((SLOTS, D), BF), ((D, SLOTS), BF), ((4, SLOTS, 192), BF),
)


def run_forward(*operands):
    sem = pltpu.SemaphoreType.DMA
    vmem = pltpu.VMEM
    return pl.pallas_call(
        forward_kernel,
        out_shape=[jax.ShapeDtypeStruct(s, t) for s, t in FORWARD_OUT],
        in_specs=[pl.BlockSpec(memory_space=vmem)] * len(operands),
        out_specs=[pl.BlockSpec(memory_space=pl.ANY)] * len(FORWARD_OUT),
        scratch_shapes=[
            vmem((4, 4, 2, 96, QW), BF), vmem((4, 4, 256, 192), BF), vmem((4, 4, 2, 96, 768), BF), vmem((4, 4, 192, 768), BF),
            vmem((2, 2 * TOK, 192), BF),
            vmem((4, SLOTS, 192), BF), vmem((4, SLOTS, 192), BF), vmem((4, SLOTS, 192), BF), vmem((4, SLOTS, 192), BF),
            vmem((SLOTS, D), BF), vmem((SLOTS, D), F32), vmem((4, SLOTS, 192), F32), vmem((SLOTS, D), BF),
            vmem((784, SLOTS), BF), vmem((784, SLOTS), BF), vmem((SLOTS, 1024), BF), vmem((1024, SLOTS), BF),
            vmem((4, SLOTS, QW), BF), vmem((4, 3, 2, BIG_SLOTS, BIG_SLOTS), BF), vmem((4, 3, 3, 128, 128), BF),
            vmem((4, SLOTS, 768), BF), vmem((4, SLOTS, 768), BF), vmem((SLOTS, D), BF), vmem((D, SLOTS), BF),
            vmem((3, SLOTS, 256), BF),
            sem((4, 4)), sem((4, 4)), sem((4, 4)), sem((4, 4)), sem((4, 4)), sem((4, 4)), sem((4, 4)), sem((4, 4)),
            sem((4, 4)), sem((4, 4)), sem((3,)), sem((4,)), sem((3,)), sem((4,)), sem((len(FORWARD_OUT),)),
        ],
        compiler_params=pltpu.CompilerParams(collective_id=0, has_side_effects=True, vmem_limit_bytes=VMEM_LIMIT),
    )(*operands)


class Reduce:
    def __init__(self, at, sends, grads, pair, corner, cross, along, owned, small, sems):
        self.at, self.sends = at, sends
        self.grads, self.pair, self.corner, self.cross, self.along = grads, pair, corner, cross, along
        self.owned, self.small = owned, small
        self.ss, self.rs = sems

    def start(self, p, n, src, dst, peer, arrival=None):
        self.sends.start(src, dst, self.ss.at[p, n], self.rs.at[p, n if arrival is None else arrival], peer)

    def pair_send(self, p):
        at = self.at
        for i in (0, 1):
            c = 2 * i + 1 - at.core
            self.start(p, i, self.grads[p].at[c], self.pair[p].at[i], at.cn)

    def add(self, dst, src):
        for s in range(dst.shape[0]):
            dst[s] = dst[s] + src[s]

    def pair_sum(self, p):
        at, grads, pair = self.at, self.grads[p], self.pair[p]
        for i in (0, 1):
            arrived(pair.at[i], self.rs.at[p, i], at.yn)
        far = 1 - at.x

        def add(c, i, y):
            def one(s):
                grads[c, y, s] = grads[c, y, s] + pair[i, y, s]

            loop(4, one)

        add(at.cx, far, 1 - at.y)
        self.start(p, 2, grads.at[at.cx, 1 - at.y, pl.ds(0, 2)], self.corner[p].at[0], at.xn)
        self.start(p, 3, grads.at[at.cx, 1 - at.y, pl.ds(2, 2)], self.corner[p].at[1], at.yn)
        add(at.cx, far, at.y)
        self.start(p, 4, grads.at[at.cx, at.y, pl.ds(0, 2)], self.cross[p].at[0, pl.ds(0, 2)], at.xn)
        add(at.c, at.x, 1 - at.y)
        self.start(p, 5, grads.at[at.c, 1 - at.y, pl.ds(2, 2)], self.cross[p].at[1, pl.ds(2, 2)], at.yn)
        add(at.c, at.x, at.y)

    def corner_sum(self, p):
        at, grads, corner = self.at, self.grads[p], self.corner[p]
        arrived(corner.at[0], self.rs.at[p, 2], at.yn)

        def one(s):
            grads[at.c, 1 - at.y, s] = grads[at.c, 1 - at.y, s] + corner[0, s]

        loop(2, one)
        self.start(p, 6, grads.at[at.c, 1 - at.y, pl.ds(0, 2)], self.cross[p].at[1, pl.ds(0, 2)], at.yn)
        arrived(corner.at[1], self.rs.at[p, 3], at.yn)

        def two(s):
            grads[at.cx, at.y, s + 2] = grads[at.cx, at.y, s + 2] + corner[1, s]

        loop(2, two)
        self.start(p, 7, grads.at[at.cx, at.y, pl.ds(2, 2)], self.cross[p].at[0, pl.ds(2, 2)], at.xn)

    def cross_sum(self, p):
        at, grads, cross = self.at, self.grads[p], self.cross[p]
        for n, (i, half) in ((4, (0, 0)), (7, (0, 2)), (5, (1, 2)), (6, (1, 0))):
            arrived(cross.at[i, pl.ds(half, 2)], self.rs.at[p, n], at.yn)

        def one(s):
            grads[at.c, at.y, s] = grads[at.c, at.y, s] + cross[0, s] + cross[1, s]

        loop(4, one)
        for k in (1, 2, 3):
            to = lax.rem(at.z + k, 4)
            self.start(p, 7 + k, grads.at[at.c, at.y, to], self.along[p].at[at.z], at.zth(to), arrival=8 + at.z)

    def along_sum(self, p):
        at, grads, along = self.at, self.grads[p], self.along[p]
        for k in (1, 2, 3):
            s = lax.rem(at.z + k, 4)
            arrived(along.at[s], self.rs.at[p, 8 + s], at.yn)
        total = grads[at.c, at.y, at.z].astype(F32)
        for k in (1, 2, 3):
            total = total + along[lax.rem(at.z + k, 4)].astype(F32)
        self.owned[p][...] = total
        wide = total.shape[1]
        self.small[14:15, 0:wide] = self.small[14:15, 0:wide] + jnp.sum(total * total, axis=0, keepdims=True)


def back_segment(c, slot, segment, qkv, weights_big, weights_trio, mixed, grads):
    first, size, is_big, index = segment
    rows = pl.ds(first, size)
    q01 = qkv[c, rows, 0:128]
    k01 = qkv[c, rows, 128:256]
    v01 = qkv[c, rows, 256:384]
    kq2 = swap_halves(qkv[c, rows, 384:512])
    v2 = qkv[c, rows, 512:640]
    g01 = mixed[rows, pl.ds(pl.multiple_of(c * 256, 256), 128)]
    g2 = mixed[rows, pl.ds(pl.multiple_of(c * 256 + 128, 128), 128)]
    low = lane_low(size)
    none = jnp.zeros((size, 128), BF)
    dq, dk, dv = [], [], []
    for h, (g, gs, q, k, v) in enumerate((
        (g01, jnp.where(low, g01, none), q01, k01, v01),
        (g01, jnp.where(low, none, g01), q01, k01, v01),
        (g2, g2, kq2, kq2, v2),
    )):
        if is_big:
            weights = weights_big[slot, h, index]
        else:
            weights = weights_trio[slot, h, index, 0:size, 0:size]
        wide = weights.astype(F32)
        product = wide * mm_nt(gs, v)
        scores = (product - wide * jnp.sum(product, axis=1, keepdims=True)).astype(BF)
        dq.append(mm(scores, k))
        dk.append(mm_tn(scores, q))
        dv.append(mm_tn(weights, g))
    scale = HEAD_DIM**-0.5
    grads[c, rows, 0:128] = (jnp.where(low, dq[0], dq[1]) * scale).astype(BF)
    grads[c, rows, 128:256] = (jnp.where(low, dk[0], dk[1]) * scale).astype(BF)
    grads[c, rows, 256:384] = jnp.where(low, dv[0], dv[1]).astype(BF)
    grads[c, rows, 384:512] = (jnp.where(low, dq[2], dk[2]) * scale).astype(BF)
    grads[c, rows, 512:640] = dv[2].astype(BF)


def backward_kernel(
    wq_h, wo_h, w1_h, w2_h, x_h, mid_h, a1t_h, a2t_h, mixt_h, qkv_h, pbig_h, ptrio_h, act_h, slope_h, cot_h, cott_h, out_h,
    gains,
    own_q, own_o, own_1, own_2, total, land_out, land_in,
    ring, wo, gq, go, g1, g2, pq, po, p1, p2, nq, no, n1, n2, rq, ro, r1, r2, lq, lo, l1, l2,
    act, slope, cot, cott, a2t, a1t, mixt, mid, x, pbig, ptrio, gmix, grad, half, send, small, sums_of, line, plane,
    ss, rs, hs, ring_s, p_s, ex_s, ex_r, in_s, in_r, line_s, line_r, plane_s, plane_r,
):
    at = Place()
    sends = Sends()
    reduce = Reduce(
        at, sends, (gq, go, g1, g2), (pq, po, p1, p2), (nq, no, n1, n2), (rq, ro, r1, r2), (lq, lo, l1, l2),
        (own_q, own_o, own_1, own_2), small, (ss, rs),
    )
    loads = {}

    def load(name, src, dst):
        copy = pltpu.make_async_copy(src, dst, hs.at[len(loads)])
        copy.start()
        loads[name] = copy

    uses = [(w2_h, c) for c in range(4)] + [(w1_h, c) for c in range(4)] + [(wq_h, c) for c in range(4)]
    ring_copies = {}

    def ring_start(u):
        if u < len(uses):
            src, c = uses[u]
            wide = src.shape[2]
            copy = pltpu.make_async_copy(src.at[c], ring.at[u % 3, :, pl.ds(0, wide)], ring_s.at[u])
            copy.start()
            ring_copies[u] = copy

    load("cott", cott_h, cott)
    load("act", act_h, act)
    for u in range(3):
        ring_start(u)
    load("cot", cot_h, cot)
    load("slope", slope_h, slope)
    load("a2t", a2t_h, a2t)
    load("mid", mid_h, mid)
    load("mixt", mixt_h, mixt)
    load("wo", wo_h, wo)
    load("a1t", a1t_h, a1t)
    load("x", x_h, x)
    at_enter(at)
    keep_out = pltpu.make_async_copy(out_h.at[at.z], land_out.at[at.z], ex_s.at[3])
    keep_out.start()
    exchange_start(at, sends, out_h, land_out, ex_s, ex_r)
    small[...] = jnp.zeros((16, D), F32)

    def group(i):
        return 2 * (i % 2) + (1 - at.core if i < 2 else at.core)

    loads["cott"].wait()
    loads["act"].wait()

    def grad_fc2(c):
        for n in range(3):
            tile = mm(cott[...], act[c, :, n * 256 : n * 256 + 256]).astype(BF)
            for z in range(4):
                part = tile[z * 192 : z * 192 + 192]
                if n == 0:
                    g2[c, 0, z, :, 0:256] = part
                elif n == 1:
                    g2[c, 0, z, :, 256:384] = part[:, 0:128]
                    g2[c, 1, z, :, 0:128] = part[:, 128:256]
                else:
                    g2[c, 1, z, :, 128:384] = part

    loop(2, lambda i: grad_fc2(2 * i + 1 - at.core))
    reduce.pair_send(W2)
    loop(2, lambda i: grad_fc2(2 * i + at.core))
    reduce.pair_sum(W2)
    loads["cot"].wait()
    loads["slope"].wait()

    def grad_hidden(c):
        ring_copies[c].wait()

        def tile(n):
            lanes = pl.ds(pl.multiple_of(n * 256, 256), 256)
            slope[c, :, lanes] = (mm(cot[...], ring[c % 3, :, lanes]) * slope[c, :, lanes].astype(F32)).astype(BF)

        loop(3, tile)
        ring_start(c + 3)

    grad_hidden(0)
    grad_hidden(1)
    grad_hidden(2)
    grad_hidden(3)
    reduce.corner_sum(W2)
    loads["a2t"].wait()

    def rows_to_shards(dst, c, lanes, tile):
        for z in range(4):
            for y in range(2):
                first = (z * 2 + y) * 96
                dst[c, y, z, :, lanes] = tile[first : first + 96].astype(BF)

    def grad_fc1(c):
        def tile(n):
            lanes = pl.ds(pl.multiple_of(n * 256, 256), 256)
            value = mm(a2t[...], slope[c, :, lanes])
            rows_to_shards(g1, c, lanes, value)
            sums_of[c, :, lanes] = value[768:769]

        loop(3, tile)

    loop(2, lambda i: grad_fc1(2 * i + 1 - at.core))
    reduce.pair_send(W1)
    loop(2, lambda i: grad_fc1(2 * i + at.core))
    reduce.pair_sum(W1)
    reduce.cross_sum(W2)

    def back_through(u, c, left, wide):
        ring_copies[u].wait()

        def tile(n):
            lanes = pl.ds(pl.multiple_of(n * 256, 256), 256)
            part = mm_nt(left[c, :, 0:wide], ring[u % 3, lanes, 0:wide])
            if c == 0:
                grad[:, lanes] = part
            else:
                grad[:, lanes] = grad[:, lanes] + part

        loop(3, tile)
        ring_start(u + 3)

    for c in range(4):
        back_through(4 + c, c, slope, 768)
    load("qkv", qkv_h, slope.at[:, :, pl.ds(0, QW)])
    reduce.corner_sum(W1)
    loads["mid"].wait()

    def norm_two(i, sums):
        rows = pl.ds(pl.multiple_of(i * CHUNK, CHUNK), CHUNK)
        normed, inverse = row_stats(mid[rows, :])
        upper = grad[rows, :]
        weighted = upper * gains[1:2, :]
        first = jnp.sum(weighted, axis=1, keepdims=True) * (1.0 / D)
        second = jnp.sum(weighted * normed, axis=1, keepdims=True) * (1.0 / D)
        straight = cot[rows, :].astype(F32)
        value = straight + inverse * (weighted - first - normed * second)
        mid[rows, :] = value
        branch = value.astype(BF)
        for r in range(4):
            half[r, rows, :] = branch[:, r * 192 : r * 192 + 192]
        parts = (upper * normed, upper, branch.astype(F32), straight)
        return tuple(s + jnp.sum(v, axis=0, keepdims=True) for s, v in zip(sums, parts))

    zero = jnp.zeros((1, D), F32)
    sums = lax.fori_loop(0, SLOTS // CHUNK, norm_two, (zero,) * 4)
    for r, value in zip((1, 3, 4, 5), sums):
        small[r : r + 1, :] = value
    loads["mixt"].wait()

    def grad_out(z):
        value = mm(mixt[...], half[z]).astype(BF)
        for c in range(4):
            for y in range(2):
                go[c, y, z] = value[c * 256 + y * 96 : c * 256 + y * 96 + 96]

    loop(4, grad_out)
    reduce.pair_send(WO)
    loads["wo"].wait()

    def grad_mixed(c):
        rows = pl.ds(pl.multiple_of(c * 256, 256), 256)
        value = mm_nt(half[0], wo[0, rows, :])
        for z in (1, 2, 3):
            value = value + mm_nt(half[z], wo[z, rows, :])
        gmix[:, rows] = value.astype(BF)

    loop(4, grad_mixed)
    reduce.pair_sum(WO)
    loads["qkv"].wait()

    def fetch(c, slot):
        return (
            pltpu.make_async_copy(pbig_h.at[c], pbig.at[slot], p_s.at[slot, 0]),
            pltpu.make_async_copy(ptrio_h.at[c], ptrio.at[slot], p_s.at[slot, 1]),
        )

    for copy in fetch(0, 0):
        copy.start()
    for c in range(4):
        for copy in fetch(c, c % 2):
            copy.wait()
        if c < 3:
            for copy in fetch(c + 1, (c + 1) % 2):
                copy.start()
        for kind in (0, 1):

            @pl.when(at.low if kind == 0 else jnp.logical_not(at.low))
            def _():
                for segment in segments(kind):
                    back_segment(c, c % 2, segment, slope, pbig, ptrio, gmix, act)

        if c == 0:
            reduce.along_sum(W2)
        elif c == 1:
            reduce.cross_sum(W1)
        elif c == 2:
            reduce.corner_sum(WO)

    loads["a1t"].wait()

    def grad_q(c):
        for n in range(0, QW, 256):
            wide = min(256, QW - n)
            value = mm(a1t[...], act[c, :, n : n + wide])
            rows_to_shards(gq, c, slice(n, n + wide), value)
            sums_of[4 + c, :, n : n + wide] = value[768:769]

    loop(2, lambda i: grad_q(2 * i + 1 - at.core))
    reduce.pair_send(WQ)
    loop(2, lambda i: grad_q(2 * i + at.core))
    reduce.pair_sum(WQ)
    for c in range(4):
        back_through(8 + c, c, act, QW)
    reduce.along_sum(W1)
    reduce.cross_sum(WO)
    loads["x"].wait()

    def norm_one(i, sums):
        rows = pl.ds(pl.multiple_of(i * CHUNK, CHUNK), CHUNK)
        normed, inverse = row_stats(x[rows, :].astype(F32))
        upper = grad[rows, :]
        weighted = upper * gains[0:1, :]
        first = jnp.sum(weighted, axis=1, keepdims=True) * (1.0 / D)
        second = jnp.sum(weighted * normed, axis=1, keepdims=True) * (1.0 / D)
        value = (mid[rows, :] + inverse * (weighted - first - normed * second)).astype(BF)
        for r in range(4):
            send[r, rows, :] = value[:, r * 192 : r * 192 + 192]
        parts = (upper * normed, upper)
        return tuple(s + jnp.sum(v, axis=0, keepdims=True) for s, v in zip(sums, parts))

    sums = lax.fori_loop(0, SLOTS // CHUNK, norm_one, (zero,) * 2)
    for r, value in zip((0, 2), sums):
        small[r : r + 1, :] = value
    exchange_start(at, sends, send, land_in, in_s, in_r)
    keep_in = pltpu.make_async_copy(send.at[at.z], land_in.at[at.z], in_s.at[3])
    keep_in.start()
    reduce.corner_sum(WQ)
    reduce.along_sum(WO)
    reduce.cross_sum(WQ)
    reduce.along_sum(WQ)

    for c in range(4):
        small[6 + c : 7 + c, :] = sums_of[c]
        small[10 + c : 11 + c, 0:QW] = sums_of[4 + c, :, 0:QW]
    line[at.z] = small[...]
    for k in (1, 2, 3):
        to = lax.rem(at.z + k, 4)
        sends.start(small, line.at[at.z], line_s.at[k - 1], line_r.at[at.z], at.zth(to))
    for k in (1, 2, 3):
        s = lax.rem(at.z + k, 4)
        arrived(line.at[s], line_r.at[s], at.yn)
    me = at.y * 4 + at.c
    plane[me] = line[0] + line[1] + line[2] + line[3]
    for k in range(1, 8):
        to = lax.rem(me + k, 8)
        sends.start(
            plane.at[me], plane.at[me], plane_s.at[k - 1], plane_r.at[me], (lax.div(to, 4), at.z, lax.rem(to, 4))
        )
    for k in range(1, 8):
        s = lax.rem(me + k, 8)
        arrived(plane.at[s], plane_r.at[s], at.yn)
    value = plane[0]
    for s in range(1, 8):
        value = value + plane[s]
    total[...] = value
    exchange_wait(at, land_out, ex_r)
    exchange_wait(at, land_in, in_r)
    keep_out.wait()
    keep_in.wait()
    sends.drain()


def at_enter(at):
    barrier = pltpu.get_barrier_semaphore()
    me = at.y * 4 + at.c
    peers = [at.zth(lax.rem(at.z + k, 4)) for k in (1, 2, 3)]
    for k in range(1, 8):
        to = lax.rem(me + k, 8)
        peers.append((lax.div(to, 4), at.z, lax.rem(to, 4)))
    for peer in peers:
        pl.semaphore_signal(barrier, inc=1, device_id=peer, device_id_type=MESH)
    pl.semaphore_wait(barrier, len(peers))


SHARDS = ((96, QW), (96, 192), (96, 768), (192, 384))


def run_backward(*operands):
    sem = pltpu.SemaphoreType.DMA
    vmem = pltpu.VMEM
    shape = jax.ShapeDtypeStruct
    stages = [(4, 2, 4), (2, 2, 4), (2, 2), (2, 4), (4,)]
    return pl.pallas_call(
        backward_kernel,
        out_shape=[shape(s, F32) for s in SHARDS] + [shape((16, D), F32)] + [shape((4, SLOTS, 192), BF)] * 2,
        in_specs=[pl.BlockSpec(memory_space=pl.ANY)] * (len(operands) - 1) + [pl.BlockSpec(memory_space=vmem)],
        out_specs=[pl.BlockSpec(memory_space=vmem)] * 5 + [pl.BlockSpec(memory_space=pl.ANY)] * 2,
        scratch_shapes=[vmem((3, 768, 768), BF), vmem((4, 1024, 192), BF)]
        + [vmem(lead + s, BF) for lead in stages for s in SHARDS]
        + [
            vmem((4, SLOTS, 768), BF), vmem((4, SLOTS, 768), BF), vmem((SLOTS, D), BF), vmem((D, SLOTS), BF),
            vmem((784, SLOTS), BF), vmem((784, SLOTS), BF), vmem((1024, SLOTS), BF), vmem((SLOTS, D), F32),
            vmem((SLOTS, D), BF), vmem((2, 3, 2, BIG_SLOTS, BIG_SLOTS), BF), vmem((2, 3, 3, 128, 128), BF),
            vmem((SLOTS, 1024), BF), vmem((SLOTS, D), F32), vmem((4, SLOTS, 192), BF), vmem((4, SLOTS, 192), BF),
            vmem((16, D), F32), vmem((8, 1, D), F32), vmem((4, 16, D), F32), vmem((8, 16, D), F32),
            sem((4, 12)), sem((4, 12)), sem((12,)), sem((12,)), sem((2, 2)), sem((4,)), sem((4,)), sem((4,)), sem((4,)),
            sem((3,)), sem((4,)), sem((7,)), sem((8,)),
        ],
        compiler_params=pltpu.CompilerParams(collective_id=1, has_side_effects=True, vmem_limit_bytes=VMEM_LIMIT),
    )(*operands)


def prepare(layer_in, grad_out, crop_ids, w_qkv, w_out, w_fc1, w_fc2, norm_gains, all_biases):
    pairs = layer_in.shape[0]
    labels = lax.ppermute(crop_ids, ("row", "col"), [(r * 4 + c, c * 4 + r) for r in range(4) for c in range(4)])
    sources = slot_sources(labels).reshape(-1, 1)
    place = jnp.where(sources < 0, -1, (sources % 2) * TOK + sources // 2)

    def packed(q, k, v):
        zero = jnp.zeros(q.shape[:-1] + (HALF,), q.dtype)
        return jnp.concatenate(
            [q[..., :128], k[..., :128], v[..., :128], q[..., 128:], k[..., 128:], v[..., 128:], zero], axis=-1
        )

    wq = packed(w_qkv[:, 0], w_qkv[:, 1], w_qkv[:, 2])
    bias = all_biases.reshape(10, D)
    bq, bv = bias[2].reshape(4, 1, 192), bias[3].reshape(4, 1, 192)
    qkv_bias = packed(bq, jnp.zeros_like(bq), bv)
    return (
        layer_in.reshape(pairs, 384), grad_out.reshape(pairs, 384), place,
        wq, w_out, w_fc1, w_fc2, norm_gains.reshape(2, D), bias, qkv_bias,
    )


def local_fast(
    layer_in, grad_out, crop_ids, w_qkv, w_out, w_fc1, w_fc2, norm_gains, all_biases,
    first_qkv, second_qkv, first_out, second_out, first_fc1, second_fc1, first_fc2, second_fc2,
    first_gains, second_gains, first_biases, second_biases,
):
    pairs = layer_in.shape[0]
    operands = prepare(layer_in, grad_out, crop_ids, w_qkv, w_out, w_fc1, w_fc2, norm_gains, all_biases)
    place = operands[2].reshape(1, -1)
    kept = run_forward(*operands)
    own_q, owned_out, owned_fc1, own_2, total, land_out, land_in = run_backward(*kept, operands[7])

    back = (jnp.arange(2 * TOK, dtype=jnp.int32)[:, None] == place).astype(BF)

    def to_tokens(value):
        halves = dot(back, value.reshape(4 * SLOTS, 192))
        return jnp.concatenate([halves[:pairs], halves[TOK : TOK + pairs]], axis=1).reshape(pairs, 1, 384)

    def unpacked(value):
        q = jnp.concatenate([value[:, 0:128], value[:, 384:448]], axis=1)
        k = jnp.concatenate([value[:, 128:256], value[:, 448:512]], axis=1)
        v = jnp.concatenate([value[:, 256:384], value[:, 512:576]], axis=1)
        return q, k, v

    owned_qkv = jnp.stack(unpacked(own_q), axis=1)
    owned_fc2 = own_2.T
    q_sums, _, v_sums = unpacked(total[10:14])
    grad_gains = total[0:2].reshape(-1)
    grad_biases = jnp.concatenate([
        total[2:4].reshape(-1), q_sums.reshape(-1), v_sums.reshape(-1), total[4:10].reshape(-1)
    ])
    weight_squares = jnp.sum(total[14])
    grad_norm = jnp.sqrt(weight_squares + jnp.sum(grad_gains * grad_gains) + jnp.sum(grad_biases * grad_biases))
    factor = jnp.minimum(1.0, CLIP_NORM / grad_norm)
    upd_qkv = adam_step(w_qkv, owned_qkv, first_qkv, second_qkv, D ** (-0.5), factor)
    upd_out = adam_step(w_out, owned_out, first_out, second_out, (D // 24) ** (-0.5), factor)
    upd_fc1 = adam_step(w_fc1, owned_fc1, first_fc1, second_fc1, D ** (-0.5), factor)
    upd_fc2 = adam_step(w_fc2, owned_fc2, first_fc2, second_fc2, FF ** (-0.5), factor)
    upd_gains = adam_step(norm_gains, grad_gains, first_gains, second_gains, 0.3, factor)
    upd_biases = adam_step(all_biases, grad_biases, first_biases, second_biases, 0.3, factor)
    return (
        to_tokens(land_out), to_tokens(land_in), grad_norm,
        *upd_qkv, *upd_out, *upd_fc1, *upd_fc2, *upd_gains, *upd_biases,
    )


def dot(a, b):
    return jnp.dot(a, b, preferred_element_type=F32)


def dot_nt(a, b):
    return lax.dot_general(a, b, (((1,), (1,)), ((), ())), preferred_element_type=F32)


def dot_tn(a, b):
    return lax.dot_general(a, b, (((0,), (0,)), ((), ())), preferred_element_type=F32)


def norm_stats(value):
    centre = jnp.mean(value, axis=1, keepdims=True)
    centred = value - centre
    spread = jnp.mean(centred * centred, axis=1, keepdims=True)
    inverse = lax.rsqrt(spread + NORM_EPS)
    return centred * inverse, inverse


def norm_back(grad, normed, inverse, gain):
    weighted = grad * gain
    first = jnp.mean(weighted, axis=1, keepdims=True)
    second = jnp.mean(weighted * normed, axis=1, keepdims=True)
    return inverse * (weighted - first - normed * second)


def layer(x, cot, crops, w_qkv, w_out, w_fc1, w_fc2, gains, biases):
    inputs = x.astype(F32)
    cotf = cot.astype(F32)
    normed_one, inverse_one = norm_stats(inputs)
    act_one = (normed_one * gains[:D] + biases[:D]).astype(BF)
    qkv_bias = jnp.concatenate([biases[2 * D : 3 * D], jnp.zeros((D,), F32), biases[3 * D : 4 * D]])
    qkv = (dot(act_one, w_qkv) + qkv_bias).astype(BF)
    heads = qkv.reshape(SLOTS, 3, HEADS, HEAD_DIM)
    q, k, v = heads[:, 0], heads[:, 1], heads[:, 2]
    scores = jnp.einsum("qhd,khd->hqk", q, k, preferred_element_type=F32) * HEAD_DIM ** (-0.5)
    scores = jnp.where((crops[:, None] == crops[None, :])[None], scores, MASKED)
    probs = jax.nn.softmax(scores, axis=2)
    half_probs = probs.astype(BF)
    mixed = jnp.einsum("hqk,khd->qhd", half_probs, v, preferred_element_type=F32)
    mixed = mixed.reshape(SLOTS, D).astype(BF)
    middle = inputs + dot(mixed, w_out) + biases[4 * D : 5 * D]
    normed_two, inverse_two = norm_stats(middle)
    act_two = (normed_two * gains[D:] + biases[D : 2 * D]).astype(BF)
    hidden = dot(act_two, w_fc1) + biases[6 * D :]
    active, gelu_pull = jax.vjp(lambda h: jax.nn.gelu(h, approximate=False), hidden)
    active = active.astype(BF)
    out = middle + dot(active, w_fc2) + biases[5 * D : 6 * D]

    g_fc2 = dot_tn(active, cot)
    grad_hidden = gelu_pull(dot_nt(cot, w_fc2))[0].astype(BF)
    g_fc1 = dot_tn(act_two, grad_hidden)
    grad_two = dot_nt(grad_hidden, w_fc1)
    grad_middle = cotf + norm_back(grad_two, normed_two, inverse_two, gains[D:])
    branch = grad_middle.astype(BF)
    g_out = dot_tn(mixed, branch)
    grad_mixed = dot_nt(branch, w_out).astype(BF).reshape(SLOTS, HEADS, HEAD_DIM)
    grad_probs = jnp.einsum("qhd,khd->hqk", grad_mixed, v, preferred_element_type=F32)
    grad_scores = (probs * (grad_probs - jnp.sum(probs * grad_probs, axis=2, keepdims=True))).astype(BF)
    scale = HEAD_DIM ** (-0.5)
    grad_q = jnp.einsum("hqk,khd->qhd", grad_scores, k, preferred_element_type=F32) * scale
    grad_k = jnp.einsum("hqk,qhd->khd", grad_scores, q, preferred_element_type=F32) * scale
    grad_v = jnp.einsum("hqk,qhd->khd", half_probs, grad_mixed, preferred_element_type=F32)
    grad_qkv = jnp.stack([grad_q, grad_k, grad_v], axis=1).astype(BF).reshape(SLOTS, 3 * D)
    g_qkv = dot_tn(act_one, grad_qkv)
    grad_one = dot_nt(grad_qkv, w_qkv)
    grad_in = grad_middle + norm_back(grad_one, normed_one, inverse_one, gains[:D])

    g_gains = jnp.concatenate([jnp.sum(grad_one * normed_one, axis=0), jnp.sum(grad_two * normed_two, axis=0)])
    qkv_sums = jnp.sum(grad_qkv.astype(F32), axis=0)
    g_biases = jnp.concatenate([
        jnp.sum(grad_one, axis=0),
        jnp.sum(grad_two, axis=0),
        qkv_sums[:D],
        qkv_sums[2 * D :],
        jnp.sum(branch.astype(F32), axis=0),
        jnp.sum(cotf, axis=0),
        jnp.sum(grad_hidden.astype(F32), axis=0),
    ])
    return out, grad_in, g_qkv, g_out, g_fc1, g_fc2, g_gains, g_biases


def adam_step(weight, grad, first, second, rate, factor):
    clipped = grad * factor
    new_first = BETA_ONE * first + (1.0 - BETA_ONE) * clipped
    new_second = BETA_TWO * second + (1.0 - BETA_TWO) * clipped * clipped
    unbiased_first = new_first / (1.0 - BETA_ONE**STEP)
    unbiased_second = new_second / (1.0 - BETA_TWO**STEP)
    new_weight = weight - rate * (
        unbiased_first / (jnp.sqrt(unbiased_second) + ADAM_EPS) + DECAY * weight
    )
    return (new_first, new_second, new_weight, new_weight.astype(BF))


def gather(value, axes):
    for name, dim in axes:
        value = lax.all_gather(value, name, axis=dim, tiled=True)
    return value


def scatter(value, axes):
    for name, dim in axes:
        value = lax.psum_scatter(value, name, scatter_dimension=dim, tiled=True)
    return value.astype(F32)


def local_plain(
    layer_in, grad_out, crop_ids, w_qkv, w_out, w_fc1, w_fc2, norm_gains, all_biases,
    first_qkv, second_qkv, first_out, second_out, first_fc1, second_fc1, first_fc2, second_fc2,
    first_gains, second_gains, first_biases, second_biases,
):
    row = lax.axis_index("row")
    n_row, n_col = lax.axis_size("row"), lax.axis_size("col")
    feat = D // n_row
    pairs = layer_in.shape[0]
    labels = lax.ppermute(
        crop_ids, ("row", "col"), [(r * n_col + c, c * n_row + r) for r in range(n_row) for c in range(n_col)]
    )
    sources = slot_sources(labels).reshape(-1)
    place = jnp.where(sources < 0, -1, (sources % 2) * pairs + sources // 2)
    pick = (place[:, None] == jnp.arange(2 * pairs, dtype=jnp.int32)[None, :]).astype(BF)

    def to_slots(value):
        halves = jnp.concatenate([value[:, 0, :feat], value[:, 0, feat:]], axis=0)
        sent = dot(pick, halves).astype(BF)
        got = lax.all_to_all(sent, "row", 0, 0, tiled=True)
        return got.reshape(n_row, SLOTS, feat).transpose(1, 0, 2).reshape(SLOTS, D)

    def to_tokens(value):
        sent = value.astype(BF).reshape(SLOTS, n_row, feat).transpose(1, 0, 2).reshape(n_row * SLOTS, feat)
        got = lax.all_to_all(sent, "row", 0, 0, tiled=True)
        halves = dot_tn(pick, got)
        return jnp.concatenate([halves[:pairs], halves[pairs:]], axis=1).reshape(pairs, 1, 2 * feat)

    full_qkv = gather(w_qkv.astype(BF), (("dp", 0), ("row", 0), ("col", 2))).reshape(D, 3 * D)
    full_out = gather(w_out.astype(BF), (("dp", 0), ("col", 0), ("row", 1)))
    full_fc1 = gather(w_fc1.astype(BF), (("dp", 0), ("row", 0), ("col", 1)))
    full_fc2 = gather(w_fc2.astype(BF), (("dp", 0), ("col", 0), ("row", 1)))
    crops = jnp.where(row < 2, slot_crops(0), slot_crops(1))
    out, grad_in, g_qkv, g_out, g_fc1, g_fc2, g_gains, g_biases = layer(
        to_slots(layer_in), to_slots(grad_out), crops, full_qkv, full_out, full_fc1, full_fc2, norm_gains, all_biases
    )
    owned_qkv = scatter(g_qkv.astype(BF).reshape(D, 3, D), (("col", 2), ("row", 0), ("dp", 0)))
    owned_out = scatter(g_out.astype(BF), (("row", 1), ("col", 0), ("dp", 0)))
    owned_fc1 = scatter(g_fc1.astype(BF), (("col", 1), ("row", 0), ("dp", 0)))
    owned_fc2 = scatter(g_fc2.astype(BF), (("row", 1), ("col", 0), ("dp", 0)))
    local_squares = (
        jnp.sum(owned_qkv * owned_qkv)
        + jnp.sum(owned_out * owned_out)
        + jnp.sum(owned_fc1 * owned_fc1)
        + jnp.sum(owned_fc2 * owned_fc2)
    )
    grad_gains, grad_biases, weight_squares = lax.psum((g_gains, g_biases, local_squares), ("dp", "row", "col"))
    grad_norm = jnp.sqrt(weight_squares + jnp.sum(grad_gains * grad_gains) + jnp.sum(grad_biases * grad_biases))
    factor = jnp.minimum(1.0, CLIP_NORM / grad_norm)
    upd_qkv = adam_step(w_qkv, owned_qkv, first_qkv, second_qkv, D ** (-0.5), factor)
    upd_out = adam_step(w_out, owned_out, first_out, second_out, (D // 24) ** (-0.5), factor)
    upd_fc1 = adam_step(w_fc1, owned_fc1, first_fc1, second_fc1, D ** (-0.5), factor)
    upd_fc2 = adam_step(w_fc2, owned_fc2, first_fc2, second_fc2, FF ** (-0.5), factor)
    upd_gains = adam_step(norm_gains, grad_gains, first_gains, second_gains, 0.3, factor)
    upd_biases = adam_step(all_biases, grad_biases, first_biases, second_biases, 0.3, factor)
    return (
        to_tokens(out), to_tokens(grad_in), grad_norm,
        *upd_qkv, *upd_out, *upd_fc1, *upd_fc2, *upd_gains, *upd_biases,
    )


def solution(mesh):
    tokens = P(("dp", "col"), "row", None)
    qkv = P(("row", "dp"), None, "col")
    out = P(("col", "dp"), "row")
    fc1 = P(("row", "dp"), "col")
    whole = P()
    return jax.shard_map(
        local_fast if mesh.shape["dp"] == 2 else local_plain,
        mesh=mesh,
        in_specs=(
            tokens, tokens, P(("dp", "row")), qkv, out, fc1, out, whole, whole,
            qkv, qkv, out, out, fc1, fc1, out, out, whole, whole, whole, whole,
        ),
        out_specs=(tokens, tokens, whole) + (qkv,) * 4 + (out,) * 4 + (fc1,) * 4 + (out,) * 4 + (whole,) * 8,
        check_vma=False,
    )
```

```python
import functools

import jax
import jax.numpy as jnp
from jax import lax
from jax.experimental import pallas as pl
from jax.experimental.pallas import tpu as pltpu
from jax.sharding import PartitionSpec as P

HEADS = 12
HEAD_DIM = 64
FF = 3072
D = 768
BIG_CROP = 197
SMALL_CROP = 37
IMAGE_LEN = 690
CROPS = 10
STEP = 5

NORM_EPS = 1e-06
CLIP_NORM = 1.0
BETA_ONE = 0.5
BETA_TWO = 0.5
ADAM_EPS = 1e-08
DECAY = 0.05
MASKED = -1e30

SLOTS = 544
BIG_SLOTS = 208
TRIO_SLOTS = 112
TRIO = 3 * SMALL_CROP
BF = jnp.bfloat16
F32 = jnp.float32


def crop_starts(labels):
    images = labels.shape[0] // IMAGE_LEN
    places = labels.reshape(images, IMAGE_LEN) % CROPS
    order = jnp.arange(CROPS, dtype=jnp.int32)
    sizes = jnp.sum((places[:, :, None] == order).astype(jnp.int32), axis=1)
    starts = jnp.sum((places[:, :, None] < order).astype(jnp.int32), axis=1)
    starts = starts + IMAGE_LEN * jnp.arange(images, dtype=jnp.int32)[:, None]
    big = (sizes == BIG_CROP).astype(jnp.int32)
    earlier = (order[:, None] < order[None, :]).astype(jnp.int32)
    big_rank = jnp.sum(big[:, :, None] * earlier, axis=1)
    small_rank = jnp.sum((1 - big)[:, :, None] * earlier, axis=1)

    def ranked(flag, rank, count):
        hit = flag[:, :, None] * (rank[:, :, None] == jnp.arange(count, dtype=jnp.int32)).astype(jnp.int32)
        return jnp.sum(hit * starts[:, :, None], axis=1).reshape(-1)

    return ranked(big, big_rank, 2), ranked(1 - big, small_rank, CROPS - 2)


def slot_segments(kind):
    if kind == 0:
        bigs, trios = 2, 1
    else:
        bigs, trios = 1, 3
    parts = []
    at = 0
    for b in range(bigs):
        parts.append((at, BIG_CROP, True, b))
        at += BIG_SLOTS
    for s in range(3 * trios):
        parts.append((at + s // 3 * TRIO_SLOTS + s % 3 * SMALL_CROP, SMALL_CROP, False, s))
    return parts


def slot_sources(labels):
    big, small = crop_starts(labels)
    rows = []
    for row in range(4):
        kind = row // 2
        at_big = (0, 2, 4, 5)[row]
        at_small = (0, 3, 6, 15)[row]
        out = []
        filled = 0
        for first, length, is_big, index in slot_segments(kind):
            if first > filled:
                out.append(jnp.full((first - filled,), -1, jnp.int32))
            start = big[at_big + index] if is_big else small[at_small + index]
            out.append(start + jnp.arange(length, dtype=jnp.int32))
            filled = first + length
        if filled < SLOTS:
            out.append(jnp.full((SLOTS - filled,), -1, jnp.int32))
        rows.append(jnp.concatenate(out))
    return jnp.stack(rows)


def slot_crops(kind):
    slot = jnp.arange(SLOTS, dtype=jnp.int32)
    crop = jnp.full((SLOTS,), -1, jnp.int32)
    for number, (first, length, _, _) in enumerate(slot_segments(kind)):
        crop = jnp.where((slot >= first) & (slot < first + length), number, crop)
    return crop


MESH = pl.DeviceIdType.MESH
HALF = 64
QW = 640
TOK = 1040
CHUNK = 32
BLOCK = SLOTS + SLOTS // 2
WQ, WO, W1, W2 = 0, 1, 2, 3
VMEM_LIMIT = 60 * 2**20


def mm(a, b):
    return lax.dot_general(a, b, (((1,), (0,)), ((), ())), preferred_element_type=F32)


def mm_nt(a, b):
    return lax.dot_general(a, b, (((1,), (1,)), ((), ())), preferred_element_type=F32)


def mm_tn(a, b):
    return lax.dot_general(a, b, (((0,), (0,)), ((), ())), preferred_element_type=F32)


class Place:
    def __init__(self):
        self.y = lax.axis_index("dp")
        self.z = lax.axis_index("row")
        self.c = lax.axis_index("col")
        self.core = lax.rem(self.c, 2)
        self.x = lax.div(self.c, 2)
        self.cx = lax.rem(self.c + 2, 4)
        self.cs = self.c + 1 - 2 * self.core
        self.xn = (self.y, self.z, self.cx)
        self.yn = (1 - self.y, self.z, self.c)
        self.cn = (self.y, self.z, self.cs)
        self.low = self.z < 2
        self.mid = jnp.logical_or(self.z == 1, self.z == 2)
        self.step = jnp.where(self.low, 1, -1)

    def zth(self, z):
        return (self.y, z, self.c)

    def other(self, j):
        return lax.rem(self.z + self.step * j + 4, 4)

    def enter(self):
        barrier = pltpu.get_barrier_semaphore()
        peers = [self.zth(lax.rem(self.z + k, 4)) for k in (1, 2, 3)] + [self.xn, self.yn, self.cn]
        for peer in peers:
            pl.semaphore_signal(barrier, inc=1, device_id=peer, device_id_type=MESH)
        pl.semaphore_wait(barrier, len(peers))


def shard_of(refs, p, c, s, y):
    ref = refs[p]
    if p == WO:
        return ref.at[s, c, pl.ds(pl.multiple_of(y * 96, 32), 96), :]
    if p == W2:
        return ref.at[c, s, :, pl.ds(pl.multiple_of(y * 384, 128), 384)]
    return ref.at[c, s, y]


def group_of(refs, p, c, y):
    ref = refs[p]
    if p == WO:
        return ref.at[:, c, pl.ds(pl.multiple_of(y * 96, 32), 96), :]
    if p == W2:
        return ref.at[c, :, :, pl.ds(pl.multiple_of(y * 384, 128), 384)]
    return ref.at[c, :, y]


class Sends:
    def __init__(self):
        self.left = []

    def start(self, src, dst, send_sem, recv_sem, peer, when=None):
        copy = pltpu.make_async_remote_copy(
            src_ref=src, dst_ref=dst, send_sem=send_sem, recv_sem=recv_sem, device_id=peer, device_id_type=MESH
        )
        if when is None:
            copy.start()
        else:
            pl.when(when)(copy.start)
        self.left.append((copy, when))

    def drain(self):
        for copy, when in self.left:
            if when is None:
                copy.wait_send()
            else:
                pl.when(when)(copy.wait_send)
        self.left = []


def arrived(ref, sem, me):
    pltpu.make_async_remote_copy(
        src_ref=ref, dst_ref=ref, send_sem=sem, recv_sem=sem, device_id=me, device_id_type=MESH
    ).wait_recv()


class Gather:
    def __init__(self, at, refs, sends, direct, zs, zr, xs, xr, ys, yr, ds, dr, cs, cr):
        self.at, self.refs, self.sends, self.direct = at, refs, sends, direct
        self.zs, self.zr, self.xs, self.xr = zs, zr, xs, xr
        self.ys, self.yr, self.ds, self.dr, self.cs, self.cr = ys, yr, ds, dr, cs, cr

    def across(self, p, s):
        at = self.at
        own = shard_of(self.refs, p, at.c, s, at.y)
        self.sends.start(own, own, self.xs.at[p, s], self.xr.at[p, s], at.xn)
        self.sends.start(own, own, self.ys.at[p, s], self.yr.at[p, s], at.yn)

    def own_across(self, p):
        self.across(p, self.at.z)

    def own_along(self, p):
        at = self.at
        own = shard_of(self.refs, p, at.c, at.z, at.y)
        if p in self.direct:
            for j in (1, 2, 3):
                self.sends.start(own, own, self.zs.at[p, j - 1], self.zr.at[p, at.z], at.zth(at.other(j)))
            return
        second = jnp.where(at.mid, at.z - at.step, at.z + 2 * at.step)
        self.sends.start(own, own, self.zs.at[p, 0], self.zr.at[p, at.z], at.zth(at.z + at.step))
        self.sends.start(own, own, self.zs.at[p, 1], self.zr.at[p, at.z], at.zth(second))

    def to_core(self, p, g, c, y):
        ref = group_of(self.refs, p, c, y)
        self.sends.start(ref, ref, self.cs.at[p, g], self.cr.at[p, g], self.at.cn)

    def along(self, p, j):
        at = self.at
        s = at.other(j)
        ref = shard_of(self.refs, p, at.c, s, at.y)
        arrived(ref, self.zr.at[p, s], at.yn)
        if j < 3 and p not in self.direct:
            self.sends.start(ref, ref, self.zs.at[p, 1 + j], self.zr.at[p, s], at.zth(at.z - at.step), when=at.mid)
        self.across(p, s)
        if j == 3:
            self.to_core(p, 0, at.c, at.y)

    def cross(self, p, j):
        at = self.at
        s = at.other(j)
        from_x = shard_of(self.refs, p, at.cx, s, at.y)
        from_y = shard_of(self.refs, p, at.c, s, 1 - at.y)
        arrived(from_x, self.xr.at[p, s], at.yn)
        arrived(from_y, self.yr.at[p, s], at.yn)
        if j < 2:
            self.sends.start(from_x, from_x, self.ds.at[p, j], self.dr.at[p, s], at.yn)
        else:
            self.sends.start(from_y, from_y, self.ds.at[p, j], self.dr.at[p, s], at.xn)
        if j == 3:
            self.to_core(p, 1, at.cx, at.y)
            self.to_core(p, 2, at.c, 1 - at.y)

    def corner(self, p):
        at = self.at
        for j in (0, 1, 2, 3):
            s = at.other(j)
            arrived(shard_of(self.refs, p, at.cx, s, 1 - at.y), self.dr.at[p, s], at.yn)
        self.to_core(p, 3, at.cx, 1 - at.y)

    def ready(self, p, half):
        at = self.at
        c = at.cs if half == 0 else at.cs + 2 - 4 * at.x
        arrived(group_of(self.refs, p, c, at.y), self.cr.at[p, half], at.yn)
        arrived(group_of(self.refs, p, c, 1 - at.y), self.cr.at[p, 2 + half], at.yn)


def exchange_start(at, sends, blocks, landing, send_sems, recv_sems):
    for k in (1, 2, 3):
        to = lax.rem(at.z + k, 4)
        sends.start(blocks.at[to], landing.at[at.z], send_sems.at[k - 1], recv_sems.at[at.z], at.zth(to))


def exchange_wait(at, landing, recv_sems):
    for k in (1, 2, 3):
        s = lax.rem(at.z + k, 4)
        arrived(landing.at[s], recv_sems.at[s], at.yn)


def row_stats(value):
    centre = jnp.sum(value, axis=1, keepdims=True) * (1.0 / D)
    centred = value - centre
    spread = jnp.sum(centred * centred, axis=1, keepdims=True) * (1.0 / D)
    inverse = lax.rsqrt(spread + NORM_EPS)
    return centred * inverse, inverse


def chunks(body):
    for i in range(SLOTS // CHUNK):
        body(i, slice(i * CHUNK, i * CHUNK + CHUNK))


def put_block(ref, r, i, value):
    ref[r, i * CHUNK : i * CHUNK + CHUNK, :] = value[:, 0:128]
    first = SLOTS + i * (CHUNK // 2)
    ref[r, first : first + CHUNK // 2, :] = jnp.concatenate([value[0:16, 128:192], value[16:32, 128:192]], axis=1)


def get_blocks(ref, i):
    parts = []
    first = SLOTS + i * (CHUNK // 2)
    for r in range(4):
        parts.append(ref[r, i * CHUNK : i * CHUNK + CHUNK, :])
        rest = ref[r, first : first + CHUNK // 2, :]
        parts.append(jnp.concatenate([rest[:, 0:HALF], rest[:, HALF:]], axis=0))
    return jnp.concatenate(parts, axis=1)


def loop(count, body):
    def step(i, carry):
        body(i)
        return carry

    lax.fori_loop(0, count, step, 0)


def lane_low(rows):
    return lax.broadcasted_iota(jnp.int32, (rows, 2 * HALF), 1) < HALF


def swap_halves(value):
    return jnp.concatenate([value[:, HALF:], value[:, :HALF]], axis=1)


def segments(at, body):
    bigs = jnp.where(at.low, 2, 1)

    def big(i, carry):
        body(pl.multiple_of(i * BIG_SLOTS, 16), True, i)
        return carry

    def trio(i, carry):
        body(pl.multiple_of(bigs * BIG_SLOTS + i * TRIO_SLOTS, 16), False, i)
        return carry

    lax.fori_loop(0, bigs, big, 0)
    lax.fori_loop(0, jnp.where(at.low, 1, 3), trio, 0)


def key_mask(size, is_big):
    key = lax.broadcasted_iota(jnp.int32, (size, size), 1)
    if is_big:
        return key < BIG_CROP
    query = lax.broadcasted_iota(jnp.int32, (size, size), 0)

    def crop(v):
        return (v >= SMALL_CROP).astype(jnp.int32) + (v >= 2 * SMALL_CROP).astype(jnp.int32) + (v >= TRIO).astype(jnp.int32)

    return jnp.logical_and(crop(query) == crop(key), key < TRIO)


def attend_segment(c, first, is_big, index, qkv, mixed, pbig, ptrio):
    size = BIG_SLOTS if is_big else TRIO_SLOTS
    rows = pl.ds(first, size)
    q01 = qkv[c, rows, 0:128]
    k01 = qkv[c, rows, 128:256]
    v01 = qkv[c, rows, 256:384]
    qk2 = qkv[c, rows, 384:512]
    v2 = qkv[c, rows, 512:640]
    low = lane_low(size)
    none = jnp.zeros((size, 128), BF)
    mask = key_mask(size, is_big)
    outs = []
    for h, (q, k, v) in enumerate((
        (jnp.where(low, q01, none), k01, v01),
        (jnp.where(low, none, q01), k01, v01),
        (jnp.where(low, qk2, none), swap_halves(qk2), v2),
    )):
        scores = jnp.where(mask, mm_nt(q, k) * HEAD_DIM**-0.5, MASKED)
        weights = jnp.exp(scores - jnp.max(scores, axis=1, keepdims=True))
        total = jnp.sum(weights, axis=1, keepdims=True)
        weights = (weights * (1.0 / total)).astype(BF)
        if is_big:
            pbig[c, h, index] = weights
        else:
            ptrio[c, h, index] = weights
        outs.append(mm(weights, v))
    mixed[rows, pl.ds(pl.multiple_of(c * 256, 256), 128)] = jnp.where(low, outs[0], outs[1]).astype(BF)
    mixed[rows, pl.ds(pl.multiple_of(c * 256 + 128, 128), 128)] = outs[2].astype(BF)


def attend(at, c, qkv, mixed, pbig, ptrio):
    mixed[SLOTS - 16 : SLOTS, pl.ds(pl.multiple_of(c * 256, 256), 256)] = jnp.zeros((16, 256), BF)
    segments(at, lambda first, is_big, i: attend_segment(c, first, is_big, i, qkv, mixed, pbig, ptrio))


def transpose_into(dst, src, tiles):
    def body(j):
        lanes = pl.ds(pl.multiple_of(j * 128, 128), 128)
        dst[lanes, :] = src[:, lanes].T

    loop(tiles, body)


def count_crops(labels, first_image):
    images = labels.shape[0]
    image = lax.broadcasted_iota(jnp.int32, labels.shape, 0)
    crop = labels - CROPS * (first_image + image)
    lane = lax.broadcasted_iota(jnp.int32, (images, 128), 1)
    offset = (IMAGE_LEN * lax.broadcasted_iota(jnp.int32, (images, 1), 0)).astype(F32)
    table = jnp.zeros((images, 128), F32)
    bigs = jnp.zeros((images, 1), F32)
    for p in range(CROPS):
        size = jnp.sum((crop == p).astype(F32), axis=1, keepdims=True)
        start = jnp.sum((crop < p).astype(F32), axis=1, keepdims=True) + offset
        big = (size == float(BIG_CROP)).astype(F32)
        at_lane = jnp.where(big > 0.5, bigs, 2.0 + float(p) - bigs)
        table = jnp.where(lane == at_lane.astype(jnp.int32), start, table)
        bigs = bigs + big
    return table


def slot_tokens(table, row, shape, dim):
    slot = lax.broadcasted_iota(jnp.int32, shape, dim)
    token = jnp.full(shape, -1, jnp.int32)
    at_big = (0, 2, 4, 5)[row]
    at_small = (0, 3, 6, 15)[row]
    for first, length, is_big, index in slot_segments(row // 2):
        if is_big:
            k = at_big + index
            start = table[k // 2 : k // 2 + 1, k % 2 : k % 2 + 1]
        else:
            k = at_small + index
            start = table[k // 8 : k // 8 + 1, 2 + k % 8 : 3 + k % 8]
        inside = jnp.logical_and(slot >= first, slot < first + length)
        token = jnp.where(inside, start.astype(jnp.int32) + (slot - first), token)
    return jnp.where(token < 0, -1, (token & 1) * TOK + (token >> 1))


def forward_kernel(
    x_in, g_in, labels, wq_in, wo_in, w1_in, w2_in, gains_in, biases_in,
    wq_h, wo_h, w1_h, w2_h, x_h, mid_h, a1t_h, a2t_h, mixt_h, qkv_h, pbig_h, ptrio_h, act_h, slope_h, cot_h, cott_h, out_h, where_h,
    wq, wo, w1, w2, tok, send_x, send_g, land_x, land_g, x, mid, midb, a1, a1t, a2t, mixed, mixt, qkv, pbig, ptrio,
    act, slope, cot, cott, gains, biases, fc1_bias, qkv_bias, tables, column, where, branch_two,
    zs, zr, xs, xr, ys, yr, ds, dr, cs, cr, exs, exr, egs, egr, tbs, tbr, hs,
):
    at = Place()
    refs = (wq, wo, w1, w2)
    sends = Sends()
    gather = Gather(at, refs, sends, FORWARD_DIRECT, zs, zr, xs, xr, ys, yr, ds, dr, cs, cr)
    stores = []

    def keep(src, dst):
        copy = pltpu.make_async_copy(src, dst, hs.at[len(stores)])
        copy.start()
        stores.append(copy)

    pairs = x_in.shape[0]
    wqv, wov = wq.reshape(4, 768, QW), wo.reshape(4, 1024, 192)
    w1v, w2v = w1.reshape(4, 768, 768), w2.reshape(4, 768, 768)
    groups = (at.c, at.cs, at.cx, at.cs + 2 - 4 * at.x)

    def joined(ref, first, count):
        return jnp.concatenate([ref[first + i : first + i + 1, :] for i in range(count)], axis=1)

    def start():
        tables[at.z] = jnp.zeros((8, 128), F32)
        tables[at.z, 0:3, :] = count_crops(labels[...], (at.y * 4 + at.z) * 3)
        heads = [wq_in[n].astype(BF) for n in range(3)]
        wq[at.c, at.z, at.y] = jnp.concatenate(
            [v[:, 0:128] for v in heads] + [v[:, 128:192] for v in heads] + [jnp.zeros((96, HALF), BF)], axis=1
        )
        wo[at.z, at.c, pl.ds(pl.multiple_of(at.y * 96, 32), 96), :] = wo_in[...].astype(BF)
        w1[at.c, at.z, at.y] = w1_in[...].astype(BF)
        w2[at.c, at.z, :, pl.ds(pl.multiple_of(at.y * 384, 128), 384)] = w2_in[...].astype(BF)
        at.enter()
        for k in (1, 2, 3):
            sends.start(tables.at[at.z], tables.at[at.z], tbs.at[k - 1], tbr.at[at.z], at.zth(lax.rem(at.z + k, 4)))

    def pick(n, send):
        for half in (0, 1):
            ref = x_in if n == 0 else g_in
            tok[n, half * TOK + TOK - 16 : half * TOK + TOK, :] = jnp.zeros((16, 192), BF)
            tok[n, half * TOK : half * TOK + pairs, :] = ref[:, half * 192 : half * 192 + 192]

        def block(r):
            one = (lax.broadcasted_iota(jnp.int32, (SLOTS, 2 * TOK), 1) == column[r]).astype(F32).astype(BF)
            value = mm(one, tok[n]).astype(BF)
            for i in range(SLOTS // CHUNK):
                put_block(send, r, i, value[i * CHUNK : i * CHUNK + CHUNK])

        loop(4, block)

    def pick_x():
        for k in (1, 2, 3):
            s = lax.rem(at.z + k, 4)
            arrived(tables.at[s], tbr.at[s], at.yn)
        table = tables[at.c]
        for r in range(4):
            column[r] = slot_tokens(table, r, (SLOTS, 1), 0)
            where[r] = slot_tokens(table, r, (1, SLOTS), 1)
        keep(where, where_h)
        pick(0, send_x)
        land_x[at.z] = send_x[at.z]
        wo[:, :, 192:256, :] = jnp.zeros((4, 4, 64, 192), BF)
        for n in (0, 1):
            gains[n : n + 1, :] = joined(gains_in, 6 * n, 6)
        for n in range(6):
            biases[n : n + 1, :] = joined(biases_in, 6 * n, 6)
        nothing = jnp.zeros((1, 128), F32)
        for c in range(4):
            fc1_bias[c] = joined(biases_in, 36 + 6 * c, 6)
            q = biases[2:3, c * 192 : c * 192 + 192]
            v = biases[3:4, c * 192 : c * 192 + 192]
            qkv_bias[c] = jnp.concatenate(
                [q[:, 0:128], nothing, v[:, 0:128], q[:, 128:192], nothing[:, 0:HALF], v[:, 128:192], nothing[:, 0:HALF]],
                axis=1,
            )

    def pick_g():
        pick(1, send_g)
        land_g[at.z] = send_g[at.z]

    def norm_one():
        def one(i, rows):
            value = get_blocks(land_x, i)
            x[rows, :] = value
            normed, _ = row_stats(value.astype(F32))
            a1[rows, :] = (normed * gains[0:1, :] + biases[0:1, :]).astype(BF)

        chunks(one)
        keep(x, x_h)

    def project(i):
        c = groups[i]
        for n in range(0, QW, 256):
            wide = min(256, QW - n)
            qkv[c, :, n : n + wide] = (mm(a1[...], wqv[c, :, n : n + wide]) + qkv_bias[c, :, n : n + wide]).astype(BF)

    def transpose_one():
        transpose_into(a1t, a1, 6)
        a1t[768:784, :] = jnp.ones((16, SLOTS), BF)
        keep(a1t, a1t_h)

    def branch():
        def one(z):
            midb[z] = mm(mixed[...], wov[z])

        loop(4, one)
        keep(qkv, qkv_h)
        keep(pbig, pbig_h)
        keep(ptrio, ptrio_h)

    def norm_two():
        def one(i, rows):
            value = x[rows, :].astype(F32) + jnp.concatenate([midb[r, rows, :] for r in range(4)], axis=1) + biases[4:5, :]
            mid[rows, :] = value
            normed, _ = row_stats(value)
            a1[rows, :] = (normed * gains[1:2, :] + biases[1:2, :]).astype(BF)

        chunks(one)
        keep(mid, mid_h)

    def expand(i):
        c = groups[i]

        def tile(n):
            lanes = pl.ds(pl.multiple_of(n * 256, 256), 256)
            hidden = mm(a1[...], w1v[c, :, lanes]) + fc1_bias[c, :, lanes]
            share = 0.5 + 0.5 * lax.erf(hidden * 0.7071067811865476)
            bell = jnp.exp(hidden * hidden * -0.5) * 0.3989422804014327
            act[c, :, lanes] = (hidden * share).astype(BF)
            slope[c, :, lanes] = (share + hidden * bell).astype(BF)

        loop(3, tile)
        keep(act.at[c], act_h.at[c])
        keep(slope.at[c], slope_h.at[c])

    def transpose_two():
        transpose_into(a2t, a1, 6)
        a2t[768:784, :] = jnp.ones((16, SLOTS), BF)
        keep(a2t, a2t_h)

    def transpose_mixed():
        transpose_into(mixt, mixed, 8)
        mixt[192:208, :] = jnp.ones((16, SLOTS), BF)
        keep(mixt, mixt_h)

    def join():
        def one(i, rows):
            cot[rows, :] = get_blocks(land_g, i)

        chunks(one)
        keep(cot, cot_h)

    def transpose_cot():
        transpose_into(cott, cot, 6)
        keep(cott, cott_h)

    def contract(i):
        c = groups[i]

        def tile(n):
            rows = pl.ds(pl.multiple_of(n * 256, 256), 256)
            part = mm_nt(act[c], w2v[c, rows, :])
            if i == 0:
                branch_two[:, rows] = part + biases[5:6, rows] + mid[:, rows]
            else:
                branch_two[:, rows] = branch_two[:, rows] + part

        loop(3, tile)

    def split():
        def one(i, rows):
            value = branch_two[rows, :].astype(BF)
            for r in range(4):
                put_block(land_x, r, i, value[:, r * 192 : r * 192 + 192])

        chunks(one)
        keep(land_x, out_h)

    def ready_b(p):
        gather.ready(p, 1)
        keep((wqv, wov, w1v, w2v)[p], (wq_h, wo_h, w1_h, w2_h)[p])

    steps = {
        "start": start, "pickX": pick_x, "pickG": pick_g, "norm1": norm_one, "a1t": transpose_one, "branch": branch,
        "norm2": norm_two, "a2t": transpose_two, "mixt": transpose_mixed, "cot": join, "cott": transpose_cot, "split": split,
        "exX": lambda: exchange_start(at, sends, send_x, land_x, exs, exr),
        "exG": lambda: exchange_start(at, sends, send_g, land_g, egs, egr),
        "exwX": lambda: exchange_wait(at, land_x, exr),
        "exwG": lambda: exchange_wait(at, land_g, egr),
    }
    many = {
        "qkv": project, "att": lambda i: attend(at, groups[i], qkv, mixed, pbig, ptrio), "fc1": expand, "fc2": contract,
    }
    for name, step in many.items():
        for i in range(4):
            steps[f"{name}{i}"] = functools.partial(step, i)
    weights = {"WQ": WQ, "WO": WO, "W1": W1, "W2": W2}
    for name, p in weights.items():
        steps[f"own_across {name}"] = functools.partial(gather.own_across, p)
        steps[f"own_along {name}"] = functools.partial(gather.own_along, p)
        steps[f"corner {name}"] = functools.partial(gather.corner, p)
        steps[f"readyA {name}"] = functools.partial(gather.ready, p, 0)
        steps[f"readyB {name}"] = functools.partial(ready_b, p)
        for j in range(4):
            steps[f"along {name} {j}"] = functools.partial(gather.along, p, j)
            steps[f"cross {name} {j}"] = functools.partial(gather.cross, p, j)
    for name in FORWARD_ORDER:
        steps[name]()
    sends.drain()
    for copy in stores:
        copy.wait()


FORWARD_OUT = (
    ((4, 768, QW), BF), ((4, 1024, 192), BF), ((4, 768, 768), BF), ((4, 768, 768), BF),
    ((SLOTS, D), BF), ((SLOTS, D), F32), ((784, SLOTS), BF), ((784, SLOTS), BF), ((1024, SLOTS), BF),
    ((4, SLOTS, QW), BF), ((4, 3, 2, BIG_SLOTS, BIG_SLOTS), BF), ((4, 3, 3, TRIO_SLOTS, TRIO_SLOTS), BF),
    ((4, SLOTS, 768), BF), ((4, SLOTS, 768), BF), ((SLOTS, D), BF), ((D, SLOTS), BF), ((4, BLOCK, 128), BF),
    ((4, 1, SLOTS), jnp.int32),
)


def run_forward(*operands):
    sem = pltpu.SemaphoreType.DMA
    vmem = pltpu.VMEM
    return pl.pallas_call(
        forward_kernel,
        out_shape=[jax.ShapeDtypeStruct(s, t) for s, t in FORWARD_OUT],
        in_specs=[pl.BlockSpec(memory_space=vmem)] * len(operands),
        out_specs=[pl.BlockSpec(memory_space=pl.ANY)] * len(FORWARD_OUT),
        scratch_shapes=[
            vmem((4, 4, 2, 96, QW), BF), vmem((4, 4, 256, 192), BF), vmem((4, 4, 2, 96, 768), BF), vmem((4, 4, 192, 768), BF),
            vmem((2, 2 * TOK, 192), BF),
            vmem((4, BLOCK, 128), BF), vmem((4, BLOCK, 128), BF), vmem((4, BLOCK, 128), BF), vmem((4, BLOCK, 128), BF),
            vmem((SLOTS, D), BF), vmem((SLOTS, D), F32), vmem((4, SLOTS, 192), F32), vmem((SLOTS, D), BF),
            vmem((784, SLOTS), BF), vmem((784, SLOTS), BF), vmem((SLOTS, 1024), BF), vmem((1024, SLOTS), BF),
            vmem((4, SLOTS, QW), BF), vmem((4, 3, 2, BIG_SLOTS, BIG_SLOTS), BF), vmem((4, 3, 3, TRIO_SLOTS, TRIO_SLOTS), BF),
            vmem((4, SLOTS, 768), BF), vmem((4, SLOTS, 768), BF), vmem((SLOTS, D), BF), vmem((D, SLOTS), BF),
            vmem((2, D), F32), vmem((6, D), F32), vmem((4, 1, D), F32), vmem((4, 1, QW), F32), vmem((4, 8, 128), F32),
            vmem((4, SLOTS, 1), jnp.int32), vmem((4, 1, SLOTS), jnp.int32), vmem((SLOTS, D), F32),
            sem((4, 4)), sem((4, 4)), sem((4, 4)), sem((4, 4)), sem((4, 4)), sem((4, 4)), sem((4, 4)), sem((4, 4)),
            sem((4, 4)), sem((4, 4)), sem((3,)), sem((4,)), sem((3,)), sem((4,)), sem((3,)), sem((4,)), sem((len(FORWARD_OUT) + 6,)),
        ],
        compiler_params=pltpu.CompilerParams(collective_id=0, has_side_effects=True, vmem_limit_bytes=VMEM_LIMIT),
    )(*operands)


FORWARD_ORDER = (
    "start", "own_along WQ", "own_across W1", "own_across WO", "own_along WO", "along WQ 1", "along WO 1",
    "own_along W1", "own_across W2", "pickX", "exX", "along WQ 2", "along WO 2", "cross W2 0", "own_across WQ",
    "pickG", "along W1 1", "cross WQ 0", "cross WQ 1", "along WQ 3", "along WO 3", "cross WQ 2", "cross WO 0",
    "cross WO 1", "along W1 2", "cross WQ 3", "own_along W2", "along W1 3", "along W2 1", "exG", "exwX", "readyA WQ",
    "cross W1 0", "corner WQ", "norm1", "cross WO 2", "cross W1 1", "qkv2", "cross WO 3", "readyB WQ", "att2",
    "cross W1 2", "a1t", "qkv3", "qkv0", "att3", "corner WO", "qkv1", "att0", "readyA WO", "cross W1 3", "readyB WO",
    "along W2 2", "att1", "readyA W1", "branch", "norm2", "corner W1", "fc10", "readyB W1", "fc12", "along W2 3",
    "cross W2 1", "a2t", "cross W2 2", "mixt", "fc11", "cross W2 3", "fc20", "fc13", "readyA W2", "fc21", "exwG",
    "cot", "cott", "corner W2", "fc22", "readyB W2", "fc23", "split",
)
FORWARD_DIRECT = ()


def parts_of(ref, p, *lead, count=1):
    *outer, first = lead
    if p != W2:
        return ref.at[(*outer, first) if count == 1 else (*outer, pl.ds(first, count))]
    rows = pl.ds(pl.multiple_of(first * 192, 192), count * 192)
    return ref.at[(*outer[:-1], rows, pl.ds(pl.multiple_of(outer[-1] * 384, 128), 384))]


class Reduce:
    def __init__(self, at, sends, grads, pair, corner, cross, along, owned, squares, direct, sems):
        self.at, self.sends = at, sends
        self.grads, self.pair, self.corner, self.cross, self.along = grads, pair, corner, cross, along
        self.owned, self.squares, self.direct = owned, squares, direct
        self.ss, self.rs = sems

    def start(self, p, n, src, dst, peer, arrival=None, when=None):
        self.sends.start(src, dst, self.ss.at[p, n], self.rs.at[p, n if arrival is None else arrival], peer, when=when)

    def grad(self, p, c, y, s, count=1):
        return parts_of(self.grads[p], p, c, y, s, count=count)

    def half(self, ref, p, i, first):
        if p != W2:
            return ref.at[i, pl.ds(first, 2)]
        return ref.at[i, pl.ds(first * 192, 384)]

    def one(self, ref, p, i, s):
        return ref.at[i, s] if p != W2 else ref.at[i, pl.ds(pl.multiple_of(s * 192, 192), 192)]

    def far_and_near(self, i):
        return self.at.cx if i == 0 else self.at.c

    def pair_send(self, p, i):
        at = self.at
        c = 2 * ((1 - at.x) if i == 0 else at.x) + 1 - at.core
        self.start(p, i, self.grads[p].at[c], self.pair[p].at[i], at.cn)

    def add(self, count, pair):
        def one(s):
            mine, other = pair(s)
            mine[...] = mine[...] + other[...]

        loop(count, one)

    def add_pair(self, p, i, y):
        c = self.far_and_near(i)
        self.add(4, lambda s: (self.grad(p, c, y, s), parts_of(self.pair[p], p, i, y, s)))

    def far_sum(self, p):
        at = self.at
        arrived(self.pair[p].at[0], self.rs.at[p, 0], at.yn)
        self.add_pair(p, 0, 1 - at.y)
        self.start(p, 2, self.grad(p, at.cx, 1 - at.y, 0, 2), self.corner[p].at[0], at.xn)
        self.start(p, 3, self.grad(p, at.cx, 1 - at.y, 2, 2), self.corner[p].at[1], at.yn)
        self.add_pair(p, 0, at.y)
        self.start(p, 4, self.grad(p, at.cx, at.y, 0, 2), self.half(self.cross[p], p, 0, 0), at.xn)

    def near_sum(self, p):
        at = self.at
        arrived(self.pair[p].at[1], self.rs.at[p, 1], at.yn)
        self.add_pair(p, 1, 1 - at.y)
        self.start(p, 5, self.grad(p, at.c, 1 - at.y, 2, 2), self.half(self.cross[p], p, 1, 2), at.yn)
        self.add_pair(p, 1, at.y)

    def corner_a(self, p):
        at, corner = self.at, self.corner[p]
        arrived(corner.at[0], self.rs.at[p, 2], at.yn)
        self.add(2, lambda s: (self.grad(p, at.c, 1 - at.y, s), self.one(corner, p, 0, s)))
        self.start(p, 6, self.grad(p, at.c, 1 - at.y, 0, 2), self.half(self.cross[p], p, 1, 0), at.yn)

    def corner_b(self, p):
        at, corner = self.at, self.corner[p]
        arrived(corner.at[1], self.rs.at[p, 3], at.yn)
        self.add(2, lambda s: (self.grad(p, at.cx, at.y, s + 2), self.one(corner, p, 1, s)))
        self.start(p, 7, self.grad(p, at.cx, at.y, 2, 2), self.half(self.cross[p], p, 0, 2), at.xn)

    def cross_sum(self, p):
        at, cross = self.at, self.cross[p]
        for n, (i, first) in ((4, (0, 0)), (7, (0, 2)), (5, (1, 2)), (6, (1, 0))):
            arrived(self.half(cross, p, i, first), self.rs.at[p, n], at.yn)

        def one(s):
            mine = self.grad(p, at.c, at.y, s)
            mine[...] = mine[...] + self.one(cross, p, 0, s)[...] + self.one(cross, p, 1, s)[...]

        loop(4, one)
        line = self.along[p]

        def mine(s):
            return self.grad(p, at.c, at.y, s)

        if p in self.direct:
            for n in (1, 2, 3):
                s = at.other(n)
                self.start(p, 7 + n, mine(s), line.at[at.z], at.zth(s), arrival=8 + at.z)
            return
        end = jnp.logical_not(at.mid)
        near = jnp.where(at.mid, at.z - at.step, at.z + at.step)
        self.start(p, 8, mine(near), line.at[0], at.zth(near), arrival=8)
        for n in (2, 3):
            self.start(p, 7 + n, mine(at.other(n)), line.at[n], at.zth(near), arrival=8 + n, when=end)

    def line_sum(self, p):
        at, line = self.at, self.along[p]
        if p in self.direct:
            return

        @pl.when(at.mid)
        def _():
            for n in (2, 3):
                arrived(line.at[n], self.rs.at[p, 8 + n], at.yn)
                mine = self.grad(p, at.c, at.y, at.other(n - 1))
                mine[...] = mine[...] + line[n]

        for n in (2, 3):
            s = at.other(n - 1)
            self.start(p, 9 + n, self.grad(p, at.c, at.y, s), line.at[1], at.zth(s), arrival=9, when=at.mid)

    def along_sum(self, p):
        at, line = self.at, self.along[p]
        total = self.grad(p, at.c, at.y, at.z)[...].astype(F32)
        for n in (1, 2, 3) if p in self.direct else (0, 1):
            s = at.other(n) if p in self.direct else n
            arrived(line.at[s], self.rs.at[p, 8 + s], at.yn)
            total = total + line[s].astype(F32)
        self.owned[p][...] = total
        wide = total.shape[1]
        self.squares[:, 0:wide] = self.squares[:, 0:wide] + jnp.sum(total * total, axis=0, keepdims=True)


class Total:
    def __init__(self, at, sends, mine, line, plane, sems):
        self.at, self.sends, self.mine, self.line, self.plane = at, sends, mine, line, plane
        self.line_s, self.line_r, self.plane_s, self.plane_r, self.back_s, self.back_r = sems
        self.rows = line.shape[1]
        self.cut = mine.shape[0] != self.rows

    def part(self, ref, z):
        return ref.at[pl.ds(pl.multiple_of(z * self.rows, 8), self.rows)] if self.cut else ref

    def start(self):
        at = self.at
        self.line[at.z] = self.part(self.mine, at.z)[...]
        for k in (1, 2, 3):
            to = lax.rem(at.z + k, 4)
            self.sends.start(
                self.part(self.mine, to), self.line.at[at.z], self.line_s.at[k - 1], self.line_r.at[at.z], at.zth(to)
            )

    def spread(self):
        at = self.at
        for k in (1, 2, 3):
            s = lax.rem(at.z + k, 4)
            arrived(self.line.at[s], self.line_r.at[s], at.yn)
        me = at.y * 4 + at.c
        self.plane[me] = self.line[0] + self.line[1] + self.line[2] + self.line[3]
        for k in range(1, 8):
            to = lax.rem(me + k, 8)
            peer = (lax.div(to, 4), at.z, lax.rem(to, 4))
            self.sends.start(self.plane.at[me], self.plane.at[me], self.plane_s.at[k - 1], self.plane_r.at[me], peer)

    def collect(self):
        at = self.at
        me = at.y * 4 + at.c
        for k in range(1, 8):
            s = lax.rem(me + k, 8)
            arrived(self.plane.at[s], self.plane_r.at[s], at.yn)
        value = self.plane[0]
        for s in range(1, 8):
            value = value + self.plane[s]
        return value

    def share(self, whole):
        at = self.at
        mine = self.part(whole, at.z)
        mine[...] = self.collect()
        for k in (1, 2, 3):
            self.sends.start(mine, mine, self.back_s.at[k - 1], self.back_r.at[at.z], at.zth(lax.rem(at.z + k, 4)))

    def finish(self, whole):
        for k in (1, 2, 3):
            s = lax.rem(self.at.z + k, 4)
            arrived(self.part(whole, s), self.back_r.at[s], self.at.yn)


def fold(value):
    return value[0:8] + value[8:16] + value[16:24] + value[24:32]


def back_segment(c, slot, first, is_big, index, qkv, weights_big, weights_trio, mixed, grads):
    size = BIG_SLOTS if is_big else TRIO_SLOTS
    rows = pl.ds(first, size)
    q01 = qkv[c, rows, 0:128]
    k01 = qkv[c, rows, 128:256]
    v01 = qkv[c, rows, 256:384]
    kq2 = swap_halves(qkv[c, rows, 384:512])
    v2 = qkv[c, rows, 512:640]
    g01 = mixed[rows, pl.ds(pl.multiple_of(c * 256, 256), 128)]
    g2 = mixed[rows, pl.ds(pl.multiple_of(c * 256 + 128, 128), 128)]
    low = lane_low(size)
    none = jnp.zeros((size, 128), BF)
    dq, dk, dv = [], [], []
    for h, (g, gs, q, k, v) in enumerate((
        (g01, jnp.where(low, g01, none), q01, k01, v01),
        (g01, jnp.where(low, none, g01), q01, k01, v01),
        (g2, g2, kq2, kq2, v2),
    )):
        if is_big:
            weights = weights_big[slot, h, index]
        else:
            weights = weights_trio[slot, h, index]
        wide = weights.astype(F32)
        product = wide * mm_nt(gs, v)
        scores = (product - wide * jnp.sum(product, axis=1, keepdims=True)).astype(BF)
        dq.append(mm(scores, k))
        dk.append(mm_tn(scores, q))
        dv.append(mm_tn(weights, g))
    scale = HEAD_DIM**-0.5
    grads[c, rows, 0:128] = (jnp.where(low, dq[0], dq[1]) * scale).astype(BF)
    grads[c, rows, 128:256] = (jnp.where(low, dk[0], dk[1]) * scale).astype(BF)
    grads[c, rows, 256:384] = jnp.where(low, dv[0], dv[1]).astype(BF)
    grads[c, rows, 384:512] = (jnp.where(low, dq[2], dk[2]) * scale).astype(BF)
    grads[c, rows, 512:640] = dv[2].astype(BF)


def backward_kernel(
    wq_h, wo_h, w1_h, w2_h, x_h, mid_h, a1t_h, a2t_h, mixt_h, qkv_h, pbig_h, ptrio_h, act_h, slope_h, cot_h, cott_h, out_h,
    gains_in,
    own_q, own_o, own_1, own_2, total, square_total, land_out, land_in,
    ring, wo, gq, go, g1, g2, pq, po, p1, p2, nq, no, n1, n2, rq, ro, r1, r2, lq, lo, l1, l2,
    act, slope, cot, cott, a2t, a1t, mixt, mid, x, pbig, ptrio, gmix, grad, half, send, gains, small, summed, squares, sums_of, line, plane, square_tile, square_line, square_plane,
    ss, rs, hs, ring_s, p_s, ex_s, ex_r, in_s, in_r, *total_sems,
):
    at = Place()
    sends = Sends()
    reduce = Reduce(
        at, sends, (gq, go, g1, g2), (pq, po, p1, p2), (nq, no, n1, n2), (rq, ro, r1, r2), (lq, lo, l1, l2),
        (own_q, own_o, own_1, own_2), squares, BACKWARD_DIRECT, (ss, rs),
    )
    loads = {}
    waited = []

    def load(name, src, dst):
        copy = pltpu.make_async_copy(src, dst, hs.at[len(loads) + len(waited)])
        copy.start()
        loads[name] = copy

    groups = (2 * (1 - at.x) + 1 - at.core, at.cx, at.cs, at.c)
    uses = [(ref, c) for ref in (w2_h, w1_h, wq_h) for c in groups]
    ring_copies = {}

    def ring_start(u):
        if u < len(uses):
            src, c = uses[u]
            wide = src.shape[2]
            copy = pltpu.make_async_copy(src.at[c], ring.at[u % 3, :, pl.ds(0, wide)], ring_s.at[u])
            copy.start()
            ring_copies[u] = copy

    def loaded(*names):
        for name in names:
            if name in loads:
                loads.pop(name).wait()
                waited.append(name)

    sums = Total(at, sends, small, line, plane, total_sems[:6])
    square_sum = Total(at, sends, square_tile, square_line, square_plane, total_sems[6:])
    keep_out = pltpu.make_async_copy(out_h.at[at.z], land_out.at[at.z], ex_s.at[3])
    keep_in = pltpu.make_async_copy(send.at[at.z], land_in.at[at.z], in_s.at[3])

    def start():
        load("cott", cott_h, cott)
        for i in range(4):
            load(f"act{i}", act_h.at[groups[i]], act.at[groups[i]])
        for u in range(3):
            ring_start(u)
        load("cot", cot_h, cot)
        for i in range(4):
            load(f"slope{i}", slope_h.at[groups[i]], slope.at[groups[i]])
        load("a2t", a2t_h, a2t)
        load("mid", mid_h, mid)
        load("mixt", mixt_h, mixt)
        load("wo", wo_h, wo)
        load("a1t", a1t_h, a1t)
        load("x", x_h, x)
        at_enter(at)
        squares[...] = jnp.zeros((1, D), F32)
        for n in (0, 1):
            gains[n : n + 1, :] = jnp.concatenate([gains_in[6 * n + i : 6 * n + i + 1, :] for i in range(6)], axis=1)

    def send_out():
        keep_out.start()
        exchange_start(at, sends, out_h, land_out, ex_s, ex_r)

    def grad_fc2(i):
        c = groups[i]
        loaded("cott", f"act{i}")

        def tile(n):
            lanes = pl.ds(pl.multiple_of(n * 256, 256), 256)
            g2[c, :, lanes] = mm(cott[...], act[c, :, lanes]).astype(BF)

        loop(3, tile)

    def grad_hidden(i):
        c = groups[i]
        loaded("cot", f"slope{i}")
        ring_copies[i].wait()

        def tile(n):
            lanes = pl.ds(pl.multiple_of(n * 256, 256), 256)
            slope[c, :, lanes] = (mm(cot[...], ring[i % 3, :, lanes]) * slope[c, :, lanes].astype(F32)).astype(BF)

        loop(3, tile)
        ring_start(i + 3)

    def rows_to_shards(dst, c, lanes, tile):
        for z in range(4):
            for y in range(2):
                first = (z * 2 + y) * 96
                dst[c, y, z, :, lanes] = tile[first : first + 96].astype(BF)

    def grad_fc1(i):
        c = groups[i]
        loaded("a2t")

        def tile(n):
            lanes = pl.ds(pl.multiple_of(n * 256, 256), 256)
            value = mm(a2t[...], slope[c, :, lanes])
            rows_to_shards(g1, c, lanes, value)
            sums_of[c, :, lanes] = value[768:769]

        loop(3, tile)

    def back_through(first_use, left, wide, i):
        u = first_use + i
        ring_copies[u].wait()

        def tile(n):
            lanes = pl.ds(pl.multiple_of(n * 256, 256), 256)
            part = mm_nt(left[groups[i], :, 0:wide], ring[u % 3, lanes, 0:wide])
            if i == 0:
                grad[:, lanes] = part
            else:
                grad[:, lanes] = grad[:, lanes] + part

        loop(3, tile)
        ring_start(u + 3)

    def put_row(first, value):
        for i in range(6):
            small[first + i : first + i + 1, :] = value[:, i * 128 : i * 128 + 128]

    def norm_two():
        loaded("mid")
        parts = [jnp.zeros((8, D), F32)] * 4

        def one(i, rows):
            normed, inverse = row_stats(mid[rows, :])
            upper = grad[rows, :]
            weighted = upper * gains[1:2, :]
            first = jnp.sum(weighted, axis=1, keepdims=True) * (1.0 / D)
            second = jnp.sum(weighted * normed, axis=1, keepdims=True) * (1.0 / D)
            straight = cot[rows, :].astype(F32)
            value = straight + inverse * (weighted - first - normed * second)
            mid[rows, :] = value
            branch = value.astype(BF)
            for r in range(4):
                half[r, rows, :] = branch[:, r * 192 : r * 192 + 192]
            for n, v in enumerate((upper * normed, upper, branch.astype(F32), straight)):
                parts[n] = parts[n] + fold(v)

        chunks(one)
        for first, value in zip((6, 18, 36, 42), parts):
            put_row(first, jnp.sum(value, axis=0, keepdims=True))

    def grad_out():
        loaded("mixt")

        def one(z):
            value = mm(mixt[...], half[z]).astype(BF)
            for c in range(4):
                for y in range(2):
                    go[c, y, z] = value[c * 256 + y * 96 : c * 256 + y * 96 + 96]

        loop(4, one)

    def grad_mixed():
        load("qkv", qkv_h, slope.at[:, :, pl.ds(0, QW)])
        loaded("wo")

        def one(c):
            rows = pl.ds(pl.multiple_of(c * 256, 256), 256)
            value = mm_nt(half[0], wo[0, rows, :])
            for z in (1, 2, 3):
                value = value + mm_nt(half[z], wo[z, rows, :])
            gmix[:, rows] = value.astype(BF)

        loop(4, one)
        for copy in fetch(0):
            copy.start()
        loaded("qkv")

    def fetch(i):
        c, slot = groups[i], i % 2
        return (
            pltpu.make_async_copy(pbig_h.at[c], pbig.at[slot], p_s.at[slot, 0]),
            pltpu.make_async_copy(ptrio_h.at[c], ptrio.at[slot], p_s.at[slot, 1]),
        )

    def attend_back(i):
        for copy in fetch(i):
            copy.wait()
        if i < 3:
            for copy in fetch(i + 1):
                copy.start()
        c = groups[i]
        act[c, SLOTS - 16 : SLOTS, 0:QW] = jnp.zeros((16, QW), BF)
        segments(
            at, lambda first, is_big, n: back_segment(c, i % 2, first, is_big, n, slope, pbig, ptrio, gmix, act)
        )

    def grad_q(i):
        c = groups[i]
        loaded("a1t")

        def tile(lanes):
            value = mm(a1t[...], act[c, :, lanes])
            rows_to_shards(gq, c, lanes, value)
            sums_of[4 + c, :, lanes] = value[768:769]

        loop(2, lambda n: tile(pl.ds(pl.multiple_of(n * 256, 256), 256)))
        tile(pl.ds(512, 128))

    def norm_one():
        loaded("x")
        parts = [jnp.zeros((8, D), F32)] * 2

        def one(i, rows):
            normed, inverse = row_stats(x[rows, :].astype(F32))
            upper = grad[rows, :]
            weighted = upper * gains[0:1, :]
            first = jnp.sum(weighted, axis=1, keepdims=True) * (1.0 / D)
            second = jnp.sum(weighted * normed, axis=1, keepdims=True) * (1.0 / D)
            value = (mid[rows, :] + inverse * (weighted - first - normed * second)).astype(BF)
            for r in range(4):
                put_block(send, r, i, value[:, r * 192 : r * 192 + 192])
            for n, v in enumerate((upper * normed, upper)):
                parts[n] = parts[n] + fold(v)

        chunks(one)
        for first, value in zip((0, 12), parts):
            put_row(first, jnp.sum(value, axis=0, keepdims=True))

    def send_in():
        exchange_start(at, sends, send, land_in, in_s, in_r)
        keep_in.start()

    def start_total():
        for c in range(4):
            put_row(48 + 6 * c, sums_of[c])
        packed = [sums_of[4 + c] for c in range(4)]
        for first, lanes in ((24, (0, 384)), (30, (256, 512))):
            parts = []
            for value in packed:
                parts += [value[:, lanes[0] : lanes[0] + 128], value[:, lanes[1] : lanes[1] + HALF]]
            put_row(first, jnp.concatenate(parts, axis=1))
        small[72:96, :] = jnp.zeros((24, 128), F32)
        sums.start()

    def finish_total():
        sums.finish(summed)
        total[...] = summed[...]

    def start_squares():
        value = squares[:, 0:128]
        for i in range(1, 6):
            value = value + squares[:, i * 128 : i * 128 + 128]
        square_tile[...] = jnp.zeros((8, 128), F32)
        square_tile[0:1, :] = value
        square_sum.start()

    def finish_squares():
        square_total[...] = square_sum.collect()

    def wait_exchanges():
        exchange_wait(at, land_out, ex_r)
        exchange_wait(at, land_in, in_r)
        keep_out.wait()
        keep_in.wait()

    steps = {
        "start": start, "exO": send_out, "norm2": norm_two, "gWO": grad_out, "gm": grad_mixed, "norm1": norm_one,
        "exI": send_in, "tstart": start_total, "tspread": sums.spread, "tshare": lambda: sums.share(summed), "tfin": finish_total,
        "sstart": start_squares, "sspread": square_sum.spread, "sfin": finish_squares, "exw": wait_exchanges,
    }
    many = {
        "gW2": grad_fc2, "gh": grad_hidden, "gW1": grad_fc1, "gt": functools.partial(back_through, 4, slope, 768),
        "att": attend_back, "gWQ": grad_q, "go": functools.partial(back_through, 8, act, QW),
    }
    for name, step in many.items():
        for i in range(4):
            steps[f"{name}{i}"] = functools.partial(step, i)
    stages = {
        "sumF": reduce.far_sum, "sumN": reduce.near_sum, "cornA": reduce.corner_a, "cornB": reduce.corner_b,
        "cross": reduce.cross_sum, "line": reduce.line_sum, "along": reduce.along_sum,
    }
    for name, p in (("WQ", WQ), ("WO", WO), ("W1", W1), ("W2", W2)):
        steps[f"sendF {name}"] = functools.partial(reduce.pair_send, p, 0)
        steps[f"sendN {name}"] = functools.partial(reduce.pair_send, p, 1)
        for stage, step in stages.items():
            steps[f"{stage} {name}"] = functools.partial(step, p)
    for name in BACKWARD_ORDER:
        steps[name]()
    sends.drain()


def at_enter(at):
    barrier = pltpu.get_barrier_semaphore()
    me = at.y * 4 + at.c
    peers = [at.zth(lax.rem(at.z + k, 4)) for k in (1, 2, 3)]
    for k in range(1, 8):
        to = lax.rem(me + k, 8)
        peers.append((lax.div(to, 4), at.z, lax.rem(to, 4)))
    for peer in peers:
        pl.semaphore_signal(barrier, inc=1, device_id=peer, device_id_type=MESH)
    pl.semaphore_wait(barrier, len(peers))


SHARDS = ((96, QW), (96, 192), (96, 768), (192, 384))


def run_backward(*operands):
    sem = pltpu.SemaphoreType.DMA
    vmem = pltpu.VMEM
    shape = jax.ShapeDtypeStruct
    stages = [(4, 2, 4), (2, 2, 4), (2, 2), (2, 4), (4,)]
    matrices = [(4, 768, 768), (2, 768, 768), (2, 384, 384), (2, 768, 384), (4, 192, 384)]
    return pl.pallas_call(
        backward_kernel,
        out_shape=[shape(s, F32) for s in SHARDS] + [shape((96, 128), F32), shape((8, 128), F32)] + [shape((4, BLOCK, 128), BF)] * 2,
        in_specs=[pl.BlockSpec(memory_space=pl.ANY)] * (len(operands) - 1) + [pl.BlockSpec(memory_space=vmem)],
        out_specs=[pl.BlockSpec(memory_space=vmem)] * 6 + [pl.BlockSpec(memory_space=pl.ANY)] * 2,
        scratch_shapes=[vmem((3, 768, 768), BF), vmem((4, 1024, 192), BF)]
        + [
            vmem(whole if s == SHARDS[W2] else lead + s, BF) for lead, whole in zip(stages, matrices) for s in SHARDS
        ]
        + [
            vmem((4, SLOTS, 768), BF), vmem((4, SLOTS, 768), BF), vmem((SLOTS, D), BF), vmem((D, SLOTS), BF),
            vmem((784, SLOTS), BF), vmem((784, SLOTS), BF), vmem((1024, SLOTS), BF), vmem((SLOTS, D), F32),
            vmem((SLOTS, D), BF), vmem((2, 3, 2, BIG_SLOTS, BIG_SLOTS), BF), vmem((2, 3, 3, TRIO_SLOTS, TRIO_SLOTS), BF),
            vmem((SLOTS, 1024), BF), vmem((SLOTS, D), F32), vmem((4, SLOTS, 192), BF), vmem((4, BLOCK, 128), BF),
            vmem((2, D), F32), vmem((96, 128), F32), vmem((96, 128), F32), vmem((1, D), F32), vmem((8, 1, D), F32),
            vmem((4, 24, 128), F32), vmem((8, 24, 128), F32), vmem((8, 128), F32), vmem((4, 8, 128), F32), vmem((8, 8, 128), F32),
            sem((4, 13)), sem((4, 13)), sem((18,)), sem((12,)), sem((2, 2)), sem((4,)), sem((4,)), sem((4,)), sem((4,)),
        ]
        + [sem((n,)) for n in (3, 4, 7, 8, 3, 4)] * 2,
        compiler_params=pltpu.CompilerParams(collective_id=1, has_side_effects=True, vmem_limit_bytes=VMEM_LIMIT),
    )(*operands)


BACKWARD_ORDER = (
    "start", "gW20", "exO", "sendF W2", "gh0", "gW10", "gW22", "gh1", "gW21", "sumF W2", "gh2", "sendN W2", "gW12",
    "sendF W1", "gh3", "gt0", "gW23", "sumN W2", "gt1", "gW13", "gt2", "gt3", "gW11", "cornA W2", "sendN W1",
    "cornB W2", "norm2", "gm", "att0", "go0", "sumF W1", "cross W2", "line W2", "sumN W1", "att1", "att2", "go1",
    "go2", "cornA W1", "att3", "cornB W1", "go3", "norm1", "exI", "gWQ1", "gWQ0", "cross W1", "sendF WQ", "along W2",
    "gWQ2", "sumF WQ", "gWQ3", "gWO", "sendN WQ", "sumN WQ", "cornB WQ", "sendF WO", "cornA WQ", "sendN WO",
    "sumN WO", "sumF WO", "line W1", "cross WQ", "tstart", "line WQ", "cornA WO", "cornB WO", "along W1", "cross WO",
    "line WO", "tspread", "along WQ", "along WO", "sstart", "tshare", "sspread", "tfin", "sfin", "exw",
)
BACKWARD_DIRECT = ()


RATES = (D**-0.5, (D // 24) ** -0.5, D**-0.5, FF**-0.5, 0.3, 0.3)
ROWS = 208


def update_kernel(
    own_q, own_o, own_1, own_2, total, square_total, land_out, land_in, where,
    wq, wo, w1, w2, wg, wb, mq, mo, m1, m2, mg, mb, vq, vo, v1, v2, vg, vb,
    out, grad_in, norm,
    nmq, nvq, nwq, hq, nmo, nvo, nwo, ho, nm1, nv1, nw1, h1, nm2, nv2, nw2, h2, nmg, nvg, nwg, hg, nmb, nvb, nwb, hb,
    blocks,
):
    gains = total[0:12, :]
    biases = total[12:72, :]
    squares = jnp.sum(jnp.sum(square_total[...], axis=0, keepdims=True), axis=1, keepdims=True)
    for part in (gains, biases):
        squares = squares + jnp.sum(jnp.sum(part * part, axis=0, keepdims=True), axis=1, keepdims=True)
    size = jnp.sqrt(squares)
    norm[...] = size
    factor = jnp.minimum(1.0, CLIP_NORM / size)

    def step(rate, grad, pick, refs):
        weight, first, second, new_first, new_second, new_weight, half = refs
        results = adam_step(weight[pick], grad, first[pick], second[pick], rate, factor)
        for ref, value in zip((new_first, new_second, new_weight, half), results):
            ref[pick] = value

    everything = (slice(None), slice(None))
    packed = own_q[...]
    for n in range(3):
        grad = jnp.concatenate([packed[:, 128 * n : 128 * n + 128], packed[:, 384 + HALF * n : 448 + HALF * n]], axis=1)
        step(RATES[0], grad, n, (wq, mq, vq, nmq, nvq, nwq, hq))
    step(RATES[1], own_o[...], everything, (wo, mo, vo, nmo, nvo, nwo, ho))
    step(RATES[2], own_1[...], everything, (w1, m1, v1, nm1, nv1, nw1, h1))
    step(RATES[3], own_2[...], everything, (w2, m2, v2, nm2, nv2, nw2, h2))
    step(RATES[4], gains, everything, (wg, mg, vg, nmg, nvg, nwg, hg))
    step(RATES[5], biases, everything, (wb, mb, vb, nmb, nvb, nwb, hb))

    pairs = out.shape[0] // 3
    for n, land in enumerate((land_out, land_in)):
        for r in range(4):
            for i in range(SLOTS // CHUNK):
                rows = slice(r * SLOTS + i * CHUNK, r * SLOTS + i * CHUNK + CHUNK)
                rest = land[r, SLOTS + i * 16 : SLOTS + i * 16 + 16, :]
                blocks[rows, n * 192 : n * 192 + 128] = land[r, i * CHUNK : i * CHUNK + CHUNK, :]
                blocks[rows, n * 192 + 128 : n * 192 + 192] = jnp.concatenate([rest[:, 0:HALF], rest[:, HALF:]], axis=0)
    for first in range(0, pairs, ROWS):
        count = min(ROWS, pairs - first)
        halves = []
        for half in (0, 1):
            token = half * TOK + first + lax.broadcasted_iota(jnp.int32, (ROWS, SLOTS), 0)
            one = jnp.concatenate([(token == where[r]).astype(F32).astype(BF) for r in range(4)], axis=1)
            halves.append(mm(one, blocks[...])[0:count])
        for ref, lanes in ((out, 0), (grad_in, 192)):
            even, odd = (value[:, lanes : lanes + 192] for value in halves)
            middle = jnp.concatenate([even[:, 128:192], odd[:, 0:HALF]], axis=1)
            for n, value in enumerate((even[:, 0:128], middle, odd[:, HALF:192])):
                ref[pl.ds(3 * first + n, count, stride=3), :] = value


def run_update(pairs, *operands):
    shape = jax.ShapeDtypeStruct
    shapes = [shape((pairs * 3, 128), F32)] * 2 + [shape((1, 1), F32)]
    for weight in operands[9:15]:
        shapes += [shape(weight.shape, F32)] * 3 + [shape(weight.shape, BF)]
    return pl.pallas_call(
        update_kernel,
        out_shape=shapes,
        in_specs=[pl.BlockSpec(memory_space=pltpu.VMEM)] * len(operands),
        out_specs=[pl.BlockSpec(memory_space=pltpu.VMEM)] * len(shapes),
        scratch_shapes=[pltpu.VMEM((4 * SLOTS, 384), BF)],
        compiler_params=pltpu.CompilerParams(vmem_limit_bytes=VMEM_LIMIT),
    )(*operands)


def prepare(layer_in, grad_out, crop_ids, w_qkv, w_out, w_fc1, w_fc2, norm_gains, all_biases):
    pairs = layer_in.shape[0]
    return (
        layer_in.reshape(pairs, 384), grad_out.reshape(pairs, 384), crop_ids.reshape(-1, IMAGE_LEN),
        w_qkv.transpose(1, 0, 2), w_out, w_fc1, w_fc2.T, norm_gains.reshape(12, 128), all_biases.reshape(60, 128),
    )


def local_fast(
    layer_in, grad_out, crop_ids, w_qkv, w_out, w_fc1, w_fc2, norm_gains, all_biases,
    first_qkv, second_qkv, first_out, second_out, first_fc1, second_fc1, first_fc2, second_fc2,
    first_gains, second_gains, first_biases, second_biases,
):
    pairs = layer_in.shape[0]
    operands = prepare(layer_in, grad_out, crop_ids, w_qkv, w_out, w_fc1, w_fc2, norm_gains, all_biases)
    *kept, where = run_forward(*operands)
    reduced = run_backward(*kept, operands[7])
    masters = operands[3:9]
    results = run_update(
        pairs, *reduced, where, *masters,
        first_qkv.transpose(1, 0, 2), first_out, first_fc1, first_fc2.T,
        first_gains.reshape(12, 128), first_biases.reshape(60, 128),
        second_qkv.transpose(1, 0, 2), second_out, second_fc1, second_fc2.T,
        second_gains.reshape(12, 128), second_biases.reshape(60, 128),
    )
    return (
        results[0].reshape(pairs, 1, 384), results[1].reshape(pairs, 1, 384), results[2].reshape(()),
        *[v.transpose(1, 0, 2) for v in results[3:7]], *results[7:15], *[v.T for v in results[15:19]],
        *[v.reshape(-1) for v in results[19:27]],
    )


def dot(a, b):
    return jnp.dot(a, b, preferred_element_type=F32)


def dot_nt(a, b):
    return lax.dot_general(a, b, (((1,), (1,)), ((), ())), preferred_element_type=F32)


def dot_tn(a, b):
    return lax.dot_general(a, b, (((0,), (0,)), ((), ())), preferred_element_type=F32)


def norm_stats(value):
    centre = jnp.mean(value, axis=1, keepdims=True)
    centred = value - centre
    spread = jnp.mean(centred * centred, axis=1, keepdims=True)
    inverse = lax.rsqrt(spread + NORM_EPS)
    return centred * inverse, inverse


def norm_back(grad, normed, inverse, gain):
    weighted = grad * gain
    first = jnp.mean(weighted, axis=1, keepdims=True)
    second = jnp.mean(weighted * normed, axis=1, keepdims=True)
    return inverse * (weighted - first - normed * second)


def layer(x, cot, crops, w_qkv, w_out, w_fc1, w_fc2, gains, biases):
    inputs = x.astype(F32)
    cotf = cot.astype(F32)
    normed_one, inverse_one = norm_stats(inputs)
    act_one = (normed_one * gains[:D] + biases[:D]).astype(BF)
    qkv_bias = jnp.concatenate([biases[2 * D : 3 * D], jnp.zeros((D,), F32), biases[3 * D : 4 * D]])
    qkv = (dot(act_one, w_qkv) + qkv_bias).astype(BF)
    heads = qkv.reshape(SLOTS, 3, HEADS, HEAD_DIM)
    q, k, v = heads[:, 0], heads[:, 1], heads[:, 2]
    scores = jnp.einsum("qhd,khd->hqk", q, k, preferred_element_type=F32) * HEAD_DIM ** (-0.5)
    scores = jnp.where((crops[:, None] == crops[None, :])[None], scores, MASKED)
    probs = jax.nn.softmax(scores, axis=2)
    half_probs = probs.astype(BF)
    mixed = jnp.einsum("hqk,khd->qhd", half_probs, v, preferred_element_type=F32)
    mixed = mixed.reshape(SLOTS, D).astype(BF)
    middle = inputs + dot(mixed, w_out) + biases[4 * D : 5 * D]
    normed_two, inverse_two = norm_stats(middle)
    act_two = (normed_two * gains[D:] + biases[D : 2 * D]).astype(BF)
    hidden = dot(act_two, w_fc1) + biases[6 * D :]
    active, gelu_pull = jax.vjp(lambda h: jax.nn.gelu(h, approximate=False), hidden)
    active = active.astype(BF)
    out = middle + dot(active, w_fc2) + biases[5 * D : 6 * D]

    g_fc2 = dot_tn(active, cot)
    grad_hidden = gelu_pull(dot_nt(cot, w_fc2))[0].astype(BF)
    g_fc1 = dot_tn(act_two, grad_hidden)
    grad_two = dot_nt(grad_hidden, w_fc1)
    grad_middle = cotf + norm_back(grad_two, normed_two, inverse_two, gains[D:])
    branch = grad_middle.astype(BF)
    g_out = dot_tn(mixed, branch)
    grad_mixed = dot_nt(branch, w_out).astype(BF).reshape(SLOTS, HEADS, HEAD_DIM)
    grad_probs = jnp.einsum("qhd,khd->hqk", grad_mixed, v, preferred_element_type=F32)
    grad_scores = (probs * (grad_probs - jnp.sum(probs * grad_probs, axis=2, keepdims=True))).astype(BF)
    scale = HEAD_DIM ** (-0.5)
    grad_q = jnp.einsum("hqk,khd->qhd", grad_scores, k, preferred_element_type=F32) * scale
    grad_k = jnp.einsum("hqk,qhd->khd", grad_scores, q, preferred_element_type=F32) * scale
    grad_v = jnp.einsum("hqk,qhd->khd", half_probs, grad_mixed, preferred_element_type=F32)
    grad_qkv = jnp.stack([grad_q, grad_k, grad_v], axis=1).astype(BF).reshape(SLOTS, 3 * D)
    g_qkv = dot_tn(act_one, grad_qkv)
    grad_one = dot_nt(grad_qkv, w_qkv)
    grad_in = grad_middle + norm_back(grad_one, normed_one, inverse_one, gains[:D])

    g_gains = jnp.concatenate([jnp.sum(grad_one * normed_one, axis=0), jnp.sum(grad_two * normed_two, axis=0)])
    qkv_sums = jnp.sum(grad_qkv.astype(F32), axis=0)
    g_biases = jnp.concatenate([
        jnp.sum(grad_one, axis=0),
        jnp.sum(grad_two, axis=0),
        qkv_sums[:D],
        qkv_sums[2 * D :],
        jnp.sum(branch.astype(F32), axis=0),
        jnp.sum(cotf, axis=0),
        jnp.sum(grad_hidden.astype(F32), axis=0),
    ])
    return out, grad_in, g_qkv, g_out, g_fc1, g_fc2, g_gains, g_biases


def adam_step(weight, grad, first, second, rate, factor):
    clipped = grad * factor
    new_first = BETA_ONE * first + (1.0 - BETA_ONE) * clipped
    new_second = BETA_TWO * second + (1.0 - BETA_TWO) * clipped * clipped
    unbiased_first = new_first / (1.0 - BETA_ONE**STEP)
    unbiased_second = new_second / (1.0 - BETA_TWO**STEP)
    new_weight = weight - rate * (
        unbiased_first / (jnp.sqrt(unbiased_second) + ADAM_EPS) + DECAY * weight
    )
    return (new_first, new_second, new_weight, new_weight.astype(BF))


def gather(value, axes):
    for name, dim in axes:
        value = lax.all_gather(value, name, axis=dim, tiled=True)
    return value


def scatter(value, axes):
    for name, dim in axes:
        value = lax.psum_scatter(value, name, scatter_dimension=dim, tiled=True)
    return value.astype(F32)


def local_plain(
    layer_in, grad_out, crop_ids, w_qkv, w_out, w_fc1, w_fc2, norm_gains, all_biases,
    first_qkv, second_qkv, first_out, second_out, first_fc1, second_fc1, first_fc2, second_fc2,
    first_gains, second_gains, first_biases, second_biases,
):
    row = lax.axis_index("row")
    n_row, n_col = lax.axis_size("row"), lax.axis_size("col")
    feat = D // n_row
    pairs = layer_in.shape[0]
    labels = lax.ppermute(
        crop_ids, ("row", "col"), [(r * n_col + c, c * n_row + r) for r in range(n_row) for c in range(n_col)]
    )
    sources = slot_sources(labels).reshape(-1)
    place = jnp.where(sources < 0, -1, (sources % 2) * pairs + sources // 2)
    pick = (place[:, None] == jnp.arange(2 * pairs, dtype=jnp.int32)[None, :]).astype(BF)

    def to_slots(value):
        halves = jnp.concatenate([value[:, 0, :feat], value[:, 0, feat:]], axis=0)
        sent = dot(pick, halves).astype(BF)
        got = lax.all_to_all(sent, "row", 0, 0, tiled=True)
        return got.reshape(n_row, SLOTS, feat).transpose(1, 0, 2).reshape(SLOTS, D)

    def to_tokens(value):
        sent = value.astype(BF).reshape(SLOTS, n_row, feat).transpose(1, 0, 2).reshape(n_row * SLOTS, feat)
        got = lax.all_to_all(sent, "row", 0, 0, tiled=True)
        halves = dot_tn(pick, got)
        return jnp.concatenate([halves[:pairs], halves[pairs:]], axis=1).reshape(pairs, 1, 2 * feat)

    full_qkv = gather(w_qkv.astype(BF), (("dp", 0), ("row", 0), ("col", 2))).reshape(D, 3 * D)
    full_out = gather(w_out.astype(BF), (("dp", 0), ("col", 0), ("row", 1)))
    full_fc1 = gather(w_fc1.astype(BF), (("dp", 0), ("row", 0), ("col", 1)))
    full_fc2 = gather(w_fc2.astype(BF), (("dp", 0), ("col", 0), ("row", 1)))
    crops = jnp.where(row < 2, slot_crops(0), slot_crops(1))
    out, grad_in, g_qkv, g_out, g_fc1, g_fc2, g_gains, g_biases = layer(
        to_slots(layer_in), to_slots(grad_out), crops, full_qkv, full_out, full_fc1, full_fc2, norm_gains, all_biases
    )
    owned_qkv = scatter(g_qkv.astype(BF).reshape(D, 3, D), (("col", 2), ("row", 0), ("dp", 0)))
    owned_out = scatter(g_out.astype(BF), (("row", 1), ("col", 0), ("dp", 0)))
    owned_fc1 = scatter(g_fc1.astype(BF), (("col", 1), ("row", 0), ("dp", 0)))
    owned_fc2 = scatter(g_fc2.astype(BF), (("row", 1), ("col", 0), ("dp", 0)))
    local_squares = (
        jnp.sum(owned_qkv * owned_qkv)
        + jnp.sum(owned_out * owned_out)
        + jnp.sum(owned_fc1 * owned_fc1)
        + jnp.sum(owned_fc2 * owned_fc2)
    )
    grad_gains, grad_biases, weight_squares = lax.psum((g_gains, g_biases, local_squares), ("dp", "row", "col"))
    grad_norm = jnp.sqrt(weight_squares + jnp.sum(grad_gains * grad_gains) + jnp.sum(grad_biases * grad_biases))
    factor = jnp.minimum(1.0, CLIP_NORM / grad_norm)
    upd_qkv = adam_step(w_qkv, owned_qkv, first_qkv, second_qkv, D ** (-0.5), factor)
    upd_out = adam_step(w_out, owned_out, first_out, second_out, (D // 24) ** (-0.5), factor)
    upd_fc1 = adam_step(w_fc1, owned_fc1, first_fc1, second_fc1, D ** (-0.5), factor)
    upd_fc2 = adam_step(w_fc2, owned_fc2, first_fc2, second_fc2, FF ** (-0.5), factor)
    upd_gains = adam_step(norm_gains, grad_gains, first_gains, second_gains, 0.3, factor)
    upd_biases = adam_step(all_biases, grad_biases, first_biases, second_biases, 0.3, factor)
    return (
        to_tokens(out), to_tokens(grad_in), grad_norm,
        *upd_qkv, *upd_out, *upd_fc1, *upd_fc2, *upd_gains, *upd_biases,
    )


def solution(mesh):
    tokens = P(("dp", "col"), "row", None)
    qkv = P(("row", "dp"), None, "col")
    out = P(("col", "dp"), "row")
    fc1 = P(("row", "dp"), "col")
    whole = P()
    return jax.shard_map(
        local_fast if mesh.shape["dp"] == 2 else local_plain,
        mesh=mesh,
        in_specs=(
            tokens, tokens, P(("dp", "row")), qkv, out, fc1, out, whole, whole,
            qkv, qkv, out, out, fc1, fc1, out, out, whole, whole, whole, whole,
        ),
        out_specs=(tokens, tokens, whole) + (qkv,) * 4 + (out,) * 4 + (fc1,) * 4 + (out,) * 4 + (whole,) * 8,
        check_vma=False,
    )
```

```python
import functools

import jax
import jax.numpy as jnp
from jax import lax
from jax.experimental import pallas as pl
from jax.experimental.pallas import tpu as pltpu
from jax.sharding import PartitionSpec as P

HEADS = 12
HEAD_DIM = 64
FF = 3072
D = 768
BIG_CROP = 197
SMALL_CROP = 37
IMAGE_LEN = 690
CROPS = 10
STEP = 5

NORM_EPS = 1e-06
CLIP_NORM = 1.0
BETA_ONE = 0.5
BETA_TWO = 0.5
ADAM_EPS = 1e-08
DECAY = 0.05
MASKED = -1e30

SLOTS = 544
BIG_SLOTS = 208
TRIO_SLOTS = 112
TRIO = 3 * SMALL_CROP
BF = jnp.bfloat16
F32 = jnp.float32


def crop_starts(labels):
    images = labels.shape[0] // IMAGE_LEN
    places = labels.reshape(images, IMAGE_LEN) % CROPS
    order = jnp.arange(CROPS, dtype=jnp.int32)
    sizes = jnp.sum((places[:, :, None] == order).astype(jnp.int32), axis=1)
    starts = jnp.sum((places[:, :, None] < order).astype(jnp.int32), axis=1)
    starts = starts + IMAGE_LEN * jnp.arange(images, dtype=jnp.int32)[:, None]
    big = (sizes == BIG_CROP).astype(jnp.int32)
    earlier = (order[:, None] < order[None, :]).astype(jnp.int32)
    big_rank = jnp.sum(big[:, :, None] * earlier, axis=1)
    small_rank = jnp.sum((1 - big)[:, :, None] * earlier, axis=1)

    def ranked(flag, rank, count):
        hit = flag[:, :, None] * (rank[:, :, None] == jnp.arange(count, dtype=jnp.int32)).astype(jnp.int32)
        return jnp.sum(hit * starts[:, :, None], axis=1).reshape(-1)

    return ranked(big, big_rank, 2), ranked(1 - big, small_rank, CROPS - 2)


def slot_segments(kind):
    if kind == 0:
        bigs, trios = 2, 1
    else:
        bigs, trios = 1, 3
    parts = []
    at = 0
    for b in range(bigs):
        parts.append((at, BIG_CROP, True, b))
        at += BIG_SLOTS
    for s in range(3 * trios):
        parts.append((at + s // 3 * TRIO_SLOTS + s % 3 * SMALL_CROP, SMALL_CROP, False, s))
    return parts


def slot_sources(labels):
    big, small = crop_starts(labels)
    rows = []
    for row in range(4):
        kind = row // 2
        at_big = (0, 2, 4, 5)[row]
        at_small = (0, 3, 6, 15)[row]
        out = []
        filled = 0
        for first, length, is_big, index in slot_segments(kind):
            if first > filled:
                out.append(jnp.full((first - filled,), -1, jnp.int32))
            start = big[at_big + index] if is_big else small[at_small + index]
            out.append(start + jnp.arange(length, dtype=jnp.int32))
            filled = first + length
        if filled < SLOTS:
            out.append(jnp.full((SLOTS - filled,), -1, jnp.int32))
        rows.append(jnp.concatenate(out))
    return jnp.stack(rows)


def slot_crops(kind):
    slot = jnp.arange(SLOTS, dtype=jnp.int32)
    crop = jnp.full((SLOTS,), -1, jnp.int32)
    for number, (first, length, _, _) in enumerate(slot_segments(kind)):
        crop = jnp.where((slot >= first) & (slot < first + length), number, crop)
    return crop


MESH = pl.DeviceIdType.MESH
HALF = 64
QW = 640
TOK = 1040
CHUNK = 32
BLOCK = SLOTS + SLOTS // 2
WQ, WO, W1, W2 = 0, 1, 2, 3
VMEM_LIMIT = 60 * 2**20


def mm(a, b):
    return lax.dot_general(a, b, (((1,), (0,)), ((), ())), preferred_element_type=F32)


def mm_nt(a, b):
    return lax.dot_general(a, b, (((1,), (1,)), ((), ())), preferred_element_type=F32)


def mm_tn(a, b):
    return lax.dot_general(a, b, (((0,), (0,)), ((), ())), preferred_element_type=F32)


class Place:
    def __init__(self):
        self.y = lax.axis_index("dp")
        self.z = lax.axis_index("row")
        self.c = lax.axis_index("col")
        self.core = lax.rem(self.c, 2)
        self.x = lax.div(self.c, 2)
        self.cx = lax.rem(self.c + 2, 4)
        self.cs = self.c + 1 - 2 * self.core
        self.xn = (self.y, self.z, self.cx)
        self.yn = (1 - self.y, self.z, self.c)
        self.cn = (self.y, self.z, self.cs)
        self.low = self.z < 2
        self.mid = jnp.logical_or(self.z == 1, self.z == 2)
        self.step = jnp.where(self.low, 1, -1)

    def zth(self, z):
        return (self.y, z, self.c)

    def other(self, j):
        return lax.rem(self.z + self.step * j + 4, 4)

    def enter(self):
        barrier = pltpu.get_barrier_semaphore()
        peers = [self.zth(lax.rem(self.z + k, 4)) for k in (1, 2, 3)] + [self.xn, self.yn, self.cn]
        for peer in peers:
            pl.semaphore_signal(barrier, inc=1, device_id=peer, device_id_type=MESH)
        pl.semaphore_wait(barrier, len(peers))


def shard_of(refs, p, c, s, y):
    ref = refs[p]
    if p == WO:
        return ref.at[s, c, pl.ds(pl.multiple_of(y * 96, 32), 96), :]
    if p == W2:
        return ref.at[c, s, :, pl.ds(pl.multiple_of(y * 384, 128), 384)]
    return ref.at[c, s, y]


def group_of(refs, p, c, y):
    ref = refs[p]
    if p == WO:
        return ref.at[:, c, pl.ds(pl.multiple_of(y * 96, 32), 96), :]
    if p == W2:
        return ref.at[c, :, :, pl.ds(pl.multiple_of(y * 384, 128), 384)]
    return ref.at[c, :, y]


class Sends:
    def __init__(self):
        self.left = []

    def start(self, src, dst, send_sem, recv_sem, peer, when=None):
        copy = pltpu.make_async_remote_copy(
            src_ref=src, dst_ref=dst, send_sem=send_sem, recv_sem=recv_sem, device_id=peer, device_id_type=MESH
        )
        if when is None:
            copy.start()
        else:
            pl.when(when)(copy.start)
        self.left.append((copy, when))

    def drain(self):
        for copy, when in self.left:
            if when is None:
                copy.wait_send()
            else:
                pl.when(when)(copy.wait_send)
        self.left = []


def arrived(ref, sem, me):
    pltpu.make_async_remote_copy(
        src_ref=ref, dst_ref=ref, send_sem=sem, recv_sem=sem, device_id=me, device_id_type=MESH
    ).wait_recv()


class Gather:
    def __init__(self, at, refs, sends, direct, zs, zr, xs, xr, ys, yr, ds, dr, cs, cr):
        self.at, self.refs, self.sends, self.direct = at, refs, sends, direct
        self.zs, self.zr, self.xs, self.xr = zs, zr, xs, xr
        self.ys, self.yr, self.ds, self.dr, self.cs, self.cr = ys, yr, ds, dr, cs, cr

    def across(self, p, s):
        at = self.at
        own = shard_of(self.refs, p, at.c, s, at.y)
        self.sends.start(own, own, self.xs.at[p, s], self.xr.at[p, s], at.xn)
        self.sends.start(own, own, self.ys.at[p, s], self.yr.at[p, s], at.yn)

    def own_across(self, p):
        self.across(p, self.at.z)

    def own_along(self, p):
        at = self.at
        own = shard_of(self.refs, p, at.c, at.z, at.y)
        if p in self.direct:
            for j in (1, 2, 3):
                self.sends.start(own, own, self.zs.at[p, j - 1], self.zr.at[p, at.z], at.zth(at.other(j)))
            return
        second = jnp.where(at.mid, at.z - at.step, at.z + 2 * at.step)
        self.sends.start(own, own, self.zs.at[p, 0], self.zr.at[p, at.z], at.zth(at.z + at.step))
        self.sends.start(own, own, self.zs.at[p, 1], self.zr.at[p, at.z], at.zth(second))

    def to_core(self, p, g, c, y):
        ref = group_of(self.refs, p, c, y)
        self.sends.start(ref, ref, self.cs.at[p, g], self.cr.at[p, g], self.at.cn)

    def along(self, p, j):
        at = self.at
        s = at.other(j)
        ref = shard_of(self.refs, p, at.c, s, at.y)
        arrived(ref, self.zr.at[p, s], at.yn)
        if j < 3 and p not in self.direct:
            self.sends.start(ref, ref, self.zs.at[p, 1 + j], self.zr.at[p, s], at.zth(at.z - at.step), when=at.mid)
        self.across(p, s)
        if j == 3:
            self.to_core(p, 0, at.c, at.y)

    def cross(self, p, j):
        at = self.at
        s = at.other(j)
        from_x = shard_of(self.refs, p, at.cx, s, at.y)
        from_y = shard_of(self.refs, p, at.c, s, 1 - at.y)
        arrived(from_x, self.xr.at[p, s], at.yn)
        arrived(from_y, self.yr.at[p, s], at.yn)
        if j < 2:
            self.sends.start(from_x, from_x, self.ds.at[p, j], self.dr.at[p, s], at.yn)
        else:
            self.sends.start(from_y, from_y, self.ds.at[p, j], self.dr.at[p, s], at.xn)
        if j == 3:
            self.to_core(p, 1, at.cx, at.y)
            self.to_core(p, 2, at.c, 1 - at.y)

    def corner(self, p):
        at = self.at
        for j in (0, 1, 2, 3):
            s = at.other(j)
            arrived(shard_of(self.refs, p, at.cx, s, 1 - at.y), self.dr.at[p, s], at.yn)
        self.to_core(p, 3, at.cx, 1 - at.y)

    def ready(self, p, half):
        at = self.at
        c = at.cs if half == 0 else at.cs + 2 - 4 * at.x
        arrived(group_of(self.refs, p, c, at.y), self.cr.at[p, half], at.yn)
        arrived(group_of(self.refs, p, c, 1 - at.y), self.cr.at[p, 2 + half], at.yn)


def exchange_start(at, sends, blocks, landing, send_sems, recv_sems):
    for k in (1, 2, 3):
        to = lax.rem(at.z + k, 4)
        sends.start(blocks.at[to], landing.at[at.z], send_sems.at[k - 1], recv_sems.at[at.z], at.zth(to))


def exchange_wait(at, landing, recv_sems):
    for k in (1, 2, 3):
        s = lax.rem(at.z + k, 4)
        arrived(landing.at[s], recv_sems.at[s], at.yn)


def row_stats(value):
    centre = jnp.sum(value, axis=1, keepdims=True) * (1.0 / D)
    centred = value - centre
    spread = jnp.sum(centred * centred, axis=1, keepdims=True) * (1.0 / D)
    inverse = lax.rsqrt(spread + NORM_EPS)
    return centred * inverse, inverse


def chunks(body):
    for i in range(SLOTS // CHUNK):
        body(i, slice(i * CHUNK, i * CHUNK + CHUNK))


def put_block(ref, r, i, value):
    ref[r, i * CHUNK : i * CHUNK + CHUNK, :] = value[:, 0:128]
    first = SLOTS + i * (CHUNK // 2)
    ref[r, first : first + CHUNK // 2, :] = jnp.concatenate([value[0:16, 128:192], value[16:32, 128:192]], axis=1)


def get_blocks(ref, i):
    parts = []
    first = SLOTS + i * (CHUNK // 2)
    for r in range(4):
        parts.append(ref[r, i * CHUNK : i * CHUNK + CHUNK, :])
        rest = ref[r, first : first + CHUNK // 2, :]
        parts.append(jnp.concatenate([rest[:, 0:HALF], rest[:, HALF:]], axis=0))
    return jnp.concatenate(parts, axis=1)


def loop(count, body):
    def step(i, carry):
        body(i)
        return carry

    lax.fori_loop(0, count, step, 0)


def lane_low(rows):
    return lax.broadcasted_iota(jnp.int32, (rows, 2 * HALF), 1) < HALF


def swap_halves(value):
    return jnp.concatenate([value[:, HALF:], value[:, :HALF]], axis=1)


def segments(at, body):
    for bigs in (2, 1):

        @pl.when(at.low if bigs == 2 else jnp.logical_not(at.low))
        def _():
            for i in range(bigs):
                body(i * BIG_SLOTS, True, i)
            for i in range(1 if bigs == 2 else 3):
                body(bigs * BIG_SLOTS + i * TRIO_SLOTS, False, i)


def key_mask(size, is_big):
    key = lax.broadcasted_iota(jnp.int32, (size, size), 1)
    if is_big:
        return key < BIG_CROP
    query = lax.broadcasted_iota(jnp.int32, (size, size), 0)

    def crop(v):
        return (v >= SMALL_CROP).astype(jnp.int32) + (v >= 2 * SMALL_CROP).astype(jnp.int32) + (v >= TRIO).astype(jnp.int32)

    return jnp.logical_and(crop(query) == crop(key), key < TRIO)


def attend_segment(c, first, is_big, index, qkv, mixed, pbig, ptrio):
    size = BIG_SLOTS if is_big else TRIO_SLOTS
    rows = pl.ds(first, size)
    q01 = qkv[c, rows, 0:128]
    k01 = qkv[c, rows, 128:256]
    v01 = qkv[c, rows, 256:384]
    qk2 = qkv[c, rows, 384:512]
    v2 = qkv[c, rows, 512:640]
    low = lane_low(size)
    none = jnp.zeros((size, 128), BF)
    mask = key_mask(size, is_big)
    outs = []
    for h, (q, k, v) in enumerate((
        (jnp.where(low, q01, none), k01, v01),
        (jnp.where(low, none, q01), k01, v01),
        (jnp.where(low, qk2, none), swap_halves(qk2), v2),
    )):
        scores = jnp.where(mask, mm_nt(q, k) * HEAD_DIM**-0.5, MASKED)
        weights = jnp.exp(scores - jnp.max(scores, axis=1, keepdims=True))
        total = jnp.sum(weights, axis=1, keepdims=True)
        weights = (weights * (1.0 / total)).astype(BF)
        if is_big:
            pbig[c, h, index] = weights
        else:
            ptrio[c, h, index] = weights
        outs.append(mm(weights, v))
    mixed[rows, pl.ds(pl.multiple_of(c * 256, 256), 128)] = jnp.where(low, outs[0], outs[1]).astype(BF)
    mixed[rows, pl.ds(pl.multiple_of(c * 256 + 128, 128), 128)] = outs[2].astype(BF)


def attend(at, c, qkv, mixed, pbig, ptrio):
    mixed[SLOTS - 16 : SLOTS, pl.ds(pl.multiple_of(c * 256, 256), 256)] = jnp.zeros((16, 256), BF)
    segments(at, lambda first, is_big, i: attend_segment(c, first, is_big, i, qkv, mixed, pbig, ptrio))


def transpose_into(dst, src, tiles):
    def body(j):
        lanes = pl.ds(pl.multiple_of(j * 128, 128), 128)
        dst[lanes, :] = src[:, lanes].T

    loop(tiles, body)


def count_crops(labels, first_image):
    images = labels.shape[0]
    image = lax.broadcasted_iota(jnp.int32, labels.shape, 0)
    crop = labels - CROPS * (first_image + image)
    lane = lax.broadcasted_iota(jnp.int32, (images, 128), 1)
    offset = (IMAGE_LEN * lax.broadcasted_iota(jnp.int32, (images, 1), 0)).astype(F32)
    table = jnp.zeros((images, 128), F32)
    bigs = jnp.zeros((images, 1), F32)
    for p in range(CROPS):
        size = jnp.sum((crop == p).astype(F32), axis=1, keepdims=True)
        start = jnp.sum((crop < p).astype(F32), axis=1, keepdims=True) + offset
        big = (size == float(BIG_CROP)).astype(F32)
        at_lane = jnp.where(big > 0.5, bigs, 2.0 + float(p) - bigs)
        table = jnp.where(lane == at_lane.astype(jnp.int32), start, table)
        bigs = bigs + big
    return table


def slot_tokens(table, row, shape, dim):
    slot = lax.broadcasted_iota(jnp.int32, shape, dim)
    token = jnp.full(shape, -1, jnp.int32)
    at_big = (0, 2, 4, 5)[row]
    at_small = (0, 3, 6, 15)[row]
    for first, length, is_big, index in slot_segments(row // 2):
        if is_big:
            k = at_big + index
            start = table[k // 2 : k // 2 + 1, k % 2 : k % 2 + 1]
        else:
            k = at_small + index
            start = table[k // 8 : k // 8 + 1, 2 + k % 8 : 3 + k % 8]
        inside = jnp.logical_and(slot >= first, slot < first + length)
        token = jnp.where(inside, start.astype(jnp.int32) + (slot - first), token)
    return jnp.where(token < 0, -1, (token & 1) * TOK + (token >> 1))


def forward_kernel(
    x_in, g_in, labels, wq_in, wo_in, w1_in, w2_in, gains_in, biases_in,
    wq_h, wo_h, w1_h, w2_h, x_h, mid_h, a1t_h, a2t_h, mixt_h, qkv_h, pbig_h, ptrio_h, act_h, slope_h, cot_h, cott_h, out_h, where_h,
    wq, wo, w1, w2, tok, send_x, send_g, land_x, land_g, x, mid, midb, a1, a1t, a2t, mixed, mixt, qkv, pbig, ptrio,
    act, slope, cot, cott, gains, biases, fc1_bias, qkv_bias, tables, column, where, branch_two,
    zs, zr, xs, xr, ys, yr, ds, dr, cs, cr, exs, exr, egs, egr, tbs, tbr, hs,
):
    at = Place()
    refs = (wq, wo, w1, w2)
    sends = Sends()
    gather = Gather(at, refs, sends, FORWARD_DIRECT, zs, zr, xs, xr, ys, yr, ds, dr, cs, cr)
    stores = []

    def keep(src, dst):
        copy = pltpu.make_async_copy(src, dst, hs.at[len(stores)])
        copy.start()
        stores.append(copy)

    pairs = x_in.shape[0]
    wqv, wov = wq.reshape(4, 768, QW), wo.reshape(4, 1024, 192)
    w1v, w2v = w1.reshape(4, 768, 768), w2.reshape(4, 768, 768)
    groups = (at.c, at.cs, at.cx, at.cs + 2 - 4 * at.x)

    def joined(ref, first, count):
        return jnp.concatenate([ref[first + i : first + i + 1, :] for i in range(count)], axis=1)

    def start():
        tables[at.z] = jnp.zeros((8, 128), F32)
        tables[at.z, 0:3, :] = count_crops(labels[...], (at.y * 4 + at.z) * 3)
        heads = [wq_in[n].astype(BF) for n in range(3)]
        wq[at.c, at.z, at.y] = jnp.concatenate(
            [v[:, 0:128] for v in heads] + [v[:, 128:192] for v in heads] + [jnp.zeros((96, HALF), BF)], axis=1
        )
        wo[at.z, at.c, pl.ds(pl.multiple_of(at.y * 96, 32), 96), :] = wo_in[...].astype(BF)
        w1[at.c, at.z, at.y] = w1_in[...].astype(BF)
        w2[at.c, at.z, :, pl.ds(pl.multiple_of(at.y * 384, 128), 384)] = w2_in[...].astype(BF)
        at.enter()
        for k in (1, 2, 3):
            sends.start(tables.at[at.z], tables.at[at.z], tbs.at[k - 1], tbr.at[at.z], at.zth(lax.rem(at.z + k, 4)))

    def pick(n, send):
        for half in (0, 1):
            ref = x_in if n == 0 else g_in
            tok[n, half * TOK + TOK - 16 : half * TOK + TOK, :] = jnp.zeros((16, 192), BF)
            tok[n, half * TOK : half * TOK + pairs, :] = ref[:, half * 192 : half * 192 + 192]

        def block(r):
            one = (lax.broadcasted_iota(jnp.int32, (SLOTS, 2 * TOK), 1) == column[r]).astype(F32).astype(BF)
            value = mm(one, tok[n]).astype(BF)
            for i in range(SLOTS // CHUNK):
                put_block(send, r, i, value[i * CHUNK : i * CHUNK + CHUNK])

        loop(4, block)

    def pick_x():
        for k in (1, 2, 3):
            s = lax.rem(at.z + k, 4)
            arrived(tables.at[s], tbr.at[s], at.yn)
        table = tables[at.c]
        for r in range(4):
            column[r] = slot_tokens(table, r, (SLOTS, 1), 0)
            where[r] = slot_tokens(table, r, (1, SLOTS), 1)
        keep(where, where_h)
        pick(0, send_x)
        land_x[at.z] = send_x[at.z]
        wo[:, :, 192:256, :] = jnp.zeros((4, 4, 64, 192), BF)
        for n in (0, 1):
            gains[n : n + 1, :] = joined(gains_in, 6 * n, 6)
        for n in range(6):
            biases[n : n + 1, :] = joined(biases_in, 6 * n, 6)
        nothing = jnp.zeros((1, 128), F32)
        for c in range(4):
            fc1_bias[c] = joined(biases_in, 36 + 6 * c, 6)
            q = biases[2:3, c * 192 : c * 192 + 192]
            v = biases[3:4, c * 192 : c * 192 + 192]
            qkv_bias[c] = jnp.concatenate(
                [q[:, 0:128], nothing, v[:, 0:128], q[:, 128:192], nothing[:, 0:HALF], v[:, 128:192], nothing[:, 0:HALF]],
                axis=1,
            )

    def pick_g():
        pick(1, send_g)
        land_g[at.z] = send_g[at.z]

    def norm_one():
        def one(i, rows):
            value = get_blocks(land_x, i)
            x[rows, :] = value
            normed, _ = row_stats(value.astype(F32))
            a1[rows, :] = (normed * gains[0:1, :] + biases[0:1, :]).astype(BF)

        chunks(one)
        keep(x, x_h)

    def project(i):
        c = groups[i]
        for n in range(0, QW, 256):
            wide = min(256, QW - n)
            qkv[c, :, n : n + wide] = (mm(a1[...], wqv[c, :, n : n + wide]) + qkv_bias[c, :, n : n + wide]).astype(BF)

    def transpose_one():
        transpose_into(a1t, a1, 6)
        a1t[768:784, :] = jnp.ones((16, SLOTS), BF)
        keep(a1t, a1t_h)

    def branch():
        def one(z):
            midb[z] = mm(mixed[...], wov[z])

        loop(4, one)
        keep(qkv, qkv_h)
        keep(pbig, pbig_h)
        keep(ptrio, ptrio_h)

    def norm_two():
        def one(i, rows):
            value = x[rows, :].astype(F32) + jnp.concatenate([midb[r, rows, :] for r in range(4)], axis=1) + biases[4:5, :]
            mid[rows, :] = value
            normed, _ = row_stats(value)
            a1[rows, :] = (normed * gains[1:2, :] + biases[1:2, :]).astype(BF)

        chunks(one)
        keep(mid, mid_h)

    def expand(i):
        c = groups[i]

        def tile(n):
            lanes = pl.ds(pl.multiple_of(n * 256, 256), 256)
            hidden = mm(a1[...], w1v[c, :, lanes]) + fc1_bias[c, :, lanes]
            share = 0.5 + 0.5 * lax.erf(hidden * 0.7071067811865476)
            bell = jnp.exp(hidden * hidden * -0.5) * 0.3989422804014327
            act[c, :, lanes] = (hidden * share).astype(BF)
            slope[c, :, lanes] = (share + hidden * bell).astype(BF)

        loop(3, tile)
        keep(act.at[c], act_h.at[c])
        keep(slope.at[c], slope_h.at[c])

    def transpose_two():
        transpose_into(a2t, a1, 6)
        a2t[768:784, :] = jnp.ones((16, SLOTS), BF)
        keep(a2t, a2t_h)

    def transpose_mixed():
        transpose_into(mixt, mixed, 8)
        mixt[192:208, :] = jnp.ones((16, SLOTS), BF)
        keep(mixt, mixt_h)

    def join():
        def one(i, rows):
            cot[rows, :] = get_blocks(land_g, i)

        chunks(one)
        keep(cot, cot_h)

    def transpose_cot():
        transpose_into(cott, cot, 6)
        keep(cott, cott_h)

    def contract(i):
        c = groups[i]

        def tile(n):
            rows = pl.ds(pl.multiple_of(n * 256, 256), 256)
            part = mm_nt(act[c], w2v[c, rows, :])
            if i == 0:
                branch_two[:, rows] = part + biases[5:6, rows] + mid[:, rows]
            else:
                branch_two[:, rows] = branch_two[:, rows] + part

        loop(3, tile)

    def split():
        def one(i, rows):
            value = branch_two[rows, :].astype(BF)
            for r in range(4):
                put_block(land_x, r, i, value[:, r * 192 : r * 192 + 192])

        chunks(one)
        keep(land_x, out_h)

    def ready_b(p):
        gather.ready(p, 1)
        keep((wqv, wov, w1v, w2v)[p], (wq_h, wo_h, w1_h, w2_h)[p])

    steps = [start, pick_x, pick_g, norm_one, transpose_one, branch, norm_two, transpose_two, transpose_mixed, join]
    steps += [
        transpose_cot,
        split,
        lambda: exchange_start(at, sends, send_x, land_x, exs, exr),
        lambda: exchange_start(at, sends, send_g, land_g, egs, egr),
        lambda: exchange_wait(at, land_x, exr),
        lambda: exchange_wait(at, land_g, egr),
    ]
    for step in (project, lambda i: attend(at, groups[i], qkv, mixed, pbig, ptrio), expand, contract):
        steps += [functools.partial(step, i) for i in range(4)]
    for p in (WQ, WO, W1, W2):
        steps += [
            functools.partial(gather.own_across, p),
            functools.partial(gather.own_along, p),
            functools.partial(gather.corner, p),
            functools.partial(gather.ready, p, 0),
            functools.partial(ready_b, p),
        ]
        steps += [functools.partial(gather.along, p, j) for j in (1, 2, 3)]
        steps += [functools.partial(gather.cross, p, j) for j in range(4)]
    for number in FORWARD_ORDER:
        steps[number]()
    sends.drain()
    for copy in stores:
        copy.wait()


FORWARD_OUT = (
    ((4, 768, QW), BF), ((4, 1024, 192), BF), ((4, 768, 768), BF), ((4, 768, 768), BF),
    ((SLOTS, D), BF), ((SLOTS, D), F32), ((784, SLOTS), BF), ((784, SLOTS), BF), ((1024, SLOTS), BF),
    ((4, SLOTS, QW), BF), ((4, 3, 2, BIG_SLOTS, BIG_SLOTS), BF), ((4, 3, 3, TRIO_SLOTS, TRIO_SLOTS), BF),
    ((4, SLOTS, 768), BF), ((4, SLOTS, 768), BF), ((SLOTS, D), BF), ((D, SLOTS), BF), ((4, BLOCK, 128), BF),
    ((4, 1, SLOTS), jnp.int32),
)


def run_forward(*operands):
    sem = pltpu.SemaphoreType.DMA
    vmem = pltpu.VMEM
    return pl.pallas_call(
        forward_kernel,
        out_shape=[jax.ShapeDtypeStruct(s, t) for s, t in FORWARD_OUT],
        in_specs=[pl.BlockSpec(memory_space=vmem)] * len(operands),
        out_specs=[pl.BlockSpec(memory_space=pl.ANY)] * len(FORWARD_OUT),
        scratch_shapes=[
            vmem((4, 4, 2, 96, QW), BF), vmem((4, 4, 256, 192), BF), vmem((4, 4, 2, 96, 768), BF), vmem((4, 4, 192, 768), BF),
            vmem((2, 2 * TOK, 192), BF),
            vmem((4, BLOCK, 128), BF), vmem((4, BLOCK, 128), BF), vmem((4, BLOCK, 128), BF), vmem((4, BLOCK, 128), BF),
            vmem((SLOTS, D), BF), vmem((SLOTS, D), F32), vmem((4, SLOTS, 192), F32), vmem((SLOTS, D), BF),
            vmem((784, SLOTS), BF), vmem((784, SLOTS), BF), vmem((SLOTS, 1024), BF), vmem((1024, SLOTS), BF),
            vmem((4, SLOTS, QW), BF), vmem((4, 3, 2, BIG_SLOTS, BIG_SLOTS), BF), vmem((4, 3, 3, TRIO_SLOTS, TRIO_SLOTS), BF),
            vmem((4, SLOTS, 768), BF), vmem((4, SLOTS, 768), BF), vmem((SLOTS, D), BF), vmem((D, SLOTS), BF),
            vmem((2, D), F32), vmem((6, D), F32), vmem((4, 1, D), F32), vmem((4, 1, QW), F32), vmem((4, 8, 128), F32),
            vmem((4, SLOTS, 1), jnp.int32), vmem((4, 1, SLOTS), jnp.int32), vmem((SLOTS, D), F32),
            sem((4, 4)), sem((4, 4)), sem((4, 4)), sem((4, 4)), sem((4, 4)), sem((4, 4)), sem((4, 4)), sem((4, 4)),
            sem((4, 4)), sem((4, 4)), sem((3,)), sem((4,)), sem((3,)), sem((4,)), sem((3,)), sem((4,)), sem((len(FORWARD_OUT) + 6,)),
        ],
        compiler_params=pltpu.CompilerParams(collective_id=0, has_side_effects=True, vmem_limit_bytes=VMEM_LIMIT),
    )(*operands)


FORWARD_ORDER = (
    0, 33, 68, 44, 45, 32, 57, 1, 37, 49, 38, 52, 40, 39, 41, 12, 53, 50, 42, 61, 56, 54, 43, 51, 62, 2, 64, 35, 34,
    36, 55, 63, 69, 13, 65, 14, 76, 66, 46, 3, 17, 16, 47, 18, 67, 73, 19, 20, 21, 4, 48, 23, 58, 22, 74, 5, 6, 59,
    77, 60, 26, 78, 27, 75, 8, 24, 7, 25, 79, 28, 71, 29, 15, 9, 10, 70, 30, 72, 31, 11,
)
FORWARD_DIRECT = ()


def parts_of(ref, p, *lead, count=1):
    *outer, first = lead
    if p != W2:
        return ref.at[(*outer, first) if count == 1 else (*outer, pl.ds(first, count))]
    rows = pl.ds(pl.multiple_of(first * 192, 192), count * 192)
    return ref.at[(*outer[:-1], rows, pl.ds(pl.multiple_of(outer[-1] * 384, 128), 384))]


class Reduce:
    def __init__(self, at, sends, grads, pair, corner, cross, along, owned, squares, direct, sems):
        self.at, self.sends = at, sends
        self.grads, self.pair, self.corner, self.cross, self.along = grads, pair, corner, cross, along
        self.owned, self.squares, self.direct = owned, squares, direct
        self.ss, self.rs = sems

    def start(self, p, n, src, dst, peer, arrival=None, when=None):
        self.sends.start(src, dst, self.ss.at[p, n], self.rs.at[p, n if arrival is None else arrival], peer, when=when)

    def grad(self, p, c, y, s, count=1):
        return parts_of(self.grads[p], p, c, y, s, count=count)

    def half(self, ref, p, i, first):
        if p != W2:
            return ref.at[i, pl.ds(first, 2)]
        return ref.at[i, pl.ds(first * 192, 384)]

    def one(self, ref, p, i, s):
        return ref.at[i, s] if p != W2 else ref.at[i, pl.ds(pl.multiple_of(s * 192, 192), 192)]

    def far_and_near(self, i):
        return self.at.cx if i == 0 else self.at.c

    def pair_send(self, p, i):
        at = self.at
        c = 2 * ((1 - at.x) if i == 0 else at.x) + 1 - at.core
        self.start(p, i, self.grads[p].at[c], self.pair[p].at[i], at.cn)

    def add(self, count, pair):
        def one(s):
            mine, other = pair(s)
            mine[...] = mine[...] + other[...]

        loop(count, one)

    def add_pair(self, p, i, y):
        c = self.far_and_near(i)
        self.add(4, lambda s: (self.grad(p, c, y, s), parts_of(self.pair[p], p, i, y, s)))

    def far_sum(self, p):
        at = self.at
        arrived(self.pair[p].at[0], self.rs.at[p, 0], at.yn)
        self.add_pair(p, 0, 1 - at.y)
        self.start(p, 2, self.grad(p, at.cx, 1 - at.y, 0, 2), self.corner[p].at[0], at.xn)
        self.start(p, 3, self.grad(p, at.cx, 1 - at.y, 2, 2), self.corner[p].at[1], at.yn)
        self.add_pair(p, 0, at.y)
        self.start(p, 4, self.grad(p, at.cx, at.y, 0, 2), self.half(self.cross[p], p, 0, 0), at.xn)

    def near_sum(self, p):
        at = self.at
        arrived(self.pair[p].at[1], self.rs.at[p, 1], at.yn)
        self.add_pair(p, 1, 1 - at.y)
        self.start(p, 5, self.grad(p, at.c, 1 - at.y, 2, 2), self.half(self.cross[p], p, 1, 2), at.yn)
        self.add_pair(p, 1, at.y)

    def corner_a(self, p):
        at, corner = self.at, self.corner[p]
        arrived(corner.at[0], self.rs.at[p, 2], at.yn)
        self.add(2, lambda s: (self.grad(p, at.c, 1 - at.y, s), self.one(corner, p, 0, s)))
        self.start(p, 6, self.grad(p, at.c, 1 - at.y, 0, 2), self.half(self.cross[p], p, 1, 0), at.yn)

    def corner_b(self, p):
        at, corner = self.at, self.corner[p]
        arrived(corner.at[1], self.rs.at[p, 3], at.yn)
        self.add(2, lambda s: (self.grad(p, at.cx, at.y, s + 2), self.one(corner, p, 1, s)))
        self.start(p, 7, self.grad(p, at.cx, at.y, 2, 2), self.half(self.cross[p], p, 0, 2), at.xn)

    def cross_sum(self, p):
        at, cross = self.at, self.cross[p]
        for n, (i, first) in ((4, (0, 0)), (7, (0, 2)), (5, (1, 2)), (6, (1, 0))):
            arrived(self.half(cross, p, i, first), self.rs.at[p, n], at.yn)

        def one(s):
            mine = self.grad(p, at.c, at.y, s)
            mine[...] = mine[...] + self.one(cross, p, 0, s)[...] + self.one(cross, p, 1, s)[...]

        loop(4, one)
        line = self.along[p]

        def mine(s):
            return self.grad(p, at.c, at.y, s)

        if p in self.direct:
            for n in (1, 2, 3):
                s = at.other(n)
                self.start(p, 7 + n, mine(s), line.at[at.z], at.zth(s), arrival=8 + at.z)
            return
        end = jnp.logical_not(at.mid)
        near = jnp.where(at.mid, at.z - at.step, at.z + at.step)
        self.start(p, 8, mine(near), line.at[0], at.zth(near), arrival=8)
        for n in (2, 3):
            self.start(p, 7 + n, mine(at.other(n)), line.at[n], at.zth(near), arrival=8 + n, when=end)

    def line_sum(self, p):
        at, line = self.at, self.along[p]
        if p in self.direct:
            return

        @pl.when(at.mid)
        def _():
            for n in (2, 3):
                arrived(line.at[n], self.rs.at[p, 8 + n], at.yn)
                mine = self.grad(p, at.c, at.y, at.other(n - 1))
                mine[...] = mine[...] + line[n]

        for n in (2, 3):
            s = at.other(n - 1)
            self.start(p, 9 + n, self.grad(p, at.c, at.y, s), line.at[1], at.zth(s), arrival=9, when=at.mid)

    def along_sum(self, p):
        at, line = self.at, self.along[p]
        total = self.grad(p, at.c, at.y, at.z)[...].astype(F32)
        for n in (1, 2, 3) if p in self.direct else (0, 1):
            s = at.other(n) if p in self.direct else n
            arrived(line.at[s], self.rs.at[p, 8 + s], at.yn)
            total = total + line[s].astype(F32)
        self.owned[p][...] = total
        wide = total.shape[1]
        self.squares[:, 0:wide] = self.squares[:, 0:wide] + jnp.sum(total * total, axis=0, keepdims=True)


class Total:
    def __init__(self, at, sends, mine, line, plane, sems):
        self.at, self.sends, self.mine, self.line, self.plane = at, sends, mine, line, plane
        self.line_s, self.line_r, self.plane_s, self.plane_r, self.back_s, self.back_r = sems
        self.rows = line.shape[1]
        self.cut = mine.shape[0] != self.rows

    def part(self, ref, z):
        return ref.at[pl.ds(pl.multiple_of(z * self.rows, 8), self.rows)] if self.cut else ref

    def start(self):
        at = self.at
        self.line[at.z] = self.part(self.mine, at.z)[...]
        for k in (1, 2, 3):
            to = lax.rem(at.z + k, 4)
            self.sends.start(
                self.part(self.mine, to), self.line.at[at.z], self.line_s.at[k - 1], self.line_r.at[at.z], at.zth(to)
            )

    def spread(self):
        at = self.at
        for k in (1, 2, 3):
            s = lax.rem(at.z + k, 4)
            arrived(self.line.at[s], self.line_r.at[s], at.yn)
        me = at.y * 4 + at.c
        self.plane[me] = self.line[0] + self.line[1] + self.line[2] + self.line[3]
        for k in range(1, 8):
            to = lax.rem(me + k, 8)
            peer = (lax.div(to, 4), at.z, lax.rem(to, 4))
            self.sends.start(self.plane.at[me], self.plane.at[me], self.plane_s.at[k - 1], self.plane_r.at[me], peer)

    def collect(self):
        at = self.at
        me = at.y * 4 + at.c
        for k in range(1, 8):
            s = lax.rem(me + k, 8)
            arrived(self.plane.at[s], self.plane_r.at[s], at.yn)
        value = self.plane[0]
        for s in range(1, 8):
            value = value + self.plane[s]
        return value

    def share(self, whole):
        at = self.at
        mine = self.part(whole, at.z)
        mine[...] = self.collect()
        for k in (1, 2, 3):
            self.sends.start(mine, mine, self.back_s.at[k - 1], self.back_r.at[at.z], at.zth(lax.rem(at.z + k, 4)))

    def finish(self, whole):
        for k in (1, 2, 3):
            s = lax.rem(self.at.z + k, 4)
            arrived(self.part(whole, s), self.back_r.at[s], self.at.yn)


def fold(value):
    return value[0:8] + value[8:16] + value[16:24] + value[24:32]


def back_segment(c, slot, first, is_big, index, qkv, weights_big, weights_trio, mixed, grads):
    size = BIG_SLOTS if is_big else TRIO_SLOTS
    rows = pl.ds(first, size)
    q01 = qkv[c, rows, 0:128]
    k01 = qkv[c, rows, 128:256]
    v01 = qkv[c, rows, 256:384]
    kq2 = swap_halves(qkv[c, rows, 384:512])
    v2 = qkv[c, rows, 512:640]
    g01 = mixed[rows, pl.ds(pl.multiple_of(c * 256, 256), 128)]
    g2 = mixed[rows, pl.ds(pl.multiple_of(c * 256 + 128, 128), 128)]
    low = lane_low(size)
    none = jnp.zeros((size, 128), BF)
    dq, dk, dv = [], [], []
    for h, (g, gs, q, k, v) in enumerate((
        (g01, jnp.where(low, g01, none), q01, k01, v01),
        (g01, jnp.where(low, none, g01), q01, k01, v01),
        (g2, g2, kq2, kq2, v2),
    )):
        if is_big:
            weights = weights_big[slot, h, index]
        else:
            weights = weights_trio[slot, h, index]
        wide = weights.astype(F32)
        product = wide * mm_nt(gs, v)
        scores = (product - wide * jnp.sum(product, axis=1, keepdims=True)).astype(BF)
        dq.append(mm(scores, k))
        dk.append(mm_tn(scores, q))
        dv.append(mm_tn(weights, g))
    scale = HEAD_DIM**-0.5
    grads[c, rows, 0:128] = (jnp.where(low, dq[0], dq[1]) * scale).astype(BF)
    grads[c, rows, 128:256] = (jnp.where(low, dk[0], dk[1]) * scale).astype(BF)
    grads[c, rows, 256:384] = jnp.where(low, dv[0], dv[1]).astype(BF)
    grads[c, rows, 384:512] = (jnp.where(low, dq[2], dk[2]) * scale).astype(BF)
    grads[c, rows, 512:640] = dv[2].astype(BF)


def backward_kernel(
    wq_h, wo_h, w1_h, w2_h, x_h, mid_h, a1t_h, a2t_h, mixt_h, qkv_h, pbig_h, ptrio_h, act_h, slope_h, cot_h, cott_h, out_h,
    gains_in,
    own_q, own_o, own_1, own_2, total, square_total, land_out, land_in,
    ring, wo, gq, go, g1, g2, pq, po, p1, p2, nq, no, n1, n2, rq, ro, r1, r2, lq, lo, l1, l2,
    act, slope, cot, cott, a2t, a1t, mixt, mid, x, pbig, ptrio, gmix, grad, half, send, gains, small, summed, squares, sums_of, line, plane, square_tile, square_line, square_plane,
    ss, rs, hs, ring_s, p_s, ex_s, ex_r, in_s, in_r, *total_sems,
):
    at = Place()
    sends = Sends()
    reduce = Reduce(
        at, sends, (gq, go, g1, g2), (pq, po, p1, p2), (nq, no, n1, n2), (rq, ro, r1, r2), (lq, lo, l1, l2),
        (own_q, own_o, own_1, own_2), squares, BACKWARD_DIRECT, (ss, rs),
    )
    loads = {}
    waited = []

    def load(name, src, dst):
        copy = pltpu.make_async_copy(src, dst, hs.at[len(loads) + len(waited)])
        copy.start()
        loads[name] = copy

    groups = (2 * (1 - at.x) + 1 - at.core, at.cx, at.cs, at.c)
    uses = [(ref, c) for ref in (w2_h, w1_h, wq_h) for c in groups]
    ring_copies = {}

    def ring_start(u):
        if u < len(uses):
            src, c = uses[u]
            wide = src.shape[2]
            copy = pltpu.make_async_copy(src.at[c], ring.at[u % 3, :, pl.ds(0, wide)], ring_s.at[u])
            copy.start()
            ring_copies[u] = copy

    def loaded(*names):
        for name in names:
            if name in loads:
                loads.pop(name).wait()
                waited.append(name)

    sums = Total(at, sends, small, line, plane, total_sems[:6])
    square_sum = Total(at, sends, square_tile, square_line, square_plane, total_sems[6:])
    keep_out = pltpu.make_async_copy(out_h.at[at.z], land_out.at[at.z], ex_s.at[3])
    keep_in = pltpu.make_async_copy(send.at[at.z], land_in.at[at.z], in_s.at[3])

    def start():
        load("cott", cott_h, cott)
        for i in range(4):
            load(f"act{i}", act_h.at[groups[i]], act.at[groups[i]])
        for u in range(3):
            ring_start(u)
        load("cot", cot_h, cot)
        for i in range(4):
            load(f"slope{i}", slope_h.at[groups[i]], slope.at[groups[i]])
        load("a2t", a2t_h, a2t)
        load("mid", mid_h, mid)
        load("mixt", mixt_h, mixt)
        load("wo", wo_h, wo)
        load("a1t", a1t_h, a1t)
        load("x", x_h, x)
        at_enter(at)
        squares[...] = jnp.zeros((1, D), F32)
        for n in (0, 1):
            gains[n : n + 1, :] = jnp.concatenate([gains_in[6 * n + i : 6 * n + i + 1, :] for i in range(6)], axis=1)

    def send_out():
        keep_out.start()
        exchange_start(at, sends, out_h, land_out, ex_s, ex_r)

    def grad_fc2(i):
        c = groups[i]
        loaded("cott", f"act{i}")

        def tile(n):
            lanes = pl.ds(pl.multiple_of(n * 256, 256), 256)
            g2[c, :, lanes] = mm(cott[...], act[c, :, lanes]).astype(BF)

        loop(3, tile)

    def grad_hidden(i):
        c = groups[i]
        loaded("cot", f"slope{i}")
        ring_copies[i].wait()

        def tile(n):
            lanes = pl.ds(pl.multiple_of(n * 256, 256), 256)
            slope[c, :, lanes] = (mm(cot[...], ring[i % 3, :, lanes]) * slope[c, :, lanes].astype(F32)).astype(BF)

        loop(3, tile)
        ring_start(i + 3)

    def rows_to_shards(dst, c, lanes, tile):
        for z in range(4):
            for y in range(2):
                first = (z * 2 + y) * 96
                dst[c, y, z, :, lanes] = tile[first : first + 96].astype(BF)

    def grad_fc1(i):
        c = groups[i]
        loaded("a2t")

        def tile(n):
            lanes = pl.ds(pl.multiple_of(n * 256, 256), 256)
            value = mm(a2t[...], slope[c, :, lanes])
            rows_to_shards(g1, c, lanes, value)
            sums_of[c, :, lanes] = value[768:769]

        loop(3, tile)

    def back_through(first_use, left, wide, i):
        u = first_use + i
        ring_copies[u].wait()

        def tile(n):
            lanes = pl.ds(pl.multiple_of(n * 256, 256), 256)
            part = mm_nt(left[groups[i], :, 0:wide], ring[u % 3, lanes, 0:wide])
            if i == 0:
                grad[:, lanes] = part
            else:
                grad[:, lanes] = grad[:, lanes] + part

        loop(3, tile)
        ring_start(u + 3)

    def put_row(first, value):
        for i in range(6):
            small[first + i : first + i + 1, :] = value[:, i * 128 : i * 128 + 128]

    def norm_two():
        loaded("mid")
        parts = [jnp.zeros((8, D), F32)] * 4

        def one(i, rows):
            normed, inverse = row_stats(mid[rows, :])
            upper = grad[rows, :]
            weighted = upper * gains[1:2, :]
            first = jnp.sum(weighted, axis=1, keepdims=True) * (1.0 / D)
            second = jnp.sum(weighted * normed, axis=1, keepdims=True) * (1.0 / D)
            straight = cot[rows, :].astype(F32)
            value = straight + inverse * (weighted - first - normed * second)
            mid[rows, :] = value
            branch = value.astype(BF)
            for r in range(4):
                half[r, rows, :] = branch[:, r * 192 : r * 192 + 192]
            for n, v in enumerate((upper * normed, upper, branch.astype(F32), straight)):
                parts[n] = parts[n] + fold(v)

        chunks(one)
        for first, value in zip((6, 18, 36, 42), parts):
            put_row(first, jnp.sum(value, axis=0, keepdims=True))

    def grad_out():
        loaded("mixt")

        def one(z):
            value = mm(mixt[...], half[z]).astype(BF)
            for c in range(4):
                for y in range(2):
                    go[c, y, z] = value[c * 256 + y * 96 : c * 256 + y * 96 + 96]

        loop(4, one)

    def grad_mixed():
        load("qkv", qkv_h, slope.at[:, :, pl.ds(0, QW)])
        loaded("wo")

        def one(c):
            rows = pl.ds(pl.multiple_of(c * 256, 256), 256)
            value = mm_nt(half[0], wo[0, rows, :])
            for z in (1, 2, 3):
                value = value + mm_nt(half[z], wo[z, rows, :])
            gmix[:, rows] = value.astype(BF)

        loop(4, one)
        for copy in fetch(0):
            copy.start()
        loaded("qkv")

    def fetch(i):
        c, slot = groups[i], i % 2
        return (
            pltpu.make_async_copy(pbig_h.at[c], pbig.at[slot], p_s.at[slot, 0]),
            pltpu.make_async_copy(ptrio_h.at[c], ptrio.at[slot], p_s.at[slot, 1]),
        )

    def attend_back(i):
        for copy in fetch(i):
            copy.wait()
        if i < 3:
            for copy in fetch(i + 1):
                copy.start()
        c = groups[i]
        act[c, SLOTS - 16 : SLOTS, 0:QW] = jnp.zeros((16, QW), BF)
        segments(
            at, lambda first, is_big, n: back_segment(c, i % 2, first, is_big, n, slope, pbig, ptrio, gmix, act)
        )

    def grad_q(i):
        c = groups[i]
        loaded("a1t")

        def tile(lanes):
            value = mm(a1t[...], act[c, :, lanes])
            rows_to_shards(gq, c, lanes, value)
            sums_of[4 + c, :, lanes] = value[768:769]

        loop(2, lambda n: tile(pl.ds(pl.multiple_of(n * 256, 256), 256)))
        tile(pl.ds(512, 128))

    def norm_one():
        loaded("x")
        parts = [jnp.zeros((8, D), F32)] * 2

        def one(i, rows):
            normed, inverse = row_stats(x[rows, :].astype(F32))
            upper = grad[rows, :]
            weighted = upper * gains[0:1, :]
            first = jnp.sum(weighted, axis=1, keepdims=True) * (1.0 / D)
            second = jnp.sum(weighted * normed, axis=1, keepdims=True) * (1.0 / D)
            value = (mid[rows, :] + inverse * (weighted - first - normed * second)).astype(BF)
            for r in range(4):
                put_block(send, r, i, value[:, r * 192 : r * 192 + 192])
            for n, v in enumerate((upper * normed, upper)):
                parts[n] = parts[n] + fold(v)

        chunks(one)
        for first, value in zip((0, 12), parts):
            put_row(first, jnp.sum(value, axis=0, keepdims=True))

    def send_in():
        exchange_start(at, sends, send, land_in, in_s, in_r)
        keep_in.start()

    def start_total():
        for c in range(4):
            put_row(48 + 6 * c, sums_of[c])
        packed = [sums_of[4 + c] for c in range(4)]
        for first, lanes in ((24, (0, 384)), (30, (256, 512))):
            parts = []
            for value in packed:
                parts += [value[:, lanes[0] : lanes[0] + 128], value[:, lanes[1] : lanes[1] + HALF]]
            put_row(first, jnp.concatenate(parts, axis=1))
        small[72:96, :] = jnp.zeros((24, 128), F32)
        sums.start()

    def finish_total():
        sums.finish(summed)
        total[...] = summed[...]

    def start_squares():
        value = squares[:, 0:128]
        for i in range(1, 6):
            value = value + squares[:, i * 128 : i * 128 + 128]
        square_tile[...] = jnp.zeros((8, 128), F32)
        square_tile[0:1, :] = value
        square_sum.start()

    def finish_squares():
        square_total[...] = square_sum.collect()

    def wait_exchanges():
        exchange_wait(at, land_out, ex_r)
        exchange_wait(at, land_in, in_r)
        keep_out.wait()
        keep_in.wait()

    steps = [start, send_out, norm_two, grad_out, grad_mixed, norm_one, send_in, start_total, sums.spread]
    steps += [lambda: sums.share(summed), finish_total, start_squares, square_sum.spread, finish_squares, wait_exchanges]
    through_fc1 = functools.partial(back_through, 4, slope, 768)
    through_q = functools.partial(back_through, 8, act, QW)
    for step in (grad_fc2, grad_hidden, grad_fc1, through_fc1, attend_back, grad_q, through_q):
        steps += [functools.partial(step, i) for i in range(4)]
    for p in (WQ, WO, W1, W2):
        steps += [functools.partial(reduce.pair_send, p, 0), functools.partial(reduce.pair_send, p, 1)]
        for step in (
            reduce.far_sum, reduce.near_sum, reduce.corner_a, reduce.corner_b, reduce.cross_sum, reduce.line_sum, reduce.along_sum
        ):
            steps.append(functools.partial(step, p))
    for number in BACKWARD_ORDER:
        steps[number]()
    sends.drain()


def at_enter(at):
    barrier = pltpu.get_barrier_semaphore()
    me = at.y * 4 + at.c
    peers = [at.zth(lax.rem(at.z + k, 4)) for k in (1, 2, 3)]
    for k in range(1, 8):
        to = lax.rem(me + k, 8)
        peers.append((lax.div(to, 4), at.z, lax.rem(to, 4)))
    for peer in peers:
        pl.semaphore_signal(barrier, inc=1, device_id=peer, device_id_type=MESH)
    pl.semaphore_wait(barrier, len(peers))


SHARDS = ((96, QW), (96, 192), (96, 768), (192, 384))


def run_backward(*operands):
    sem = pltpu.SemaphoreType.DMA
    vmem = pltpu.VMEM
    shape = jax.ShapeDtypeStruct
    stages = [(4, 2, 4), (2, 2, 4), (2, 2), (2, 4), (4,)]
    matrices = [(4, 768, 768), (2, 768, 768), (2, 384, 384), (2, 768, 384), (4, 192, 384)]
    return pl.pallas_call(
        backward_kernel,
        out_shape=[shape(s, F32) for s in SHARDS] + [shape((96, 128), F32), shape((8, 128), F32)] + [shape((4, BLOCK, 128), BF)] * 2,
        in_specs=[pl.BlockSpec(memory_space=pl.ANY)] * (len(operands) - 1) + [pl.BlockSpec(memory_space=vmem)],
        out_specs=[pl.BlockSpec(memory_space=vmem)] * 6 + [pl.BlockSpec(memory_space=pl.ANY)] * 2,
        scratch_shapes=[vmem((3, 768, 768), BF), vmem((4, 1024, 192), BF)]
        + [
            vmem(whole if s == SHARDS[W2] else lead + s, BF) for lead, whole in zip(stages, matrices) for s in SHARDS
        ]
        + [
            vmem((4, SLOTS, 768), BF), vmem((4, SLOTS, 768), BF), vmem((SLOTS, D), BF), vmem((D, SLOTS), BF),
            vmem((784, SLOTS), BF), vmem((784, SLOTS), BF), vmem((1024, SLOTS), BF), vmem((SLOTS, D), F32),
            vmem((SLOTS, D), BF), vmem((2, 3, 2, BIG_SLOTS, BIG_SLOTS), BF), vmem((2, 3, 3, TRIO_SLOTS, TRIO_SLOTS), BF),
            vmem((SLOTS, 1024), BF), vmem((SLOTS, D), F32), vmem((4, SLOTS, 192), BF), vmem((4, BLOCK, 128), BF),
            vmem((2, D), F32), vmem((96, 128), F32), vmem((96, 128), F32), vmem((1, D), F32), vmem((8, 1, D), F32),
            vmem((4, 24, 128), F32), vmem((8, 24, 128), F32), vmem((8, 128), F32), vmem((4, 8, 128), F32), vmem((8, 8, 128), F32),
            sem((4, 13)), sem((4, 13)), sem((18,)), sem((12,)), sem((2, 2)), sem((4,)), sem((4,)), sem((4,)), sem((4,)),
        ]
        + [sem((n,)) for n in (3, 4, 7, 8, 3, 4)] * 2,
        compiler_params=pltpu.CompilerParams(collective_id=1, has_side_effects=True, vmem_limit_bytes=VMEM_LIMIT),
    )(*operands)


BACKWARD_ORDER = (
    0, 1, 15, 70, 16, 17, 72, 18, 71, 19, 20, 21, 73, 24, 23, 22, 75, 74, 25, 61, 27, 28, 63, 62, 26, 29, 30, 2, 64,
    3, 4, 76, 66, 53, 31, 65, 77, 32, 36, 55, 33, 67, 52, 68, 35, 39, 54, 34, 57, 56, 43, 40, 41, 42, 45, 58, 5, 6,
    59, 78, 37, 44, 38, 48, 69, 46, 7, 47, 49, 60, 50, 8, 51, 11, 9, 12, 10, 13, 14,
)
BACKWARD_DIRECT = ()


RATES = (D**-0.5, (D // 24) ** -0.5, D**-0.5, FF**-0.5, 0.3, 0.3)
ROWS = 208


def update_kernel(
    own_q, own_o, own_1, own_2, total, square_total, land_out, land_in, where,
    wq, wo, w1, w2, wg, wb, mq, mo, m1, m2, mg, mb, vq, vo, v1, v2, vg, vb,
    out, grad_in, norm,
    nmq, nvq, nwq, hq, nmo, nvo, nwo, ho, nm1, nv1, nw1, h1, nm2, nv2, nw2, h2, nmg, nvg, nwg, hg, nmb, nvb, nwb, hb,
    blocks,
):
    gains = total[0:12, :]
    biases = total[12:72, :]
    squares = jnp.sum(jnp.sum(square_total[...], axis=0, keepdims=True), axis=1, keepdims=True)
    for part in (gains, biases):
        squares = squares + jnp.sum(jnp.sum(part * part, axis=0, keepdims=True), axis=1, keepdims=True)
    size = jnp.sqrt(squares)
    norm[...] = size
    factor = jnp.minimum(1.0, CLIP_NORM / size)

    def step(rate, grad, pick, refs):
        weight, first, second, new_first, new_second, new_weight, half = refs
        results = adam_step(weight[pick], grad, first[pick], second[pick], rate, factor)
        for ref, value in zip((new_first, new_second, new_weight, half), results):
            ref[pick] = value

    everything = (slice(None), slice(None))
    packed = own_q[...]
    for n in range(3):
        grad = jnp.concatenate([packed[:, 128 * n : 128 * n + 128], packed[:, 384 + HALF * n : 448 + HALF * n]], axis=1)
        step(RATES[0], grad, n, (wq, mq, vq, nmq, nvq, nwq, hq))
    step(RATES[1], own_o[...], everything, (wo, mo, vo, nmo, nvo, nwo, ho))
    step(RATES[2], own_1[...], everything, (w1, m1, v1, nm1, nv1, nw1, h1))
    step(RATES[3], own_2[...], everything, (w2, m2, v2, nm2, nv2, nw2, h2))
    step(RATES[4], gains, everything, (wg, mg, vg, nmg, nvg, nwg, hg))
    step(RATES[5], biases, everything, (wb, mb, vb, nmb, nvb, nwb, hb))

    pairs = out.shape[0]
    for n, land in enumerate((land_out, land_in)):
        for r in range(4):
            for i in range(SLOTS // CHUNK):
                rows = slice(r * SLOTS + i * CHUNK, r * SLOTS + i * CHUNK + CHUNK)
                rest = land[r, SLOTS + i * 16 : SLOTS + i * 16 + 16, :]
                blocks[rows, n * 192 : n * 192 + 128] = land[r, i * CHUNK : i * CHUNK + CHUNK, :]
                blocks[rows, n * 192 + 128 : n * 192 + 192] = jnp.concatenate([rest[:, 0:HALF], rest[:, HALF:]], axis=0)
    for first in range(0, pairs, ROWS):
        count = min(ROWS, pairs - first)
        halves = []
        for half in (0, 1):
            token = half * TOK + first + lax.broadcasted_iota(jnp.int32, (ROWS, SLOTS), 0)
            one = jnp.concatenate([(token == where[r]).astype(F32).astype(BF) for r in range(4)], axis=1)
            halves.append(mm(one, blocks[...])[0:count])
        for ref, lanes in ((out, 0), (grad_in, 192)):
            even, odd = (value[:, lanes : lanes + 192] for value in halves)
            ref[first : first + count, 0, :] = jnp.concatenate([even, odd], axis=1)


def run_update(pairs, *operands):
    shape = jax.ShapeDtypeStruct
    shapes = [shape((pairs, 1, 384), F32)] * 2 + [shape((1, 1), F32)]
    for weight in operands[9:15]:
        shapes += [shape(weight.shape, F32)] * 3 + [shape(weight.shape, BF)]
    return pl.pallas_call(
        update_kernel,
        out_shape=shapes,
        in_specs=[pl.BlockSpec(memory_space=pltpu.VMEM)] * len(operands),
        out_specs=[pl.BlockSpec(memory_space=pltpu.VMEM)] * len(shapes),
        scratch_shapes=[pltpu.VMEM((4 * SLOTS, 384), BF)],
        compiler_params=pltpu.CompilerParams(vmem_limit_bytes=VMEM_LIMIT),
    )(*operands)


def prepare(layer_in, grad_out, crop_ids, w_qkv, w_out, w_fc1, w_fc2, norm_gains, all_biases):
    pairs = layer_in.shape[0]
    return (
        layer_in.reshape(pairs, 384), grad_out.reshape(pairs, 384), crop_ids.reshape(-1, IMAGE_LEN),
        w_qkv.transpose(1, 0, 2), w_out, w_fc1, w_fc2.T, norm_gains.reshape(12, 128), all_biases.reshape(60, 128),
    )


def local_fast(
    layer_in, grad_out, crop_ids, w_qkv, w_out, w_fc1, w_fc2, norm_gains, all_biases,
    first_qkv, second_qkv, first_out, second_out, first_fc1, second_fc1, first_fc2, second_fc2,
    first_gains, second_gains, first_biases, second_biases,
):
    pairs = layer_in.shape[0]
    operands = prepare(layer_in, grad_out, crop_ids, w_qkv, w_out, w_fc1, w_fc2, norm_gains, all_biases)
    *kept, where = run_forward(*operands)
    reduced = run_backward(*kept, operands[7])
    masters = operands[3:9]
    results = run_update(
        pairs, *reduced, where, *masters,
        first_qkv.transpose(1, 0, 2), first_out, first_fc1, first_fc2.T,
        first_gains.reshape(12, 128), first_biases.reshape(60, 128),
        second_qkv.transpose(1, 0, 2), second_out, second_fc1, second_fc2.T,
        second_gains.reshape(12, 128), second_biases.reshape(60, 128),
    )
    return (
        results[0], results[1], results[2].reshape(()),
        *[v.transpose(1, 0, 2) for v in results[3:7]], *results[7:15], *[v.T for v in results[15:19]],
        *[v.reshape(-1) for v in results[19:27]],
    )


def dot(a, b):
    return jnp.dot(a, b, preferred_element_type=F32)


def dot_nt(a, b):
    return lax.dot_general(a, b, (((1,), (1,)), ((), ())), preferred_element_type=F32)


def dot_tn(a, b):
    return lax.dot_general(a, b, (((0,), (0,)), ((), ())), preferred_element_type=F32)


def norm_stats(value):
    centre = jnp.mean(value, axis=1, keepdims=True)
    centred = value - centre
    spread = jnp.mean(centred * centred, axis=1, keepdims=True)
    inverse = lax.rsqrt(spread + NORM_EPS)
    return centred * inverse, inverse


def norm_back(grad, normed, inverse, gain):
    weighted = grad * gain
    first = jnp.mean(weighted, axis=1, keepdims=True)
    second = jnp.mean(weighted * normed, axis=1, keepdims=True)
    return inverse * (weighted - first - normed * second)


def layer(x, cot, crops, w_qkv, w_out, w_fc1, w_fc2, gains, biases):
    inputs = x.astype(F32)
    cotf = cot.astype(F32)
    normed_one, inverse_one = norm_stats(inputs)
    act_one = (normed_one * gains[:D] + biases[:D]).astype(BF)
    qkv_bias = jnp.concatenate([biases[2 * D : 3 * D], jnp.zeros((D,), F32), biases[3 * D : 4 * D]])
    qkv = (dot(act_one, w_qkv) + qkv_bias).astype(BF)
    heads = qkv.reshape(SLOTS, 3, HEADS, HEAD_DIM)
    q, k, v = heads[:, 0], heads[:, 1], heads[:, 2]
    scores = jnp.einsum("qhd,khd->hqk", q, k, preferred_element_type=F32) * HEAD_DIM ** (-0.5)
    scores = jnp.where((crops[:, None] == crops[None, :])[None], scores, MASKED)
    probs = jax.nn.softmax(scores, axis=2)
    half_probs = probs.astype(BF)
    mixed = jnp.einsum("hqk,khd->qhd", half_probs, v, preferred_element_type=F32)
    mixed = mixed.reshape(SLOTS, D).astype(BF)
    middle = inputs + dot(mixed, w_out) + biases[4 * D : 5 * D]
    normed_two, inverse_two = norm_stats(middle)
    act_two = (normed_two * gains[D:] + biases[D : 2 * D]).astype(BF)
    hidden = dot(act_two, w_fc1) + biases[6 * D :]
    active, gelu_pull = jax.vjp(lambda h: jax.nn.gelu(h, approximate=False), hidden)
    active = active.astype(BF)
    out = middle + dot(active, w_fc2) + biases[5 * D : 6 * D]

    g_fc2 = dot_tn(active, cot)
    grad_hidden = gelu_pull(dot_nt(cot, w_fc2))[0].astype(BF)
    g_fc1 = dot_tn(act_two, grad_hidden)
    grad_two = dot_nt(grad_hidden, w_fc1)
    grad_middle = cotf + norm_back(grad_two, normed_two, inverse_two, gains[D:])
    branch = grad_middle.astype(BF)
    g_out = dot_tn(mixed, branch)
    grad_mixed = dot_nt(branch, w_out).astype(BF).reshape(SLOTS, HEADS, HEAD_DIM)
    grad_probs = jnp.einsum("qhd,khd->hqk", grad_mixed, v, preferred_element_type=F32)
    grad_scores = (probs * (grad_probs - jnp.sum(probs * grad_probs, axis=2, keepdims=True))).astype(BF)
    scale = HEAD_DIM ** (-0.5)
    grad_q = jnp.einsum("hqk,khd->qhd", grad_scores, k, preferred_element_type=F32) * scale
    grad_k = jnp.einsum("hqk,qhd->khd", grad_scores, q, preferred_element_type=F32) * scale
    grad_v = jnp.einsum("hqk,qhd->khd", half_probs, grad_mixed, preferred_element_type=F32)
    grad_qkv = jnp.stack([grad_q, grad_k, grad_v], axis=1).astype(BF).reshape(SLOTS, 3 * D)
    g_qkv = dot_tn(act_one, grad_qkv)
    grad_one = dot_nt(grad_qkv, w_qkv)
    grad_in = grad_middle + norm_back(grad_one, normed_one, inverse_one, gains[:D])

    g_gains = jnp.concatenate([jnp.sum(grad_one * normed_one, axis=0), jnp.sum(grad_two * normed_two, axis=0)])
    qkv_sums = jnp.sum(grad_qkv.astype(F32), axis=0)
    g_biases = jnp.concatenate([
        jnp.sum(grad_one, axis=0),
        jnp.sum(grad_two, axis=0),
        qkv_sums[:D],
        qkv_sums[2 * D :],
        jnp.sum(branch.astype(F32), axis=0),
        jnp.sum(cotf, axis=0),
        jnp.sum(grad_hidden.astype(F32), axis=0),
    ])
    return out, grad_in, g_qkv, g_out, g_fc1, g_fc2, g_gains, g_biases


def adam_step(weight, grad, first, second, rate, factor):
    clipped = grad * factor
    new_first = BETA_ONE * first + (1.0 - BETA_ONE) * clipped
    new_second = BETA_TWO * second + (1.0 - BETA_TWO) * clipped * clipped
    unbiased_first = new_first / (1.0 - BETA_ONE**STEP)
    unbiased_second = new_second / (1.0 - BETA_TWO**STEP)
    new_weight = weight - rate * (
        unbiased_first / (jnp.sqrt(unbiased_second) + ADAM_EPS) + DECAY * weight
    )
    return (new_first, new_second, new_weight, new_weight.astype(BF))


def gather(value, axes):
    for name, dim in axes:
        value = lax.all_gather(value, name, axis=dim, tiled=True)
    return value


def scatter(value, axes):
    for name, dim in axes:
        value = lax.psum_scatter(value, name, scatter_dimension=dim, tiled=True)
    return value.astype(F32)


def local_plain(
    layer_in, grad_out, crop_ids, w_qkv, w_out, w_fc1, w_fc2, norm_gains, all_biases,
    first_qkv, second_qkv, first_out, second_out, first_fc1, second_fc1, first_fc2, second_fc2,
    first_gains, second_gains, first_biases, second_biases,
):
    row = lax.axis_index("row")
    n_row, n_col = lax.axis_size("row"), lax.axis_size("col")
    feat = D // n_row
    pairs = layer_in.shape[0]
    labels = lax.ppermute(
        crop_ids, ("row", "col"), [(r * n_col + c, c * n_row + r) for r in range(n_row) for c in range(n_col)]
    )
    sources = slot_sources(labels).reshape(-1)
    place = jnp.where(sources < 0, -1, (sources % 2) * pairs + sources // 2)
    pick = (place[:, None] == jnp.arange(2 * pairs, dtype=jnp.int32)[None, :]).astype(BF)

    def to_slots(value):
        halves = jnp.concatenate([value[:, 0, :feat], value[:, 0, feat:]], axis=0)
        sent = dot(pick, halves).astype(BF)
        got = lax.all_to_all(sent, "row", 0, 0, tiled=True)
        return got.reshape(n_row, SLOTS, feat).transpose(1, 0, 2).reshape(SLOTS, D)

    def to_tokens(value):
        sent = value.astype(BF).reshape(SLOTS, n_row, feat).transpose(1, 0, 2).reshape(n_row * SLOTS, feat)
        got = lax.all_to_all(sent, "row", 0, 0, tiled=True)
        halves = dot_tn(pick, got)
        return jnp.concatenate([halves[:pairs], halves[pairs:]], axis=1).reshape(pairs, 1, 2 * feat)

    full_qkv = gather(w_qkv.astype(BF), (("dp", 0), ("row", 0), ("col", 2))).reshape(D, 3 * D)
    full_out = gather(w_out.astype(BF), (("dp", 0), ("col", 0), ("row", 1)))
    full_fc1 = gather(w_fc1.astype(BF), (("dp", 0), ("row", 0), ("col", 1)))
    full_fc2 = gather(w_fc2.astype(BF), (("dp", 0), ("col", 0), ("row", 1)))
    crops = jnp.where(row < 2, slot_crops(0), slot_crops(1))
    out, grad_in, g_qkv, g_out, g_fc1, g_fc2, g_gains, g_biases = layer(
        to_slots(layer_in), to_slots(grad_out), crops, full_qkv, full_out, full_fc1, full_fc2, norm_gains, all_biases
    )
    owned_qkv = scatter(g_qkv.astype(BF).reshape(D, 3, D), (("col", 2), ("row", 0), ("dp", 0)))
    owned_out = scatter(g_out.astype(BF), (("row", 1), ("col", 0), ("dp", 0)))
    owned_fc1 = scatter(g_fc1.astype(BF), (("col", 1), ("row", 0), ("dp", 0)))
    owned_fc2 = scatter(g_fc2.astype(BF), (("row", 1), ("col", 0), ("dp", 0)))
    local_squares = (
        jnp.sum(owned_qkv * owned_qkv)
        + jnp.sum(owned_out * owned_out)
        + jnp.sum(owned_fc1 * owned_fc1)
        + jnp.sum(owned_fc2 * owned_fc2)
    )
    grad_gains, grad_biases, weight_squares = lax.psum((g_gains, g_biases, local_squares), ("dp", "row", "col"))
    grad_norm = jnp.sqrt(weight_squares + jnp.sum(grad_gains * grad_gains) + jnp.sum(grad_biases * grad_biases))
    factor = jnp.minimum(1.0, CLIP_NORM / grad_norm)
    upd_qkv = adam_step(w_qkv, owned_qkv, first_qkv, second_qkv, D ** (-0.5), factor)
    upd_out = adam_step(w_out, owned_out, first_out, second_out, (D // 24) ** (-0.5), factor)
    upd_fc1 = adam_step(w_fc1, owned_fc1, first_fc1, second_fc1, D ** (-0.5), factor)
    upd_fc2 = adam_step(w_fc2, owned_fc2, first_fc2, second_fc2, FF ** (-0.5), factor)
    upd_gains = adam_step(norm_gains, grad_gains, first_gains, second_gains, 0.3, factor)
    upd_biases = adam_step(all_biases, grad_biases, first_biases, second_biases, 0.3, factor)
    return (
        to_tokens(out), to_tokens(grad_in), grad_norm,
        *upd_qkv, *upd_out, *upd_fc1, *upd_fc2, *upd_gains, *upd_biases,
    )


def solution(mesh):
    tokens = P(("dp", "col"), "row", None)
    qkv = P(("row", "dp"), None, "col")
    out = P(("col", "dp"), "row")
    fc1 = P(("row", "dp"), "col")
    whole = P()
    return jax.shard_map(
        local_fast if mesh.shape["dp"] == 2 else local_plain,
        mesh=mesh,
        in_specs=(
            tokens, tokens, P(("dp", "row")), qkv, out, fc1, out, whole, whole,
            qkv, qkv, out, out, fc1, fc1, out, out, whole, whole, whole, whole,
        ),
        out_specs=(tokens, tokens, whole) + (qkv,) * 4 + (out,) * 4 + (fc1,) * 4 + (out,) * 4 + (whole,) * 8,
        check_vma=False,
    )
```

```python
import functools

import jax
import jax.numpy as jnp
from jax import lax
from jax.experimental import pallas as pl
from jax.experimental.pallas import tpu as pltpu
from jax.sharding import PartitionSpec as P

HEADS = 12
HEAD_DIM = 64
FF = 3072
D = 768
BIG_CROP = 197
SMALL_CROP = 37
IMAGE_LEN = 690
CROPS = 10
STEP = 5

NORM_EPS = 1e-06
CLIP_NORM = 1.0
BETA_ONE = 0.5
BETA_TWO = 0.5
ADAM_EPS = 1e-08
DECAY = 0.05
MASKED = -1e30

SLOTS = 544
BIG_SLOTS = 208
TRIO_SLOTS = 112
TRIO = 3 * SMALL_CROP
BF = jnp.bfloat16
F32 = jnp.float32


def crop_starts(labels):
    images = labels.shape[0] // IMAGE_LEN
    places = labels.reshape(images, IMAGE_LEN) % CROPS
    order = jnp.arange(CROPS, dtype=jnp.int32)
    sizes = jnp.sum((places[:, :, None] == order).astype(jnp.int32), axis=1)
    starts = jnp.sum((places[:, :, None] < order).astype(jnp.int32), axis=1)
    starts = starts + IMAGE_LEN * jnp.arange(images, dtype=jnp.int32)[:, None]
    big = (sizes == BIG_CROP).astype(jnp.int32)
    earlier = (order[:, None] < order[None, :]).astype(jnp.int32)
    big_rank = jnp.sum(big[:, :, None] * earlier, axis=1)
    small_rank = jnp.sum((1 - big)[:, :, None] * earlier, axis=1)

    def ranked(flag, rank, count):
        hit = flag[:, :, None] * (rank[:, :, None] == jnp.arange(count, dtype=jnp.int32)).astype(jnp.int32)
        return jnp.sum(hit * starts[:, :, None], axis=1).reshape(-1)

    return ranked(big, big_rank, 2), ranked(1 - big, small_rank, CROPS - 2)


def slot_segments(kind):
    if kind == 0:
        bigs, trios = 2, 1
    else:
        bigs, trios = 1, 3
    parts = []
    at = 0
    for b in range(bigs):
        parts.append((at, BIG_CROP, True, b))
        at += BIG_SLOTS
    for s in range(3 * trios):
        parts.append((at + s // 3 * TRIO_SLOTS + s % 3 * SMALL_CROP, SMALL_CROP, False, s))
    return parts


def slot_sources(labels):
    big, small = crop_starts(labels)
    rows = []
    for row in range(4):
        kind = row // 2
        at_big = (0, 2, 4, 5)[row]
        at_small = (0, 3, 6, 15)[row]
        out = []
        filled = 0
        for first, length, is_big, index in slot_segments(kind):
            if first > filled:
                out.append(jnp.full((first - filled,), -1, jnp.int32))
            start = big[at_big + index] if is_big else small[at_small + index]
            out.append(start + jnp.arange(length, dtype=jnp.int32))
            filled = first + length
        if filled < SLOTS:
            out.append(jnp.full((SLOTS - filled,), -1, jnp.int32))
        rows.append(jnp.concatenate(out))
    return jnp.stack(rows)


def slot_crops(kind):
    slot = jnp.arange(SLOTS, dtype=jnp.int32)
    crop = jnp.full((SLOTS,), -1, jnp.int32)
    for number, (first, length, _, _) in enumerate(slot_segments(kind)):
        crop = jnp.where((slot >= first) & (slot < first + length), number, crop)
    return crop


MESH = pl.DeviceIdType.MESH
HALF = 64
QW = 640
TOK = 1040
CHUNK = 32
BLOCK = SLOTS + SLOTS // 2
WQ, WO, W1, W2 = 0, 1, 2, 3
VMEM_LIMIT = 60 * 2**20


def mm(a, b):
    return lax.dot_general(a, b, (((1,), (0,)), ((), ())), preferred_element_type=F32)


def mm_nt(a, b):
    return lax.dot_general(a, b, (((1,), (1,)), ((), ())), preferred_element_type=F32)


def mm_tn(a, b):
    return lax.dot_general(a, b, (((0,), (0,)), ((), ())), preferred_element_type=F32)


class Place:
    def __init__(self):
        self.y = lax.axis_index("dp")
        self.z = lax.axis_index("row")
        self.c = lax.axis_index("col")
        self.core = lax.rem(self.c, 2)
        self.x = lax.div(self.c, 2)
        self.cx = lax.rem(self.c + 2, 4)
        self.cs = self.c + 1 - 2 * self.core
        self.xn = (self.y, self.z, self.cx)
        self.yn = (1 - self.y, self.z, self.c)
        self.cn = (self.y, self.z, self.cs)
        self.low = self.z < 2
        self.mid = jnp.logical_or(self.z == 1, self.z == 2)
        self.step = jnp.where(self.low, 1, -1)

    def zth(self, z):
        return (self.y, z, self.c)

    def other(self, j):
        return lax.rem(self.z + self.step * j + 4, 4)

    def enter(self):
        barrier = pltpu.get_barrier_semaphore()
        peers = [self.zth(lax.rem(self.z + k, 4)) for k in (1, 2, 3)] + [self.xn, self.yn, self.cn]
        for peer in peers:
            pl.semaphore_signal(barrier, inc=1, device_id=peer, device_id_type=MESH)
        pl.semaphore_wait(barrier, len(peers))


def shard_of(refs, p, c, s, y):
    ref = refs[p]
    if p == WO:
        return ref.at[s, c, pl.ds(pl.multiple_of(y * 96, 32), 96), :]
    if p == W2:
        return ref.at[c, s, :, pl.ds(pl.multiple_of(y * 384, 128), 384)]
    return ref.at[c, s, y]


def group_of(refs, p, c, y):
    ref = refs[p]
    if p == WO:
        return ref.at[:, c, pl.ds(pl.multiple_of(y * 96, 32), 96), :]
    if p == W2:
        return ref.at[c, :, :, pl.ds(pl.multiple_of(y * 384, 128), 384)]
    return ref.at[c, :, y]


class Sends:
    def __init__(self):
        self.left = []

    def start(self, src, dst, send_sem, recv_sem, peer, when=None):
        copy = pltpu.make_async_remote_copy(
            src_ref=src, dst_ref=dst, send_sem=send_sem, recv_sem=recv_sem, device_id=peer, device_id_type=MESH
        )
        if when is None:
            copy.start()
        else:
            pl.when(when)(copy.start)
        self.left.append((copy, when))

    def drain(self):
        for copy, when in self.left:
            if when is None:
                copy.wait_send()
            else:
                pl.when(when)(copy.wait_send)
        self.left = []


def arrived(ref, sem, me):
    pltpu.make_async_remote_copy(
        src_ref=ref, dst_ref=ref, send_sem=sem, recv_sem=sem, device_id=me, device_id_type=MESH
    ).wait_recv()


class Gather:
    def __init__(self, at, refs, sends, direct, zs, zr, xs, xr, ys, yr, ds, dr, cs, cr):
        self.at, self.refs, self.sends, self.direct = at, refs, sends, direct
        self.zs, self.zr, self.xs, self.xr = zs, zr, xs, xr
        self.ys, self.yr, self.ds, self.dr, self.cs, self.cr = ys, yr, ds, dr, cs, cr

    def across(self, p, s):
        at = self.at
        own = shard_of(self.refs, p, at.c, s, at.y)
        self.sends.start(own, own, self.xs.at[p, s], self.xr.at[p, s], at.xn)
        self.sends.start(own, own, self.ys.at[p, s], self.yr.at[p, s], at.yn)

    def own_across(self, p):
        self.across(p, self.at.z)

    def own_along(self, p):
        at = self.at
        own = shard_of(self.refs, p, at.c, at.z, at.y)
        if p in self.direct:
            for j in (1, 2, 3):
                self.sends.start(own, own, self.zs.at[p, j - 1], self.zr.at[p, at.z], at.zth(at.other(j)))
            return
        second = jnp.where(at.mid, at.z - at.step, at.z + 2 * at.step)
        self.sends.start(own, own, self.zs.at[p, 0], self.zr.at[p, at.z], at.zth(at.z + at.step))
        self.sends.start(own, own, self.zs.at[p, 1], self.zr.at[p, at.z], at.zth(second))

    def to_core(self, p, g, c, y):
        ref = group_of(self.refs, p, c, y)
        self.sends.start(ref, ref, self.cs.at[p, g], self.cr.at[p, g], self.at.cn)

    def along(self, p, j):
        at = self.at
        s = at.other(j)
        ref = shard_of(self.refs, p, at.c, s, at.y)
        arrived(ref, self.zr.at[p, s], at.yn)
        if j < 3 and p not in self.direct:
            self.sends.start(ref, ref, self.zs.at[p, 1 + j], self.zr.at[p, s], at.zth(at.z - at.step), when=at.mid)
        self.across(p, s)
        if j == 3:
            self.to_core(p, 0, at.c, at.y)

    def cross(self, p, j):
        at = self.at
        s = at.other(j)
        from_x = shard_of(self.refs, p, at.cx, s, at.y)
        from_y = shard_of(self.refs, p, at.c, s, 1 - at.y)
        arrived(from_x, self.xr.at[p, s], at.yn)
        arrived(from_y, self.yr.at[p, s], at.yn)
        if j < 2:
            self.sends.start(from_x, from_x, self.ds.at[p, j], self.dr.at[p, s], at.yn)
        else:
            self.sends.start(from_y, from_y, self.ds.at[p, j], self.dr.at[p, s], at.xn)
        if j == 3:
            self.to_core(p, 1, at.cx, at.y)
            self.to_core(p, 2, at.c, 1 - at.y)

    def corner(self, p):
        at = self.at
        for j in (0, 1, 2, 3):
            s = at.other(j)
            arrived(shard_of(self.refs, p, at.cx, s, 1 - at.y), self.dr.at[p, s], at.yn)
        self.to_core(p, 3, at.cx, 1 - at.y)

    def ready(self, p, half):
        at = self.at
        c = at.cs if half == 0 else at.cs + 2 - 4 * at.x
        arrived(group_of(self.refs, p, c, at.y), self.cr.at[p, half], at.yn)
        arrived(group_of(self.refs, p, c, 1 - at.y), self.cr.at[p, 2 + half], at.yn)


def exchange_start(at, sends, blocks, landing, send_sems, recv_sems):
    for k in (1, 2, 3):
        to = lax.rem(at.z + k, 4)
        sends.start(blocks.at[to], landing.at[at.z], send_sems.at[k - 1], recv_sems.at[at.z], at.zth(to))


def exchange_wait(at, landing, recv_sems):
    for k in (1, 2, 3):
        s = lax.rem(at.z + k, 4)
        arrived(landing.at[s], recv_sems.at[s], at.yn)


def row_stats(value):
    centre = jnp.sum(value, axis=1, keepdims=True) * (1.0 / D)
    centred = value - centre
    spread = jnp.sum(centred * centred, axis=1, keepdims=True) * (1.0 / D)
    inverse = lax.rsqrt(spread + NORM_EPS)
    return centred * inverse, inverse


def chunks(body):
    for i in range(SLOTS // CHUNK):
        body(i, slice(i * CHUNK, i * CHUNK + CHUNK))


def put_block(ref, r, i, value):
    ref[r, i * CHUNK : i * CHUNK + CHUNK, :] = value[:, 0:128]
    first = SLOTS + i * (CHUNK // 2)
    ref[r, first : first + CHUNK // 2, :] = jnp.concatenate([value[0:16, 128:192], value[16:32, 128:192]], axis=1)


def get_blocks(ref, i):
    parts = []
    first = SLOTS + i * (CHUNK // 2)
    for r in range(4):
        parts.append(ref[r, i * CHUNK : i * CHUNK + CHUNK, :])
        rest = ref[r, first : first + CHUNK // 2, :]
        parts.append(jnp.concatenate([rest[:, 0:HALF], rest[:, HALF:]], axis=0))
    return jnp.concatenate(parts, axis=1)


def loop(count, body):
    def step(i, carry):
        body(i)
        return carry

    lax.fori_loop(0, count, step, 0)


def lane_low(rows):
    return lax.broadcasted_iota(jnp.int32, (rows, 2 * HALF), 1) < HALF


def swap_halves(value):
    return jnp.concatenate([value[:, HALF:], value[:, :HALF]], axis=1)


def segments(at, body):
    for bigs in (2, 1):

        @pl.when(at.low if bigs == 2 else jnp.logical_not(at.low))
        def _():
            for i in range(bigs):
                body(i * BIG_SLOTS, True, i)
            for i in range(1 if bigs == 2 else 3):
                body(bigs * BIG_SLOTS + i * TRIO_SLOTS, False, i)


def key_mask(size, is_big):
    key = lax.broadcasted_iota(jnp.int32, (size, size), 0)
    if is_big:
        return key < BIG_CROP
    query = lax.broadcasted_iota(jnp.int32, (size, size), 1)

    def crop(v):
        return (v >= SMALL_CROP).astype(jnp.int32) + (v >= 2 * SMALL_CROP).astype(jnp.int32) + (v >= TRIO).astype(jnp.int32)

    return jnp.logical_and(crop(query) == crop(key), key < TRIO)


def attend_segment(c, first, is_big, index, qkv, mixed, pbig, ptrio):
    size = BIG_SLOTS if is_big else TRIO_SLOTS
    rows = pl.ds(first, size)
    q01 = qkv[c, rows, 0:128]
    k01 = qkv[c, rows, 128:256]
    v01 = qkv[c, rows, 256:384]
    qk2 = qkv[c, rows, 384:512]
    v2 = qkv[c, rows, 512:640]
    low = lane_low(size)
    none = jnp.zeros((size, 128), BF)
    mask = key_mask(size, is_big)
    outs = []
    for h, (q, k, v) in enumerate((
        (jnp.where(low, q01, none), k01, v01),
        (jnp.where(low, none, q01), k01, v01),
        (jnp.where(low, qk2, none), swap_halves(qk2), v2),
    )):
        scores = jnp.where(mask, mm_nt(k, q) * HEAD_DIM**-0.5, MASKED)
        weights = jnp.exp(scores - jnp.max(scores, axis=0, keepdims=True))
        total = jnp.sum(weights, axis=0, keepdims=True)
        weights = (weights * (1.0 / total)).astype(BF)
        if is_big:
            pbig[c, h, index] = weights
        else:
            ptrio[c, h, index] = weights
        outs.append(mm_tn(weights, v))
    mixed[rows, pl.ds(pl.multiple_of(c * 256, 256), 128)] = jnp.where(low, outs[0], outs[1]).astype(BF)
    mixed[rows, pl.ds(pl.multiple_of(c * 256 + 128, 128), 128)] = outs[2].astype(BF)


def attend(at, c, qkv, mixed, pbig, ptrio):
    mixed[SLOTS - 16 : SLOTS, pl.ds(pl.multiple_of(c * 256, 256), 256)] = jnp.zeros((16, 256), BF)
    segments(at, lambda first, is_big, i: attend_segment(c, first, is_big, i, qkv, mixed, pbig, ptrio))


def transpose_into(dst, src, tiles):
    def body(j):
        lanes = pl.ds(pl.multiple_of(j * 128, 128), 128)
        dst[lanes, :] = src[:, lanes].T

    loop(tiles, body)


def count_crops(labels, first_image):
    images = labels.shape[0]
    image = lax.broadcasted_iota(jnp.int32, labels.shape, 0)
    crop = labels - CROPS * (first_image + image)
    lane = lax.broadcasted_iota(jnp.int32, (images, 128), 1)
    offset = (IMAGE_LEN * lax.broadcasted_iota(jnp.int32, (images, 1), 0)).astype(F32)
    table = jnp.zeros((images, 128), F32)
    bigs = jnp.zeros((images, 1), F32)
    for p in range(CROPS):
        size = jnp.sum((crop == p).astype(F32), axis=1, keepdims=True)
        start = jnp.sum((crop < p).astype(F32), axis=1, keepdims=True) + offset
        big = (size == float(BIG_CROP)).astype(F32)
        at_lane = jnp.where(big > 0.5, bigs, 2.0 + float(p) - bigs)
        table = jnp.where(lane == at_lane.astype(jnp.int32), start, table)
        bigs = bigs + big
    return table


def slot_tokens(table, row, shape, dim):
    slot = lax.broadcasted_iota(jnp.int32, shape, dim)
    token = jnp.full(shape, -1, jnp.int32)
    at_big = (0, 2, 4, 5)[row]
    at_small = (0, 3, 6, 15)[row]
    for first, length, is_big, index in slot_segments(row // 2):
        if is_big:
            k = at_big + index
            start = table[k // 2 : k // 2 + 1, k % 2 : k % 2 + 1]
        else:
            k = at_small + index
            start = table[k // 8 : k // 8 + 1, 2 + k % 8 : 3 + k % 8]
        inside = jnp.logical_and(slot >= first, slot < first + length)
        token = jnp.where(inside, start.astype(jnp.int32) + (slot - first), token)
    return jnp.where(token < 0, -1, (token & 1) * TOK + (token >> 1))


def forward_kernel(
    x_in, g_in, labels, wq_in, wo_in, w1_in, w2_in, gains_in, biases_in,
    wq_h, wo_h, w1_h, w2_h, x_h, mid_h, a1t_h, a2t_h, mixt_h, qkv_h, pbig_h, ptrio_h, act_h, slope_h, cot_h, cott_h, out_h, where_h,
    wq, wo, w1, w2, tok, send_x, send_g, land_x, land_g, x, mid, midb, a1, a1t, a2t, mixed, mixt, qkv, pbig, ptrio,
    act, slope, cot, cott, gains, biases, fc1_bias, qkv_bias, tables, column, where, branch_two,
    zs, zr, xs, xr, ys, yr, ds, dr, cs, cr, exs, exr, egs, egr, tbs, tbr, hs,
):
    at = Place()
    refs = (wq, wo, w1, w2)
    sends = Sends()
    gather = Gather(at, refs, sends, FORWARD_DIRECT, zs, zr, xs, xr, ys, yr, ds, dr, cs, cr)
    stores = []

    def keep(src, dst):
        copy = pltpu.make_async_copy(src, dst, hs.at[len(stores)])
        copy.start()
        stores.append(copy)

    pairs = x_in.shape[0]
    wqv, wov = wq.reshape(4, 768, QW), wo.reshape(4, 1024, 192)
    w1v, w2v = w1.reshape(4, 768, 768), w2.reshape(4, 768, 768)
    groups = (at.c, at.cs, at.cx, at.cs + 2 - 4 * at.x)

    def joined(ref, first, count):
        return jnp.concatenate([ref[first + i : first + i + 1, :] for i in range(count)], axis=1)

    def start():
        tables[at.z] = jnp.zeros((8, 128), F32)
        tables[at.z, 0:3, :] = count_crops(labels[...], (at.y * 4 + at.z) * 3)
        heads = [wq_in[n].astype(BF) for n in range(3)]
        wq[at.c, at.z, at.y] = jnp.concatenate(
            [v[:, 0:128] for v in heads] + [v[:, 128:192] for v in heads] + [jnp.zeros((96, HALF), BF)], axis=1
        )
        wo[at.z, at.c, pl.ds(pl.multiple_of(at.y * 96, 32), 96), :] = wo_in[...].astype(BF)
        w1[at.c, at.z, at.y] = w1_in[...].astype(BF)
        w2[at.c, at.z, :, pl.ds(pl.multiple_of(at.y * 384, 128), 384)] = w2_in[...].astype(BF)
        at.enter()
        for k in (1, 2, 3):
            sends.start(tables.at[at.z], tables.at[at.z], tbs.at[k - 1], tbr.at[at.z], at.zth(lax.rem(at.z + k, 4)))

    def pick(n, send):
        for half in (0, 1):
            ref = x_in if n == 0 else g_in
            tok[n, half * TOK + TOK - 16 : half * TOK + TOK, :] = jnp.zeros((16, 192), BF)
            tok[n, half * TOK : half * TOK + pairs, :] = ref[:, half * 192 : half * 192 + 192]

        def block(r):
            one = (lax.broadcasted_iota(jnp.int32, (SLOTS, 2 * TOK), 1) == column[r]).astype(F32).astype(BF)
            value = mm(one, tok[n]).astype(BF)
            for i in range(SLOTS // CHUNK):
                put_block(send, r, i, value[i * CHUNK : i * CHUNK + CHUNK])

        loop(4, block)

    def pick_x():
        for k in (1, 2, 3):
            s = lax.rem(at.z + k, 4)
            arrived(tables.at[s], tbr.at[s], at.yn)
        table = tables[at.c]
        for r in range(4):
            column[r] = slot_tokens(table, r, (SLOTS, 1), 0)
            where[r] = slot_tokens(table, r, (1, SLOTS), 1)
        keep(where, where_h)
        pick(0, send_x)
        land_x[at.z] = send_x[at.z]
        wo[:, :, 192:256, :] = jnp.zeros((4, 4, 64, 192), BF)
        for n in (0, 1):
            gains[n : n + 1, :] = joined(gains_in, 6 * n, 6)
        for n in range(6):
            biases[n : n + 1, :] = joined(biases_in, 6 * n, 6)
        nothing = jnp.zeros((1, 128), F32)
        for c in range(4):
            fc1_bias[c] = joined(biases_in, 36 + 6 * c, 6)
            q = biases[2:3, c * 192 : c * 192 + 192]
            v = biases[3:4, c * 192 : c * 192 + 192]
            qkv_bias[c] = jnp.concatenate(
                [q[:, 0:128], nothing, v[:, 0:128], q[:, 128:192], nothing[:, 0:HALF], v[:, 128:192], nothing[:, 0:HALF]],
                axis=1,
            )

    def pick_g():
        pick(1, send_g)
        land_g[at.z] = send_g[at.z]

    def norm_one():
        def one(i, rows):
            value = get_blocks(land_x, i)
            x[rows, :] = value
            normed, _ = row_stats(value.astype(F32))
            a1[rows, :] = (normed * gains[0:1, :] + biases[0:1, :]).astype(BF)

        chunks(one)
        keep(x, x_h)

    def project(i):
        c = groups[i]
        for n in range(0, QW, 256):
            wide = min(256, QW - n)
            qkv[c, :, n : n + wide] = (mm(a1[...], wqv[c, :, n : n + wide]) + qkv_bias[c, :, n : n + wide]).astype(BF)

    def transpose_one():
        transpose_into(a1t, a1, 6)
        a1t[768:784, :] = jnp.ones((16, SLOTS), BF)
        keep(a1t, a1t_h)

    def branch():
        def one(z):
            midb[z] = mm(mixed[...], wov[z])

        loop(4, one)
        keep(qkv, qkv_h)
        keep(pbig, pbig_h)
        keep(ptrio, ptrio_h)

    def norm_two():
        def one(i, rows):
            value = x[rows, :].astype(F32) + jnp.concatenate([midb[r, rows, :] for r in range(4)], axis=1) + biases[4:5, :]
            mid[rows, :] = value
            normed, _ = row_stats(value)
            a1[rows, :] = (normed * gains[1:2, :] + biases[1:2, :]).astype(BF)

        chunks(one)
        keep(mid, mid_h)

    def expand(i):
        c = groups[i]

        def tile(n):
            lanes = pl.ds(pl.multiple_of(n * 256, 256), 256)
            hidden = mm(a1[...], w1v[c, :, lanes]) + fc1_bias[c, :, lanes]
            share = 0.5 + 0.5 * lax.erf(hidden * 0.7071067811865476)
            bell = jnp.exp(hidden * hidden * -0.5) * 0.3989422804014327
            act[c, :, lanes] = (hidden * share).astype(BF)
            slope[c, :, lanes] = (share + hidden * bell).astype(BF)

        loop(3, tile)
        keep(act.at[c], act_h.at[c])
        keep(slope.at[c], slope_h.at[c])

    def transpose_two():
        transpose_into(a2t, a1, 6)
        a2t[768:784, :] = jnp.ones((16, SLOTS), BF)
        keep(a2t, a2t_h)

    def transpose_mixed():
        transpose_into(mixt, mixed, 8)
        mixt[192:208, :] = jnp.ones((16, SLOTS), BF)
        keep(mixt, mixt_h)

    def join():
        def one(i, rows):
            cot[rows, :] = get_blocks(land_g, i)

        chunks(one)
        keep(cot, cot_h)

    def transpose_cot():
        transpose_into(cott, cot, 6)
        keep(cott, cott_h)

    def contract(i):
        c = groups[i]

        def tile(n):
            rows = pl.ds(pl.multiple_of(n * 256, 256), 256)
            part = mm_nt(act[c], w2v[c, rows, :])
            if i == 0:
                branch_two[:, rows] = part + biases[5:6, rows] + mid[:, rows]
            else:
                branch_two[:, rows] = branch_two[:, rows] + part

        loop(3, tile)

    def split():
        def one(i, rows):
            value = branch_two[rows, :].astype(BF)
            for r in range(4):
                put_block(land_x, r, i, value[:, r * 192 : r * 192 + 192])

        chunks(one)
        keep(land_x, out_h)

    def ready_b(p):
        gather.ready(p, 1)
        keep((wqv, wov, w1v, w2v)[p], (wq_h, wo_h, w1_h, w2_h)[p])

    steps = [start, pick_x, pick_g, norm_one, transpose_one, branch, norm_two, transpose_two, transpose_mixed, join]
    steps += [
        transpose_cot,
        split,
        lambda: exchange_start(at, sends, send_x, land_x, exs, exr),
        lambda: exchange_start(at, sends, send_g, land_g, egs, egr),
        lambda: exchange_wait(at, land_x, exr),
        lambda: exchange_wait(at, land_g, egr),
    ]
    for step in (project, lambda i: attend(at, groups[i], qkv, mixed, pbig, ptrio), expand, contract):
        steps += [functools.partial(step, i) for i in range(4)]
    for p in (WQ, WO, W1, W2):
        steps += [
            functools.partial(gather.own_across, p),
            functools.partial(gather.own_along, p),
            functools.partial(gather.corner, p),
            functools.partial(gather.ready, p, 0),
            functools.partial(ready_b, p),
        ]
        steps += [functools.partial(gather.along, p, j) for j in (1, 2, 3)]
        steps += [functools.partial(gather.cross, p, j) for j in range(4)]
    for number in FORWARD_ORDER:
        steps[number]()
    sends.drain()
    for copy in stores:
        copy.wait()


FORWARD_OUT = (
    ((4, 768, QW), BF), ((4, 1024, 192), BF), ((4, 768, 768), BF), ((4, 768, 768), BF),
    ((SLOTS, D), BF), ((SLOTS, D), F32), ((784, SLOTS), BF), ((784, SLOTS), BF), ((1024, SLOTS), BF),
    ((4, SLOTS, QW), BF), ((4, 3, 2, BIG_SLOTS, BIG_SLOTS), BF), ((4, 3, 3, TRIO_SLOTS, TRIO_SLOTS), BF),
    ((4, SLOTS, 768), BF), ((4, SLOTS, 768), BF), ((SLOTS, D), BF), ((D, SLOTS), BF), ((4, BLOCK, 128), BF),
    ((4, 1, SLOTS), jnp.int32),
)


def run_forward(*operands):
    sem = pltpu.SemaphoreType.DMA
    vmem = pltpu.VMEM
    return pl.pallas_call(
        forward_kernel,
        out_shape=[jax.ShapeDtypeStruct(s, t) for s, t in FORWARD_OUT],
        in_specs=[pl.BlockSpec(memory_space=vmem)] * len(operands),
        out_specs=[pl.BlockSpec(memory_space=pl.ANY)] * len(FORWARD_OUT),
        scratch_shapes=[
            vmem((4, 4, 2, 96, QW), BF), vmem((4, 4, 256, 192), BF), vmem((4, 4, 2, 96, 768), BF), vmem((4, 4, 192, 768), BF),
            vmem((2, 2 * TOK, 192), BF),
            vmem((4, BLOCK, 128), BF), vmem((4, BLOCK, 128), BF), vmem((4, BLOCK, 128), BF), vmem((4, BLOCK, 128), BF),
            vmem((SLOTS, D), BF), vmem((SLOTS, D), F32), vmem((4, SLOTS, 192), F32), vmem((SLOTS, D), BF),
            vmem((784, SLOTS), BF), vmem((784, SLOTS), BF), vmem((SLOTS, 1024), BF), vmem((1024, SLOTS), BF),
            vmem((4, SLOTS, QW), BF), vmem((4, 3, 2, BIG_SLOTS, BIG_SLOTS), BF), vmem((4, 3, 3, TRIO_SLOTS, TRIO_SLOTS), BF),
            vmem((4, SLOTS, 768), BF), vmem((4, SLOTS, 768), BF), vmem((SLOTS, D), BF), vmem((D, SLOTS), BF),
            vmem((2, D), F32), vmem((6, D), F32), vmem((4, 1, D), F32), vmem((4, 1, QW), F32), vmem((4, 8, 128), F32),
            vmem((4, SLOTS, 1), jnp.int32), vmem((4, 1, SLOTS), jnp.int32), vmem((SLOTS, D), F32),
            sem((4, 4)), sem((4, 4)), sem((4, 4)), sem((4, 4)), sem((4, 4)), sem((4, 4)), sem((4, 4)), sem((4, 4)),
            sem((4, 4)), sem((4, 4)), sem((3,)), sem((4,)), sem((3,)), sem((4,)), sem((3,)), sem((4,)), sem((len(FORWARD_OUT) + 6,)),
        ],
        compiler_params=pltpu.CompilerParams(collective_id=0, has_side_effects=True, vmem_limit_bytes=VMEM_LIMIT),
    )(*operands)


FORWARD_ORDER = (
    0, 33, 68, 44, 45, 32, 57, 1, 37, 49, 38, 52, 40, 39, 41, 12, 53, 50, 42, 61, 56, 54, 43, 51, 62, 2, 64, 35, 34,
    36, 55, 63, 69, 13, 65, 14, 76, 66, 46, 3, 17, 16, 47, 18, 67, 73, 19, 20, 21, 4, 48, 23, 58, 22, 74, 5, 6, 59,
    77, 60, 26, 78, 27, 75, 8, 24, 7, 25, 79, 28, 71, 29, 15, 9, 10, 70, 30, 72, 31, 11,
)
FORWARD_DIRECT = ()


def parts_of(ref, p, *lead, count=1):
    *outer, first = lead
    if p != W2:
        return ref.at[(*outer, first) if count == 1 else (*outer, pl.ds(first, count))]
    rows = pl.ds(pl.multiple_of(first * 192, 192), count * 192)
    return ref.at[(*outer[:-1], rows, pl.ds(pl.multiple_of(outer[-1] * 384, 128), 384))]


class Reduce:
    def __init__(self, at, sends, grads, pair, corner, cross, along, owned, squares, direct, sems):
        self.at, self.sends = at, sends
        self.grads, self.pair, self.corner, self.cross, self.along = grads, pair, corner, cross, along
        self.owned, self.squares, self.direct = owned, squares, direct
        self.ss, self.rs = sems

    def start(self, p, n, src, dst, peer, arrival=None, when=None):
        self.sends.start(src, dst, self.ss.at[p, n], self.rs.at[p, n if arrival is None else arrival], peer, when=when)

    def grad(self, p, c, y, s, count=1):
        return parts_of(self.grads[p], p, c, y, s, count=count)

    def half(self, ref, p, i, first):
        if p != W2:
            return ref.at[i, pl.ds(first, 2)]
        return ref.at[i, pl.ds(first * 192, 384)]

    def one(self, ref, p, i, s):
        return ref.at[i, s] if p != W2 else ref.at[i, pl.ds(pl.multiple_of(s * 192, 192), 192)]

    def far_and_near(self, i):
        return self.at.cx if i == 0 else self.at.c

    def pair_send(self, p, i):
        at = self.at
        c = 2 * ((1 - at.x) if i == 0 else at.x) + 1 - at.core
        self.start(p, i, self.grads[p].at[c], self.pair[p].at[i], at.cn)

    def add(self, count, pair):
        def one(s):
            mine, other = pair(s)
            mine[...] = mine[...] + other[...]

        loop(count, one)

    def add_pair(self, p, i, y):
        c = self.far_and_near(i)
        self.add(4, lambda s: (self.grad(p, c, y, s), parts_of(self.pair[p], p, i, y, s)))

    def far_sum(self, p):
        at = self.at
        arrived(self.pair[p].at[0], self.rs.at[p, 0], at.yn)
        self.add_pair(p, 0, 1 - at.y)
        self.start(p, 2, self.grad(p, at.cx, 1 - at.y, 0, 2), self.corner[p].at[0], at.xn)
        self.start(p, 3, self.grad(p, at.cx, 1 - at.y, 2, 2), self.corner[p].at[1], at.yn)
        self.add_pair(p, 0, at.y)
        self.start(p, 4, self.grad(p, at.cx, at.y, 0, 2), self.half(self.cross[p], p, 0, 0), at.xn)

    def near_sum(self, p):
        at = self.at
        arrived(self.pair[p].at[1], self.rs.at[p, 1], at.yn)
        self.add_pair(p, 1, 1 - at.y)
        self.start(p, 5, self.grad(p, at.c, 1 - at.y, 2, 2), self.half(self.cross[p], p, 1, 2), at.yn)
        self.add_pair(p, 1, at.y)

    def corner_a(self, p):
        at, corner = self.at, self.corner[p]
        arrived(corner.at[0], self.rs.at[p, 2], at.yn)
        self.add(2, lambda s: (self.grad(p, at.c, 1 - at.y, s), self.one(corner, p, 0, s)))
        self.start(p, 6, self.grad(p, at.c, 1 - at.y, 0, 2), self.half(self.cross[p], p, 1, 0), at.yn)

    def corner_b(self, p):
        at, corner = self.at, self.corner[p]
        arrived(corner.at[1], self.rs.at[p, 3], at.yn)
        self.add(2, lambda s: (self.grad(p, at.cx, at.y, s + 2), self.one(corner, p, 1, s)))
        self.start(p, 7, self.grad(p, at.cx, at.y, 2, 2), self.half(self.cross[p], p, 0, 2), at.xn)

    def cross_sum(self, p):
        at, cross = self.at, self.cross[p]
        for n, (i, first) in ((4, (0, 0)), (7, (0, 2)), (5, (1, 2)), (6, (1, 0))):
            arrived(self.half(cross, p, i, first), self.rs.at[p, n], at.yn)

        def one(s):
            mine = self.grad(p, at.c, at.y, s)
            mine[...] = mine[...] + self.one(cross, p, 0, s)[...] + self.one(cross, p, 1, s)[...]

        loop(4, one)
        line = self.along[p]

        def mine(s):
            return self.grad(p, at.c, at.y, s)

        if p in self.direct:
            for n in (1, 2, 3):
                s = at.other(n)
                self.start(p, 7 + n, mine(s), line.at[at.z], at.zth(s), arrival=8 + at.z)
            return
        end = jnp.logical_not(at.mid)
        near = jnp.where(at.mid, at.z - at.step, at.z + at.step)
        self.start(p, 8, mine(near), line.at[0], at.zth(near), arrival=8)
        for n in (2, 3):
            self.start(p, 7 + n, mine(at.other(n)), line.at[n], at.zth(near), arrival=8 + n, when=end)

    def line_sum(self, p):
        at, line = self.at, self.along[p]
        if p in self.direct:
            return

        @pl.when(at.mid)
        def _():
            for n in (2, 3):
                arrived(line.at[n], self.rs.at[p, 8 + n], at.yn)
                mine = self.grad(p, at.c, at.y, at.other(n - 1))
                mine[...] = mine[...] + line[n]

        for n in (2, 3):
            s = at.other(n - 1)
            self.start(p, 9 + n, self.grad(p, at.c, at.y, s), line.at[1], at.zth(s), arrival=9, when=at.mid)

    def along_sum(self, p):
        at, line = self.at, self.along[p]
        total = self.grad(p, at.c, at.y, at.z)[...].astype(F32)
        for n in (1, 2, 3) if p in self.direct else (0, 1):
            s = at.other(n) if p in self.direct else n
            arrived(line.at[s], self.rs.at[p, 8 + s], at.yn)
            total = total + line[s].astype(F32)
        self.owned[p][...] = total
        wide = total.shape[1]
        self.squares[:, 0:wide] = self.squares[:, 0:wide] + jnp.sum(total * total, axis=0, keepdims=True)


class Total:
    def __init__(self, at, sends, mine, line, plane, sems):
        self.at, self.sends, self.mine, self.line, self.plane = at, sends, mine, line, plane
        self.line_s, self.line_r, self.plane_s, self.plane_r, self.back_s, self.back_r = sems
        self.rows = line.shape[1]
        self.cut = mine.shape[0] != self.rows

    def part(self, ref, z):
        return ref.at[pl.ds(pl.multiple_of(z * self.rows, 8), self.rows)] if self.cut else ref

    def start(self):
        at = self.at
        self.line[at.z] = self.part(self.mine, at.z)[...]
        for k in (1, 2, 3):
            to = lax.rem(at.z + k, 4)
            self.sends.start(
                self.part(self.mine, to), self.line.at[at.z], self.line_s.at[k - 1], self.line_r.at[at.z], at.zth(to)
            )

    def spread(self):
        at = self.at
        for k in (1, 2, 3):
            s = lax.rem(at.z + k, 4)
            arrived(self.line.at[s], self.line_r.at[s], at.yn)
        me = at.y * 4 + at.c
        self.plane[me] = self.line[0] + self.line[1] + self.line[2] + self.line[3]
        for k in range(1, 8):
            to = lax.rem(me + k, 8)
            peer = (lax.div(to, 4), at.z, lax.rem(to, 4))
            self.sends.start(self.plane.at[me], self.plane.at[me], self.plane_s.at[k - 1], self.plane_r.at[me], peer)

    def collect(self):
        at = self.at
        me = at.y * 4 + at.c
        for k in range(1, 8):
            s = lax.rem(me + k, 8)
            arrived(self.plane.at[s], self.plane_r.at[s], at.yn)
        value = self.plane[0]
        for s in range(1, 8):
            value = value + self.plane[s]
        return value

    def share(self, whole):
        at = self.at
        mine = self.part(whole, at.z)
        mine[...] = self.collect()
        for k in (1, 2, 3):
            self.sends.start(mine, mine, self.back_s.at[k - 1], self.back_r.at[at.z], at.zth(lax.rem(at.z + k, 4)))

    def finish(self, whole):
        for k in (1, 2, 3):
            s = lax.rem(self.at.z + k, 4)
            arrived(self.part(whole, s), self.back_r.at[s], self.at.yn)


def fold(value):
    return value[0:8] + value[8:16] + value[16:24] + value[24:32]


def back_segment(c, slot, first, is_big, index, qkv, weights_big, weights_trio, mixed, grads):
    size = BIG_SLOTS if is_big else TRIO_SLOTS
    rows = pl.ds(first, size)
    q01 = qkv[c, rows, 0:128]
    k01 = qkv[c, rows, 128:256]
    v01 = qkv[c, rows, 256:384]
    kq2 = swap_halves(qkv[c, rows, 384:512])
    v2 = qkv[c, rows, 512:640]
    g01 = mixed[rows, pl.ds(pl.multiple_of(c * 256, 256), 128)]
    g2 = mixed[rows, pl.ds(pl.multiple_of(c * 256 + 128, 128), 128)]
    low = lane_low(size)
    none = jnp.zeros((size, 128), BF)
    dq, dk, dv = [], [], []
    for h, (g, gs, q, k, v) in enumerate((
        (g01, jnp.where(low, g01, none), q01, k01, v01),
        (g01, jnp.where(low, none, g01), q01, k01, v01),
        (g2, g2, kq2, kq2, v2),
    )):
        if is_big:
            weights = weights_big[slot, h, index]
        else:
            weights = weights_trio[slot, h, index]
        wide = weights.astype(F32)
        product = wide * mm_nt(v, gs)
        scores = (product - wide * jnp.sum(product, axis=0, keepdims=True)).astype(BF)
        dq.append(mm_tn(scores, k))
        dk.append(mm(scores, q))
        dv.append(mm(weights, g))
    scale = HEAD_DIM**-0.5
    grads[c, rows, 0:128] = (jnp.where(low, dq[0], dq[1]) * scale).astype(BF)
    grads[c, rows, 128:256] = (jnp.where(low, dk[0], dk[1]) * scale).astype(BF)
    grads[c, rows, 256:384] = jnp.where(low, dv[0], dv[1]).astype(BF)
    grads[c, rows, 384:512] = (jnp.where(low, dq[2], dk[2]) * scale).astype(BF)
    grads[c, rows, 512:640] = dv[2].astype(BF)


def backward_kernel(
    wq_h, wo_h, w1_h, w2_h, x_h, mid_h, a1t_h, a2t_h, mixt_h, qkv_h, pbig_h, ptrio_h, act_h, slope_h, cot_h, cott_h, out_h,
    gains_in,
    own_q, own_o, own_1, own_2, total, square_total, land_out, land_in,
    ring, wo, gq, go, g1, g2, pq, po, p1, p2, nq, no, n1, n2, rq, ro, r1, r2, lq, lo, l1, l2,
    act, slope, cot, cott, a2t, a1t, mixt, mid, x, pbig, ptrio, gmix, grad, half, send, gains, small, summed, squares, sums_of, line, plane, square_tile, square_line, square_plane,
    ss, rs, hs, ring_s, p_s, ex_s, ex_r, in_s, in_r, *total_sems,
):
    at = Place()
    sends = Sends()
    reduce = Reduce(
        at, sends, (gq, go, g1, g2), (pq, po, p1, p2), (nq, no, n1, n2), (rq, ro, r1, r2), (lq, lo, l1, l2),
        (own_q, own_o, own_1, own_2), squares, BACKWARD_DIRECT, (ss, rs),
    )
    loads = {}
    waited = []

    def load(name, src, dst):
        copy = pltpu.make_async_copy(src, dst, hs.at[len(loads) + len(waited)])
        copy.start()
        loads[name] = copy

    groups = (2 * (1 - at.x) + 1 - at.core, at.cx, at.cs, at.c)
    uses = [(ref, c) for ref in (w2_h, w1_h, wq_h) for c in groups]
    ring_copies = {}

    def ring_start(u):
        if u < len(uses):
            src, c = uses[u]
            wide = src.shape[2]
            copy = pltpu.make_async_copy(src.at[c], ring.at[u % 3, :, pl.ds(0, wide)], ring_s.at[u])
            copy.start()
            ring_copies[u] = copy

    def loaded(*names):
        for name in names:
            if name in loads:
                loads.pop(name).wait()
                waited.append(name)

    sums = Total(at, sends, small, line, plane, total_sems[:6])
    square_sum = Total(at, sends, square_tile, square_line, square_plane, total_sems[6:])
    keep_out = pltpu.make_async_copy(out_h.at[at.z], land_out.at[at.z], ex_s.at[3])
    keep_in = pltpu.make_async_copy(send.at[at.z], land_in.at[at.z], in_s.at[3])

    def start():
        load("cott", cott_h, cott)
        for i in range(4):
            load(f"act{i}", act_h.at[groups[i]], act.at[groups[i]])
        for u in range(3):
            ring_start(u)
        load("cot", cot_h, cot)
        for i in range(4):
            load(f"slope{i}", slope_h.at[groups[i]], slope.at[groups[i]])
        load("a2t", a2t_h, a2t)
        load("mid", mid_h, mid)
        load("mixt", mixt_h, mixt)
        load("wo", wo_h, wo)
        load("a1t", a1t_h, a1t)
        load("x", x_h, x)
        at_enter(at)
        squares[...] = jnp.zeros((1, D), F32)
        for n in (0, 1):
            gains[n : n + 1, :] = jnp.concatenate([gains_in[6 * n + i : 6 * n + i + 1, :] for i in range(6)], axis=1)

    def send_out():
        keep_out.start()
        exchange_start(at, sends, out_h, land_out, ex_s, ex_r)

    def grad_fc2(i):
        c = groups[i]
        loaded("cott", f"act{i}")

        def tile(n):
            lanes = pl.ds(pl.multiple_of(n * 256, 256), 256)
            g2[c, :, lanes] = mm(cott[...], act[c, :, lanes]).astype(BF)

        loop(3, tile)

    def grad_hidden(i):
        c = groups[i]
        loaded("cot", f"slope{i}")
        ring_copies[i].wait()

        def tile(n):
            lanes = pl.ds(pl.multiple_of(n * 256, 256), 256)
            slope[c, :, lanes] = (mm(cot[...], ring[i % 3, :, lanes]) * slope[c, :, lanes].astype(F32)).astype(BF)

        loop(3, tile)
        ring_start(i + 3)

    def rows_to_shards(dst, c, lanes, tile):
        for z in range(4):
            for y in range(2):
                first = (z * 2 + y) * 96
                dst[c, y, z, :, lanes] = tile[first : first + 96].astype(BF)

    def grad_fc1(i):
        c = groups[i]
        loaded("a2t")

        def tile(n):
            lanes = pl.ds(pl.multiple_of(n * 256, 256), 256)
            value = mm(a2t[...], slope[c, :, lanes])
            rows_to_shards(g1, c, lanes, value)
            sums_of[c, :, lanes] = value[768:769]

        loop(3, tile)

    def back_through(first_use, left, wide, i):
        u = first_use + i
        ring_copies[u].wait()

        part = mm_nt(left[groups[i], :, 0:wide], ring[u % 3, :, 0:wide])
        if i == 0:
            grad[...] = part
        else:
            grad[...] = grad[...] + part
        ring_start(u + 3)

    def put_row(first, value):
        for i in range(6):
            small[first + i : first + i + 1, :] = value[:, i * 128 : i * 128 + 128]

    def norm_two():
        loaded("mid")
        parts = [jnp.zeros((8, D), F32)] * 4

        def one(i, rows):
            normed, inverse = row_stats(mid[rows, :])
            upper = grad[rows, :]
            weighted = upper * gains[1:2, :]
            first = jnp.sum(weighted, axis=1, keepdims=True) * (1.0 / D)
            second = jnp.sum(weighted * normed, axis=1, keepdims=True) * (1.0 / D)
            straight = cot[rows, :].astype(F32)
            value = straight + inverse * (weighted - first - normed * second)
            mid[rows, :] = value
            branch = value.astype(BF)
            for r in range(4):
                half[r, rows, :] = branch[:, r * 192 : r * 192 + 192]
            for n, v in enumerate((upper * normed, upper, branch.astype(F32), straight)):
                parts[n] = parts[n] + fold(v)

        chunks(one)
        for first, value in zip((6, 18, 36, 42), parts):
            put_row(first, jnp.sum(value, axis=0, keepdims=True))

    def grad_out():
        loaded("mixt")

        def one(z):
            value = mm(mixt[...], half[z]).astype(BF)
            for c in range(4):
                for y in range(2):
                    go[c, y, z] = value[c * 256 + y * 96 : c * 256 + y * 96 + 96]

        loop(4, one)

    def grad_mixed():
        load("qkv", qkv_h, slope.at[:, :, pl.ds(0, QW)])
        loaded("wo")

        def one(c):
            rows = pl.ds(pl.multiple_of(c * 256, 256), 256)
            value = mm_nt(half[0], wo[0, rows, :])
            for z in (1, 2, 3):
                value = value + mm_nt(half[z], wo[z, rows, :])
            gmix[:, rows] = value.astype(BF)

        loop(4, one)
        for copy in fetch(0):
            copy.start()
        loaded("qkv")

    def fetch(i):
        c, slot = groups[i], i % 2
        return (
            pltpu.make_async_copy(pbig_h.at[c], pbig.at[slot], p_s.at[slot, 0]),
            pltpu.make_async_copy(ptrio_h.at[c], ptrio.at[slot], p_s.at[slot, 1]),
        )

    def attend_back(i):
        for copy in fetch(i):
            copy.wait()
        if i < 3:
            for copy in fetch(i + 1):
                copy.start()
        c = groups[i]
        act[c, SLOTS - 16 : SLOTS, 0:QW] = jnp.zeros((16, QW), BF)
        segments(
            at, lambda first, is_big, n: back_segment(c, i % 2, first, is_big, n, slope, pbig, ptrio, gmix, act)
        )

    def grad_q(i):
        c = groups[i]
        loaded("a1t")

        def tile(lanes):
            value = mm(a1t[...], act[c, :, lanes])
            rows_to_shards(gq, c, lanes, value)
            sums_of[4 + c, :, lanes] = value[768:769]

        loop(2, lambda n: tile(pl.ds(pl.multiple_of(n * 256, 256), 256)))
        tile(pl.ds(512, 128))

    def norm_one():
        loaded("x")
        parts = [jnp.zeros((8, D), F32)] * 2

        def one(i, rows):
            normed, inverse = row_stats(x[rows, :].astype(F32))
            upper = grad[rows, :]
            weighted = upper * gains[0:1, :]
            first = jnp.sum(weighted, axis=1, keepdims=True) * (1.0 / D)
            second = jnp.sum(weighted * normed, axis=1, keepdims=True) * (1.0 / D)
            value = (mid[rows, :] + inverse * (weighted - first - normed * second)).astype(BF)
            for r in range(4):
                put_block(send, r, i, value[:, r * 192 : r * 192 + 192])
            for n, v in enumerate((upper * normed, upper)):
                parts[n] = parts[n] + fold(v)

        chunks(one)
        for first, value in zip((0, 12), parts):
            put_row(first, jnp.sum(value, axis=0, keepdims=True))

    def send_in():
        exchange_start(at, sends, send, land_in, in_s, in_r)
        keep_in.start()

    def start_total():
        for c in range(4):
            put_row(48 + 6 * c, sums_of[c])
        packed = [sums_of[4 + c] for c in range(4)]
        for first, lanes in ((24, (0, 384)), (30, (256, 512))):
            parts = []
            for value in packed:
                parts += [value[:, lanes[0] : lanes[0] + 128], value[:, lanes[1] : lanes[1] + HALF]]
            put_row(first, jnp.concatenate(parts, axis=1))
        small[72:96, :] = jnp.zeros((24, 128), F32)
        sums.start()

    def finish_total():
        sums.finish(summed)
        total[...] = summed[...]

    def start_squares():
        value = squares[:, 0:128]
        for i in range(1, 6):
            value = value + squares[:, i * 128 : i * 128 + 128]
        square_tile[...] = jnp.zeros((8, 128), F32)
        square_tile[0:1, :] = value
        square_sum.start()

    def finish_squares():
        square_total[...] = square_sum.collect()

    def wait_exchanges():
        exchange_wait(at, land_out, ex_r)
        exchange_wait(at, land_in, in_r)
        keep_out.wait()
        keep_in.wait()

    steps = [start, send_out, norm_two, grad_out, grad_mixed, norm_one, send_in, start_total, sums.spread]
    steps += [lambda: sums.share(summed), finish_total, start_squares, square_sum.spread, finish_squares, wait_exchanges]
    through_fc1 = functools.partial(back_through, 4, slope, 768)
    through_q = functools.partial(back_through, 8, act, QW)
    for step in (grad_fc2, grad_hidden, grad_fc1, through_fc1, attend_back, grad_q, through_q):
        steps += [functools.partial(step, i) for i in range(4)]
    for p in (WQ, WO, W1, W2):
        steps += [functools.partial(reduce.pair_send, p, 0), functools.partial(reduce.pair_send, p, 1)]
        for step in (
            reduce.far_sum, reduce.near_sum, reduce.corner_a, reduce.corner_b, reduce.cross_sum, reduce.line_sum, reduce.along_sum
        ):
            steps.append(functools.partial(step, p))
    for number in BACKWARD_ORDER:
        steps[number]()
    sends.drain()


def at_enter(at):
    barrier = pltpu.get_barrier_semaphore()
    me = at.y * 4 + at.c
    peers = [at.zth(lax.rem(at.z + k, 4)) for k in (1, 2, 3)]
    for k in range(1, 8):
        to = lax.rem(me + k, 8)
        peers.append((lax.div(to, 4), at.z, lax.rem(to, 4)))
    for peer in peers:
        pl.semaphore_signal(barrier, inc=1, device_id=peer, device_id_type=MESH)
    pl.semaphore_wait(barrier, len(peers))


SHARDS = ((96, QW), (96, 192), (96, 768), (192, 384))


def run_backward(*operands):
    sem = pltpu.SemaphoreType.DMA
    vmem = pltpu.VMEM
    shape = jax.ShapeDtypeStruct
    stages = [(4, 2, 4), (2, 2, 4), (2, 2), (2, 4), (4,)]
    matrices = [(4, 768, 768), (2, 768, 768), (2, 384, 384), (2, 768, 384), (4, 192, 384)]
    return pl.pallas_call(
        backward_kernel,
        out_shape=[shape(s, F32) for s in SHARDS] + [shape((96, 128), F32), shape((8, 128), F32)] + [shape((4, BLOCK, 128), BF)] * 2,
        in_specs=[pl.BlockSpec(memory_space=pl.ANY)] * (len(operands) - 1) + [pl.BlockSpec(memory_space=vmem)],
        out_specs=[pl.BlockSpec(memory_space=vmem)] * 6 + [pl.BlockSpec(memory_space=pl.ANY)] * 2,
        scratch_shapes=[vmem((3, 768, 768), BF), vmem((4, 1024, 192), BF)]
        + [
            vmem(whole if s == SHARDS[W2] else lead + s, BF) for lead, whole in zip(stages, matrices) for s in SHARDS
        ]
        + [
            vmem((4, SLOTS, 768), BF), vmem((4, SLOTS, 768), BF), vmem((SLOTS, D), BF), vmem((D, SLOTS), BF),
            vmem((784, SLOTS), BF), vmem((784, SLOTS), BF), vmem((1024, SLOTS), BF), vmem((SLOTS, D), F32),
            vmem((SLOTS, D), BF), vmem((2, 3, 2, BIG_SLOTS, BIG_SLOTS), BF), vmem((2, 3, 3, TRIO_SLOTS, TRIO_SLOTS), BF),
            vmem((SLOTS, 1024), BF), vmem((SLOTS, D), F32), vmem((4, SLOTS, 192), BF), vmem((4, BLOCK, 128), BF),
            vmem((2, D), F32), vmem((96, 128), F32), vmem((96, 128), F32), vmem((1, D), F32), vmem((8, 1, D), F32),
            vmem((4, 24, 128), F32), vmem((8, 24, 128), F32), vmem((8, 128), F32), vmem((4, 8, 128), F32), vmem((8, 8, 128), F32),
            sem((4, 13)), sem((4, 13)), sem((18,)), sem((12,)), sem((2, 2)), sem((4,)), sem((4,)), sem((4,)), sem((4,)),
        ]
        + [sem((n,)) for n in (3, 4, 7, 8, 3, 4)] * 2,
        compiler_params=pltpu.CompilerParams(collective_id=1, has_side_effects=True, vmem_limit_bytes=VMEM_LIMIT),
    )(*operands)


BACKWARD_ORDER = (
    0, 1, 15, 70, 16, 17, 72, 18, 71, 19, 20, 21, 73, 24, 23, 22, 75, 74, 25, 61, 27, 28, 63, 62, 26, 29, 30, 2, 64,
    3, 4, 76, 66, 53, 31, 65, 77, 32, 36, 55, 33, 67, 52, 68, 35, 39, 54, 34, 57, 56, 43, 40, 41, 42, 45, 58, 5, 6,
    59, 78, 37, 44, 38, 48, 69, 46, 7, 47, 49, 60, 50, 8, 51, 11, 9, 12, 10, 13, 14,
)
BACKWARD_DIRECT = ()


RATES = (D**-0.5, (D // 24) ** -0.5, D**-0.5, FF**-0.5, 0.3, 0.3)
ROWS = 208


def update_kernel(
    own_q, own_o, own_1, own_2, total, square_total, land_out, land_in, where,
    wq, wo, w1, w2, wg, wb, mq, mo, m1, m2, mg, mb, vq, vo, v1, v2, vg, vb,
    out, grad_in, norm,
    nmq, nvq, nwq, hq, nmo, nvo, nwo, ho, nm1, nv1, nw1, h1, nm2, nv2, nw2, h2, nmg, nvg, nwg, hg, nmb, nvb, nwb, hb,
    blocks,
):
    gains = total[0:12, :]
    biases = total[12:72, :]
    squares = jnp.sum(jnp.sum(square_total[...], axis=0, keepdims=True), axis=1, keepdims=True)
    for part in (gains, biases):
        squares = squares + jnp.sum(jnp.sum(part * part, axis=0, keepdims=True), axis=1, keepdims=True)
    size = jnp.sqrt(squares)
    norm[...] = size
    factor = jnp.minimum(1.0, CLIP_NORM / size)

    def step(rate, grad, pick, refs):
        weight, first, second, new_first, new_second, new_weight, half = refs
        results = adam_step(weight[pick], grad, first[pick], second[pick], rate, factor)
        for ref, value in zip((new_first, new_second, new_weight, half), results):
            ref[pick] = value

    everything = (slice(None), slice(None))
    packed = own_q[...]
    for n in range(3):
        grad = jnp.concatenate([packed[:, 128 * n : 128 * n + 128], packed[:, 384 + HALF * n : 448 + HALF * n]], axis=1)
        step(RATES[0], grad, n, (wq, mq, vq, nmq, nvq, nwq, hq))
    step(RATES[1], own_o[...], everything, (wo, mo, vo, nmo, nvo, nwo, ho))
    step(RATES[2], own_1[...], everything, (w1, m1, v1, nm1, nv1, nw1, h1))
    step(RATES[3], own_2[...], everything, (w2, m2, v2, nm2, nv2, nw2, h2))
    step(RATES[4], gains, everything, (wg, mg, vg, nmg, nvg, nwg, hg))
    step(RATES[5], biases, everything, (wb, mb, vb, nmb, nvb, nwb, hb))

    pairs = out.shape[0]
    for n, land in enumerate((land_out, land_in)):
        for r in range(4):
            for i in range(SLOTS // CHUNK):
                rows = slice(r * SLOTS + i * CHUNK, r * SLOTS + i * CHUNK + CHUNK)
                rest = land[r, SLOTS + i * 16 : SLOTS + i * 16 + 16, :]
                blocks[rows, n * 192 : n * 192 + 128] = land[r, i * CHUNK : i * CHUNK + CHUNK, :]
                blocks[rows, n * 192 + 128 : n * 192 + 192] = jnp.concatenate([rest[:, 0:HALF], rest[:, HALF:]], axis=0)
    for first in range(0, pairs, ROWS):
        count = min(ROWS, pairs - first)
        halves = []
        for half in (0, 1):
            token = half * TOK + first + lax.broadcasted_iota(jnp.int32, (ROWS, SLOTS), 0)
            one = jnp.concatenate([(token == where[r]).astype(F32).astype(BF) for r in range(4)], axis=1)
            halves.append(mm(one, blocks[...])[0:count])
        for ref, lanes in ((out, 0), (grad_in, 192)):
            even, odd = (value[:, lanes : lanes + 192] for value in halves)
            ref[first : first + count, 0, :] = jnp.concatenate([even, odd], axis=1)


def run_update(pairs, *operands):
    shape = jax.ShapeDtypeStruct
    shapes = [shape((pairs, 1, 384), F32)] * 2 + [shape((1, 1), F32)]
    for weight in operands[9:15]:
        shapes += [shape(weight.shape, F32)] * 3 + [shape(weight.shape, BF)]
    return pl.pallas_call(
        update_kernel,
        out_shape=shapes,
        in_specs=[pl.BlockSpec(memory_space=pltpu.VMEM)] * len(operands),
        out_specs=[pl.BlockSpec(memory_space=pltpu.VMEM)] * len(shapes),
        scratch_shapes=[pltpu.VMEM((4 * SLOTS, 384), BF)],
        compiler_params=pltpu.CompilerParams(vmem_limit_bytes=VMEM_LIMIT),
    )(*operands)


def prepare(layer_in, grad_out, crop_ids, w_qkv, w_out, w_fc1, w_fc2, norm_gains, all_biases):
    pairs = layer_in.shape[0]
    return (
        layer_in.reshape(pairs, 384), grad_out.reshape(pairs, 384), crop_ids.reshape(-1, IMAGE_LEN),
        w_qkv.transpose(1, 0, 2), w_out, w_fc1, w_fc2.T, norm_gains.reshape(12, 128), all_biases.reshape(60, 128),
    )


def local_fast(
    layer_in, grad_out, crop_ids, w_qkv, w_out, w_fc1, w_fc2, norm_gains, all_biases,
    first_qkv, second_qkv, first_out, second_out, first_fc1, second_fc1, first_fc2, second_fc2,
    first_gains, second_gains, first_biases, second_biases,
):
    pairs = layer_in.shape[0]
    operands = prepare(layer_in, grad_out, crop_ids, w_qkv, w_out, w_fc1, w_fc2, norm_gains, all_biases)
    *kept, where = run_forward(*operands)
    reduced = run_backward(*kept, operands[7])
    masters = operands[3:9]
    results = run_update(
        pairs, *reduced, where, *masters,
        first_qkv.transpose(1, 0, 2), first_out, first_fc1, first_fc2.T,
        first_gains.reshape(12, 128), first_biases.reshape(60, 128),
        second_qkv.transpose(1, 0, 2), second_out, second_fc1, second_fc2.T,
        second_gains.reshape(12, 128), second_biases.reshape(60, 128),
    )
    return (
        results[0], results[1], results[2].reshape(()),
        *[v.transpose(1, 0, 2) for v in results[3:7]], *results[7:15], *[v.T for v in results[15:19]],
        *[v.reshape(-1) for v in results[19:27]],
    )


def dot(a, b):
    return jnp.dot(a, b, preferred_element_type=F32)


def dot_nt(a, b):
    return lax.dot_general(a, b, (((1,), (1,)), ((), ())), preferred_element_type=F32)


def dot_tn(a, b):
    return lax.dot_general(a, b, (((0,), (0,)), ((), ())), preferred_element_type=F32)


def norm_stats(value):
    centre = jnp.mean(value, axis=1, keepdims=True)
    centred = value - centre
    spread = jnp.mean(centred * centred, axis=1, keepdims=True)
    inverse = lax.rsqrt(spread + NORM_EPS)
    return centred * inverse, inverse


def norm_back(grad, normed, inverse, gain):
    weighted = grad * gain
    first = jnp.mean(weighted, axis=1, keepdims=True)
    second = jnp.mean(weighted * normed, axis=1, keepdims=True)
    return inverse * (weighted - first - normed * second)


def layer(x, cot, crops, w_qkv, w_out, w_fc1, w_fc2, gains, biases):
    inputs = x.astype(F32)
    cotf = cot.astype(F32)
    normed_one, inverse_one = norm_stats(inputs)
    act_one = (normed_one * gains[:D] + biases[:D]).astype(BF)
    qkv_bias = jnp.concatenate([biases[2 * D : 3 * D], jnp.zeros((D,), F32), biases[3 * D : 4 * D]])
    qkv = (dot(act_one, w_qkv) + qkv_bias).astype(BF)
    heads = qkv.reshape(SLOTS, 3, HEADS, HEAD_DIM)
    q, k, v = heads[:, 0], heads[:, 1], heads[:, 2]
    scores = jnp.einsum("qhd,khd->hqk", q, k, preferred_element_type=F32) * HEAD_DIM ** (-0.5)
    scores = jnp.where((crops[:, None] == crops[None, :])[None], scores, MASKED)
    probs = jax.nn.softmax(scores, axis=2)
    half_probs = probs.astype(BF)
    mixed = jnp.einsum("hqk,khd->qhd", half_probs, v, preferred_element_type=F32)
    mixed = mixed.reshape(SLOTS, D).astype(BF)
    middle = inputs + dot(mixed, w_out) + biases[4 * D : 5 * D]
    normed_two, inverse_two = norm_stats(middle)
    act_two = (normed_two * gains[D:] + biases[D : 2 * D]).astype(BF)
    hidden = dot(act_two, w_fc1) + biases[6 * D :]
    active, gelu_pull = jax.vjp(lambda h: jax.nn.gelu(h, approximate=False), hidden)
    active = active.astype(BF)
    out = middle + dot(active, w_fc2) + biases[5 * D : 6 * D]

    g_fc2 = dot_tn(active, cot)
    grad_hidden = gelu_pull(dot_nt(cot, w_fc2))[0].astype(BF)
    g_fc1 = dot_tn(act_two, grad_hidden)
    grad_two = dot_nt(grad_hidden, w_fc1)
    grad_middle = cotf + norm_back(grad_two, normed_two, inverse_two, gains[D:])
    branch = grad_middle.astype(BF)
    g_out = dot_tn(mixed, branch)
    grad_mixed = dot_nt(branch, w_out).astype(BF).reshape(SLOTS, HEADS, HEAD_DIM)
    grad_probs = jnp.einsum("qhd,khd->hqk", grad_mixed, v, preferred_element_type=F32)
    grad_scores = (probs * (grad_probs - jnp.sum(probs * grad_probs, axis=2, keepdims=True))).astype(BF)
    scale = HEAD_DIM ** (-0.5)
    grad_q = jnp.einsum("hqk,khd->qhd", grad_scores, k, preferred_element_type=F32) * scale
    grad_k = jnp.einsum("hqk,qhd->khd", grad_scores, q, preferred_element_type=F32) * scale
    grad_v = jnp.einsum("hqk,qhd->khd", half_probs, grad_mixed, preferred_element_type=F32)
    grad_qkv = jnp.stack([grad_q, grad_k, grad_v], axis=1).astype(BF).reshape(SLOTS, 3 * D)
    g_qkv = dot_tn(act_one, grad_qkv)
    grad_one = dot_nt(grad_qkv, w_qkv)
    grad_in = grad_middle + norm_back(grad_one, normed_one, inverse_one, gains[:D])

    g_gains = jnp.concatenate([jnp.sum(grad_one * normed_one, axis=0), jnp.sum(grad_two * normed_two, axis=0)])
    qkv_sums = jnp.sum(grad_qkv.astype(F32), axis=0)
    g_biases = jnp.concatenate([
        jnp.sum(grad_one, axis=0),
        jnp.sum(grad_two, axis=0),
        qkv_sums[:D],
        qkv_sums[2 * D :],
        jnp.sum(branch.astype(F32), axis=0),
        jnp.sum(cotf, axis=0),
        jnp.sum(grad_hidden.astype(F32), axis=0),
    ])
    return out, grad_in, g_qkv, g_out, g_fc1, g_fc2, g_gains, g_biases


def adam_step(weight, grad, first, second, rate, factor):
    clipped = grad * factor
    new_first = BETA_ONE * first + (1.0 - BETA_ONE) * clipped
    new_second = BETA_TWO * second + (1.0 - BETA_TWO) * clipped * clipped
    unbiased_first = new_first / (1.0 - BETA_ONE**STEP)
    unbiased_second = new_second / (1.0 - BETA_TWO**STEP)
    new_weight = weight - rate * (
        unbiased_first / (jnp.sqrt(unbiased_second) + ADAM_EPS) + DECAY * weight
    )
    return (new_first, new_second, new_weight, new_weight.astype(BF))


def gather(value, axes):
    for name, dim in axes:
        value = lax.all_gather(value, name, axis=dim, tiled=True)
    return value


def scatter(value, axes):
    for name, dim in axes:
        value = lax.psum_scatter(value, name, scatter_dimension=dim, tiled=True)
    return value.astype(F32)


def local_plain(
    layer_in, grad_out, crop_ids, w_qkv, w_out, w_fc1, w_fc2, norm_gains, all_biases,
    first_qkv, second_qkv, first_out, second_out, first_fc1, second_fc1, first_fc2, second_fc2,
    first_gains, second_gains, first_biases, second_biases,
):
    row = lax.axis_index("row")
    n_row, n_col = lax.axis_size("row"), lax.axis_size("col")
    feat = D // n_row
    pairs = layer_in.shape[0]
    labels = lax.ppermute(
        crop_ids, ("row", "col"), [(r * n_col + c, c * n_row + r) for r in range(n_row) for c in range(n_col)]
    )
    sources = slot_sources(labels).reshape(-1)
    place = jnp.where(sources < 0, -1, (sources % 2) * pairs + sources // 2)
    pick = (place[:, None] == jnp.arange(2 * pairs, dtype=jnp.int32)[None, :]).astype(BF)

    def to_slots(value):
        halves = jnp.concatenate([value[:, 0, :feat], value[:, 0, feat:]], axis=0)
        sent = dot(pick, halves).astype(BF)
        got = lax.all_to_all(sent, "row", 0, 0, tiled=True)
        return got.reshape(n_row, SLOTS, feat).transpose(1, 0, 2).reshape(SLOTS, D)

    def to_tokens(value):
        sent = value.astype(BF).reshape(SLOTS, n_row, feat).transpose(1, 0, 2).reshape(n_row * SLOTS, feat)
        got = lax.all_to_all(sent, "row", 0, 0, tiled=True)
        halves = dot_tn(pick, got)
        return jnp.concatenate([halves[:pairs], halves[pairs:]], axis=1).reshape(pairs, 1, 2 * feat)

    full_qkv = gather(w_qkv.astype(BF), (("dp", 0), ("row", 0), ("col", 2))).reshape(D, 3 * D)
    full_out = gather(w_out.astype(BF), (("dp", 0), ("col", 0), ("row", 1)))
    full_fc1 = gather(w_fc1.astype(BF), (("dp", 0), ("row", 0), ("col", 1)))
    full_fc2 = gather(w_fc2.astype(BF), (("dp", 0), ("col", 0), ("row", 1)))
    crops = jnp.where(row < 2, slot_crops(0), slot_crops(1))
    out, grad_in, g_qkv, g_out, g_fc1, g_fc2, g_gains, g_biases = layer(
        to_slots(layer_in), to_slots(grad_out), crops, full_qkv, full_out, full_fc1, full_fc2, norm_gains, all_biases
    )
    owned_qkv = scatter(g_qkv.astype(BF).reshape(D, 3, D), (("col", 2), ("row", 0), ("dp", 0)))
    owned_out = scatter(g_out.astype(BF), (("row", 1), ("col", 0), ("dp", 0)))
    owned_fc1 = scatter(g_fc1.astype(BF), (("col", 1), ("row", 0), ("dp", 0)))
    owned_fc2 = scatter(g_fc2.astype(BF), (("row", 1), ("col", 0), ("dp", 0)))
    local_squares = (
        jnp.sum(owned_qkv * owned_qkv)
        + jnp.sum(owned_out * owned_out)
        + jnp.sum(owned_fc1 * owned_fc1)
        + jnp.sum(owned_fc2 * owned_fc2)
    )
    grad_gains, grad_biases, weight_squares = lax.psum((g_gains, g_biases, local_squares), ("dp", "row", "col"))
    grad_norm = jnp.sqrt(weight_squares + jnp.sum(grad_gains * grad_gains) + jnp.sum(grad_biases * grad_biases))
    factor = jnp.minimum(1.0, CLIP_NORM / grad_norm)
    upd_qkv = adam_step(w_qkv, owned_qkv, first_qkv, second_qkv, D ** (-0.5), factor)
    upd_out = adam_step(w_out, owned_out, first_out, second_out, (D // 24) ** (-0.5), factor)
    upd_fc1 = adam_step(w_fc1, owned_fc1, first_fc1, second_fc1, D ** (-0.5), factor)
    upd_fc2 = adam_step(w_fc2, owned_fc2, first_fc2, second_fc2, FF ** (-0.5), factor)
    upd_gains = adam_step(norm_gains, grad_gains, first_gains, second_gains, 0.3, factor)
    upd_biases = adam_step(all_biases, grad_biases, first_biases, second_biases, 0.3, factor)
    return (
        to_tokens(out), to_tokens(grad_in), grad_norm,
        *upd_qkv, *upd_out, *upd_fc1, *upd_fc2, *upd_gains, *upd_biases,
    )


def solution(mesh):
    tokens = P(("dp", "col"), "row", None)
    qkv = P(("row", "dp"), None, "col")
    out = P(("col", "dp"), "row")
    fc1 = P(("row", "dp"), "col")
    whole = P()
    return jax.shard_map(
        local_fast if mesh.shape["dp"] == 2 else local_plain,
        mesh=mesh,
        in_specs=(
            tokens, tokens, P(("dp", "row")), qkv, out, fc1, out, whole, whole,
            qkv, qkv, out, out, fc1, fc1, out, out, whole, whole, whole, whole,
        ),
        out_specs=(tokens, tokens, whole) + (qkv,) * 4 + (out,) * 4 + (fc1,) * 4 + (out,) * 4 + (whole,) * 8,
        check_vma=False,
    )
```

```python
import functools

import jax
import jax.numpy as jnp
from jax import lax
from jax.experimental import pallas as pl
from jax.experimental.pallas import tpu as pltpu
from jax.sharding import PartitionSpec as P

HEADS = 12
HEAD_DIM = 64
FF = 3072
D = 768
BIG_CROP = 197
SMALL_CROP = 37
IMAGE_LEN = 690
CROPS = 10
STEP = 5

NORM_EPS = 1e-06
CLIP_NORM = 1.0
BETA_ONE = 0.5
BETA_TWO = 0.5
ADAM_EPS = 1e-08
DECAY = 0.05
MASKED = -1e30

SLOTS = 544
BIG_SLOTS = 208
TRIO_SLOTS = 112
TRIO = 3 * SMALL_CROP
BF = jnp.bfloat16
F32 = jnp.float32


def crop_starts(labels):
    images = labels.shape[0] // IMAGE_LEN
    places = labels.reshape(images, IMAGE_LEN) % CROPS
    order = jnp.arange(CROPS, dtype=jnp.int32)
    sizes = jnp.sum((places[:, :, None] == order).astype(jnp.int32), axis=1)
    starts = jnp.sum((places[:, :, None] < order).astype(jnp.int32), axis=1)
    starts = starts + IMAGE_LEN * jnp.arange(images, dtype=jnp.int32)[:, None]
    big = (sizes == BIG_CROP).astype(jnp.int32)
    earlier = (order[:, None] < order[None, :]).astype(jnp.int32)
    big_rank = jnp.sum(big[:, :, None] * earlier, axis=1)
    small_rank = jnp.sum((1 - big)[:, :, None] * earlier, axis=1)

    def ranked(flag, rank, count):
        hit = flag[:, :, None] * (rank[:, :, None] == jnp.arange(count, dtype=jnp.int32)).astype(jnp.int32)
        return jnp.sum(hit * starts[:, :, None], axis=1).reshape(-1)

    return ranked(big, big_rank, 2), ranked(1 - big, small_rank, CROPS - 2)


def slot_segments(kind):
    if kind == 0:
        bigs, trios = 2, 1
    else:
        bigs, trios = 1, 3
    parts = []
    at = 0
    for b in range(bigs):
        parts.append((at, BIG_CROP, True, b))
        at += BIG_SLOTS
    for s in range(3 * trios):
        parts.append((at + s // 3 * TRIO_SLOTS + s % 3 * SMALL_CROP, SMALL_CROP, False, s))
    return parts


def slot_sources(labels):
    big, small = crop_starts(labels)
    rows = []
    for row in range(4):
        kind = row // 2
        at_big = (0, 2, 4, 5)[row]
        at_small = (0, 3, 6, 15)[row]
        out = []
        filled = 0
        for first, length, is_big, index in slot_segments(kind):
            if first > filled:
                out.append(jnp.full((first - filled,), -1, jnp.int32))
            start = big[at_big + index] if is_big else small[at_small + index]
            out.append(start + jnp.arange(length, dtype=jnp.int32))
            filled = first + length
        if filled < SLOTS:
            out.append(jnp.full((SLOTS - filled,), -1, jnp.int32))
        rows.append(jnp.concatenate(out))
    return jnp.stack(rows)


def slot_crops(kind):
    slot = jnp.arange(SLOTS, dtype=jnp.int32)
    crop = jnp.full((SLOTS,), -1, jnp.int32)
    for number, (first, length, _, _) in enumerate(slot_segments(kind)):
        crop = jnp.where((slot >= first) & (slot < first + length), number, crop)
    return crop


MESH = pl.DeviceIdType.MESH
HALF = 64
QW = 640
TOK = 1040
CHUNK = 32
BLOCK = SLOTS + SLOTS // 2
WQ, WO, W1, W2 = 0, 1, 2, 3
VMEM_LIMIT = 60 * 2**20


def mm(a, b):
    return lax.dot_general(a, b, (((1,), (0,)), ((), ())), preferred_element_type=F32)


def mm_nt(a, b):
    return lax.dot_general(a, b, (((1,), (1,)), ((), ())), preferred_element_type=F32)


def mm_tn(a, b):
    return lax.dot_general(a, b, (((0,), (0,)), ((), ())), preferred_element_type=F32)


class Place:
    def __init__(self):
        self.y = lax.axis_index("dp")
        self.z = lax.axis_index("row")
        self.c = lax.axis_index("col")
        self.core = lax.rem(self.c, 2)
        self.x = lax.div(self.c, 2)
        self.cx = lax.rem(self.c + 2, 4)
        self.cs = self.c + 1 - 2 * self.core
        self.xn = (self.y, self.z, self.cx)
        self.yn = (1 - self.y, self.z, self.c)
        self.cn = (self.y, self.z, self.cs)
        self.low = self.z < 2
        self.mid = jnp.logical_or(self.z == 1, self.z == 2)
        self.step = jnp.where(self.low, 1, -1)

    def zth(self, z):
        return (self.y, z, self.c)

    def other(self, j):
        return lax.rem(self.z + self.step * j + 4, 4)

    def enter(self):
        barrier = pltpu.get_barrier_semaphore()
        peers = [self.zth(lax.rem(self.z + k, 4)) for k in (1, 2, 3)] + [self.xn, self.yn, self.cn]
        for peer in peers:
            pl.semaphore_signal(barrier, inc=1, device_id=peer, device_id_type=MESH)
        pl.semaphore_wait(barrier, len(peers))


def shard_of(refs, p, c, s, y):
    ref = refs[p]
    if p == WO:
        return ref.at[s, c, pl.ds(pl.multiple_of(y * 96, 32), 96), :]
    if p == W2:
        return ref.at[c, s, :, pl.ds(pl.multiple_of(y * 384, 128), 384)]
    return ref.at[c, s, y]


def group_of(refs, p, c, y):
    ref = refs[p]
    if p == WO:
        return ref.at[:, c, pl.ds(pl.multiple_of(y * 96, 32), 96), :]
    if p == W2:
        return ref.at[c, :, :, pl.ds(pl.multiple_of(y * 384, 128), 384)]
    return ref.at[c, :, y]


class Sends:
    def __init__(self):
        self.left = []

    def start(self, src, dst, send_sem, recv_sem, peer, when=None):
        copy = pltpu.make_async_remote_copy(
            src_ref=src, dst_ref=dst, send_sem=send_sem, recv_sem=recv_sem, device_id=peer, device_id_type=MESH
        )
        if when is None:
            copy.start()
        else:
            pl.when(when)(copy.start)
        self.left.append((copy, when))

    def drain(self):
        for copy, when in self.left:
            if when is None:
                copy.wait_send()
            else:
                pl.when(when)(copy.wait_send)
        self.left = []


def arrived(ref, sem, me):
    pltpu.make_async_remote_copy(
        src_ref=ref, dst_ref=ref, send_sem=sem, recv_sem=sem, device_id=me, device_id_type=MESH
    ).wait_recv()


class Gather:
    def __init__(self, at, refs, sends, direct, zs, zr, xs, xr, ys, yr, ds, dr, cs, cr):
        self.at, self.refs, self.sends, self.direct = at, refs, sends, direct
        self.zs, self.zr, self.xs, self.xr = zs, zr, xs, xr
        self.ys, self.yr, self.ds, self.dr, self.cs, self.cr = ys, yr, ds, dr, cs, cr

    def across(self, p, s):
        at = self.at
        own = shard_of(self.refs, p, at.c, s, at.y)
        self.sends.start(own, own, self.xs.at[p, s], self.xr.at[p, s], at.xn)
        self.sends.start(own, own, self.ys.at[p, s], self.yr.at[p, s], at.yn)

    def own_across(self, p):
        self.across(p, self.at.z)

    def own_along(self, p):
        at = self.at
        own = shard_of(self.refs, p, at.c, at.z, at.y)
        if p in self.direct:
            for j in (1, 2, 3):
                self.sends.start(own, own, self.zs.at[p, j - 1], self.zr.at[p, at.z], at.zth(at.other(j)))
            return
        second = jnp.where(at.mid, at.z - at.step, at.z + 2 * at.step)
        self.sends.start(own, own, self.zs.at[p, 0], self.zr.at[p, at.z], at.zth(at.z + at.step))
        self.sends.start(own, own, self.zs.at[p, 1], self.zr.at[p, at.z], at.zth(second))

    def to_core(self, p, g, c, y):
        ref = group_of(self.refs, p, c, y)
        self.sends.start(ref, ref, self.cs.at[p, g], self.cr.at[p, g], self.at.cn)

    def along(self, p, j):
        at = self.at
        s = at.other(j)
        ref = shard_of(self.refs, p, at.c, s, at.y)
        arrived(ref, self.zr.at[p, s], at.yn)
        if j < 3 and p not in self.direct:
            self.sends.start(ref, ref, self.zs.at[p, 1 + j], self.zr.at[p, s], at.zth(at.z - at.step), when=at.mid)
        self.across(p, s)
        if j == 3:
            self.to_core(p, 0, at.c, at.y)

    def cross(self, p, j):
        at = self.at
        s = at.other(j)
        from_x = shard_of(self.refs, p, at.cx, s, at.y)
        from_y = shard_of(self.refs, p, at.c, s, 1 - at.y)
        arrived(from_x, self.xr.at[p, s], at.yn)
        arrived(from_y, self.yr.at[p, s], at.yn)
        if j < 2:
            self.sends.start(from_x, from_x, self.ds.at[p, j], self.dr.at[p, s], at.yn)
        else:
            self.sends.start(from_y, from_y, self.ds.at[p, j], self.dr.at[p, s], at.xn)
        if j == 3:
            self.to_core(p, 1, at.cx, at.y)
            self.to_core(p, 2, at.c, 1 - at.y)

    def corner(self, p):
        at = self.at
        for j in (0, 1, 2, 3):
            s = at.other(j)
            arrived(shard_of(self.refs, p, at.cx, s, 1 - at.y), self.dr.at[p, s], at.yn)
        self.to_core(p, 3, at.cx, 1 - at.y)

    def ready(self, p, half):
        at = self.at
        c = at.cs if half == 0 else at.cs + 2 - 4 * at.x
        arrived(group_of(self.refs, p, c, at.y), self.cr.at[p, half], at.yn)
        arrived(group_of(self.refs, p, c, 1 - at.y), self.cr.at[p, 2 + half], at.yn)


def exchange_start(at, sends, blocks, landing, send_sems, recv_sems):
    for k in (1, 2, 3):
        to = lax.rem(at.z + k, 4)
        sends.start(blocks.at[to], landing.at[at.z], send_sems.at[k - 1], recv_sems.at[at.z], at.zth(to))


def exchange_wait(at, landing, recv_sems):
    for k in (1, 2, 3):
        s = lax.rem(at.z + k, 4)
        arrived(landing.at[s], recv_sems.at[s], at.yn)


def row_stats(value):
    centre = jnp.sum(value, axis=1, keepdims=True) * (1.0 / D)
    centred = value - centre
    spread = jnp.sum(centred * centred, axis=1, keepdims=True) * (1.0 / D)
    inverse = lax.rsqrt(spread + NORM_EPS)
    return centred * inverse, inverse


def chunks(body):
    for i in range(SLOTS // CHUNK):
        body(i, slice(i * CHUNK, i * CHUNK + CHUNK))


def put_block(ref, r, i, value):
    ref[r, i * CHUNK : i * CHUNK + CHUNK, :] = value[:, 0:128]
    first = SLOTS + i * (CHUNK // 2)
    ref[r, first : first + CHUNK // 2, :] = jnp.concatenate([value[0:16, 128:192], value[16:32, 128:192]], axis=1)


def get_blocks(ref, i):
    parts = []
    first = SLOTS + i * (CHUNK // 2)
    for r in range(4):
        parts.append(ref[r, i * CHUNK : i * CHUNK + CHUNK, :])
        rest = ref[r, first : first + CHUNK // 2, :]
        parts.append(jnp.concatenate([rest[:, 0:HALF], rest[:, HALF:]], axis=0))
    return jnp.concatenate(parts, axis=1)


def loop(count, body):
    def step(i, carry):
        body(i)
        return carry

    lax.fori_loop(0, count, step, 0)


def lane_low(rows):
    return lax.broadcasted_iota(jnp.int32, (rows, 2 * HALF), 1) < HALF


def swap_halves(value):
    return jnp.concatenate([value[:, HALF:], value[:, :HALF]], axis=1)


def segments(at, body):
    for bigs in (2, 1):

        @pl.when(at.low if bigs == 2 else jnp.logical_not(at.low))
        def _():
            for i in range(bigs):
                body(i * BIG_SLOTS, True, i)
            for i in range(1 if bigs == 2 else 3):
                body(bigs * BIG_SLOTS + i * TRIO_SLOTS, False, i)


def key_mask(size, is_big):
    key = lax.broadcasted_iota(jnp.int32, (size, size), 0)
    if is_big:
        return key < BIG_CROP
    query = lax.broadcasted_iota(jnp.int32, (size, size), 1)

    def crop(v):
        return (v >= SMALL_CROP).astype(jnp.int32) + (v >= 2 * SMALL_CROP).astype(jnp.int32) + (v >= TRIO).astype(jnp.int32)

    return jnp.logical_and(crop(query) == crop(key), key < TRIO)


def attend_segment(c, first, is_big, index, qkv, mixed, pbig, ptrio):
    size = BIG_SLOTS if is_big else TRIO_SLOTS
    rows = pl.ds(first, size)
    q01 = qkv[c, rows, 0:128]
    k01 = qkv[c, rows, 128:256]
    v01 = qkv[c, rows, 256:384]
    qk2 = qkv[c, rows, 384:512]
    v2 = qkv[c, rows, 512:640]
    low = lane_low(size)
    none = jnp.zeros((size, 128), BF)
    mask = key_mask(size, is_big)
    outs = []
    for h, (q, k, v) in enumerate((
        (jnp.where(low, q01, none), k01, v01),
        (jnp.where(low, none, q01), k01, v01),
        (jnp.where(low, qk2, none), swap_halves(qk2), v2),
    )):
        scores = jnp.where(mask, mm_nt(k, q) * HEAD_DIM**-0.5, MASKED)
        weights = jnp.exp(scores - jnp.max(scores, axis=0, keepdims=True))
        total = jnp.sum(weights, axis=0, keepdims=True)
        weights = (weights * (1.0 / total)).astype(BF)
        if is_big:
            pbig[c, h, index] = weights
        else:
            ptrio[c, h, index] = weights
        outs.append(mm_tn(weights, v))
    mixed[rows, pl.ds(pl.multiple_of(c * 256, 256), 128)] = jnp.where(low, outs[0], outs[1]).astype(BF)
    mixed[rows, pl.ds(pl.multiple_of(c * 256 + 128, 128), 128)] = outs[2].astype(BF)


def attend(at, c, qkv, mixed, pbig, ptrio):
    mixed[SLOTS - 16 : SLOTS, pl.ds(pl.multiple_of(c * 256, 256), 256)] = jnp.zeros((16, 256), BF)
    segments(at, lambda first, is_big, i: attend_segment(c, first, is_big, i, qkv, mixed, pbig, ptrio))


def transpose_into(dst, src, tiles):
    def body(j):
        lanes = pl.ds(pl.multiple_of(j * 128, 128), 128)
        dst[lanes, :] = src[:, lanes].T

    loop(tiles, body)


def count_crops(labels, first_image):
    images = labels.shape[0]
    image = lax.broadcasted_iota(jnp.int32, labels.shape, 0)
    crop = labels - CROPS * (first_image + image)
    lane = lax.broadcasted_iota(jnp.int32, (images, 128), 1)
    offset = (IMAGE_LEN * lax.broadcasted_iota(jnp.int32, (images, 1), 0)).astype(F32)
    table = jnp.zeros((images, 128), F32)
    bigs = jnp.zeros((images, 1), F32)
    for p in range(CROPS):
        size = jnp.sum((crop == p).astype(F32), axis=1, keepdims=True)
        start = jnp.sum((crop < p).astype(F32), axis=1, keepdims=True) + offset
        big = (size == float(BIG_CROP)).astype(F32)
        at_lane = jnp.where(big > 0.5, bigs, 2.0 + float(p) - bigs)
        table = jnp.where(lane == at_lane.astype(jnp.int32), start, table)
        bigs = bigs + big
    return table


def slot_tokens(table, row, shape, dim):
    slot = lax.broadcasted_iota(jnp.int32, shape, dim)
    token = jnp.full(shape, -1, jnp.int32)
    at_big = (0, 2, 4, 5)[row]
    at_small = (0, 3, 6, 15)[row]
    for first, length, is_big, index in slot_segments(row // 2):
        if is_big:
            k = at_big + index
            start = table[k // 2 : k // 2 + 1, k % 2 : k % 2 + 1]
        else:
            k = at_small + index
            start = table[k // 8 : k // 8 + 1, 2 + k % 8 : 3 + k % 8]
        inside = jnp.logical_and(slot >= first, slot < first + length)
        token = jnp.where(inside, start.astype(jnp.int32) + (slot - first), token)
    return jnp.where(token < 0, -1, (token & 1) * TOK + (token >> 1))


def forward_kernel(
    x_in, g_in, labels, wq_in, wo_in, w1_in, w2_in, gains_in, biases_in,
    wq_h, wo_h, w1_h, w2_h, x_h, mid_h, a1t_h, a2t_h, mixt_h, qkv_h, pbig_h, ptrio_h, act_h, slope_h, cot_h, cott_h, out_h, where_h,
    wq, wo, w1, w2, tok, send_x, send_g, land_x, land_g, x, mid, midb, a1, a1t, a2t, mixed, mixt, qkv, pbig, ptrio,
    act, slope, cot, cott, gains, biases, fc1_bias, qkv_bias, tables, column, where, branch_two,
    zs, zr, xs, xr, ys, yr, ds, dr, cs, cr, exs, exr, egs, egr, tbs, tbr, hs,
):
    at = Place()
    refs = (wq, wo, w1, w2)
    sends = Sends()
    gather = Gather(at, refs, sends, FORWARD_DIRECT, zs, zr, xs, xr, ys, yr, ds, dr, cs, cr)
    stores = []

    def keep(src, dst):
        copy = pltpu.make_async_copy(src, dst, hs.at[len(stores)])
        copy.start()
        stores.append(copy)

    pairs = x_in.shape[0]
    wqv, wov = wq.reshape(4, 768, QW), wo.reshape(4, 1024, 192)
    w1v, w2v = w1.reshape(4, 768, 768), w2.reshape(4, 768, 768)
    groups = (at.c, at.cs, at.cx, at.cs + 2 - 4 * at.x)

    def joined(ref, first, count):
        return jnp.concatenate([ref[first + i : first + i + 1, :] for i in range(count)], axis=1)

    def start():
        tables[at.z] = jnp.zeros((8, 128), F32)
        tables[at.z, 0:3, :] = count_crops(labels[...], (at.y * 4 + at.z) * 3)
        heads = [wq_in[n].astype(BF) for n in range(3)]
        wq[at.c, at.z, at.y] = jnp.concatenate(
            [v[:, 0:128] for v in heads] + [v[:, 128:192] for v in heads] + [jnp.zeros((96, HALF), BF)], axis=1
        )
        wo[at.z, at.c, pl.ds(pl.multiple_of(at.y * 96, 32), 96), :] = wo_in[...].astype(BF)
        w1[at.c, at.z, at.y] = w1_in[...].astype(BF)
        w2[at.c, at.z, :, pl.ds(pl.multiple_of(at.y * 384, 128), 384)] = w2_in[...].astype(BF)
        at.enter()
        for k in (1, 2, 3):
            sends.start(tables.at[at.z], tables.at[at.z], tbs.at[k - 1], tbr.at[at.z], at.zth(lax.rem(at.z + k, 4)))

    def pick(n, send):
        for half in (0, 1):
            ref = x_in if n == 0 else g_in
            tok[n, half * TOK + TOK - 16 : half * TOK + TOK, :] = jnp.zeros((16, 192), BF)
            tok[n, half * TOK : half * TOK + pairs, :] = ref[:, half * 192 : half * 192 + 192]

        def block(r):
            one = (lax.broadcasted_iota(jnp.int32, (SLOTS, 2 * TOK), 1) == column[r]).astype(F32).astype(BF)
            value = mm(one, tok[n]).astype(BF)
            for i in range(SLOTS // CHUNK):
                put_block(send, r, i, value[i * CHUNK : i * CHUNK + CHUNK])

        loop(4, block)

    def pick_x():
        for k in (1, 2, 3):
            s = lax.rem(at.z + k, 4)
            arrived(tables.at[s], tbr.at[s], at.yn)
        table = tables[at.c]
        for r in range(4):
            column[r] = slot_tokens(table, r, (SLOTS, 1), 0)
            where[r] = slot_tokens(table, r, (1, SLOTS), 1)
        keep(where, where_h)
        pick(0, send_x)
        land_x[at.z] = send_x[at.z]
        wo[:, :, 192:256, :] = jnp.zeros((4, 4, 64, 192), BF)
        for n in (0, 1):
            gains[n : n + 1, :] = joined(gains_in, 6 * n, 6)
        for n in range(6):
            biases[n : n + 1, :] = joined(biases_in, 6 * n, 6)
        nothing = jnp.zeros((1, 128), F32)
        for c in range(4):
            fc1_bias[c] = joined(biases_in, 36 + 6 * c, 6)
            q = biases[2:3, c * 192 : c * 192 + 192]
            v = biases[3:4, c * 192 : c * 192 + 192]
            qkv_bias[c] = jnp.concatenate(
                [q[:, 0:128], nothing, v[:, 0:128], q[:, 128:192], nothing[:, 0:HALF], v[:, 128:192], nothing[:, 0:HALF]],
                axis=1,
            )

    def pick_g():
        pick(1, send_g)
        land_g[at.z] = send_g[at.z]

    def norm_one():
        def one(i, rows):
            value = get_blocks(land_x, i)
            x[rows, :] = value
            normed, _ = row_stats(value.astype(F32))
            a1[rows, :] = (normed * gains[0:1, :] + biases[0:1, :]).astype(BF)

        chunks(one)
        keep(x, x_h)

    def project(i):
        c = groups[i]
        for n in range(0, QW, 256):
            wide = min(256, QW - n)
            qkv[c, :, n : n + wide] = (mm(a1[...], wqv[c, :, n : n + wide]) + qkv_bias[c, :, n : n + wide]).astype(BF)

    def transpose_one():
        transpose_into(a1t, a1, 6)
        a1t[768:784, :] = jnp.ones((16, SLOTS), BF)
        keep(a1t, a1t_h)

    def branch():
        def one(z):
            midb[z] = mm(mixed[...], wov[z])

        loop(4, one)
        keep(qkv, qkv_h)
        keep(pbig, pbig_h)
        keep(ptrio, ptrio_h)

    def norm_two():
        def one(i, rows):
            value = x[rows, :].astype(F32) + jnp.concatenate([midb[r, rows, :] for r in range(4)], axis=1) + biases[4:5, :]
            mid[rows, :] = value
            normed, _ = row_stats(value)
            a1[rows, :] = (normed * gains[1:2, :] + biases[1:2, :]).astype(BF)

        chunks(one)
        keep(mid, mid_h)

    def expand(i):
        c = groups[i]

        def tile(n):
            lanes = pl.ds(pl.multiple_of(n * 256, 256), 256)
            hidden = mm(a1[...], w1v[c, :, lanes]) + fc1_bias[c, :, lanes]
            share = 0.5 + 0.5 * lax.erf(hidden * 0.7071067811865476)
            bell = jnp.exp(hidden * hidden * -0.5) * 0.3989422804014327
            act[c, :, lanes] = (hidden * share).astype(BF)
            slope[c, :, lanes] = (share + hidden * bell).astype(BF)

        loop(3, tile)
        keep(act.at[c], act_h.at[c])
        keep(slope.at[c], slope_h.at[c])

    def transpose_two():
        transpose_into(a2t, a1, 6)
        a2t[768:784, :] = jnp.ones((16, SLOTS), BF)
        keep(a2t, a2t_h)

    def transpose_mixed():
        transpose_into(mixt, mixed, 8)
        mixt[192:208, :] = jnp.ones((16, SLOTS), BF)
        keep(mixt, mixt_h)

    def join():
        def one(i, rows):
            cot[rows, :] = get_blocks(land_g, i)

        chunks(one)
        keep(cot, cot_h)

    def transpose_cot():
        transpose_into(cott, cot, 6)
        keep(cott, cott_h)

    def contract(i):
        c = groups[i]

        def tile(n):
            rows = pl.ds(pl.multiple_of(n * 256, 256), 256)
            part = mm_nt(act[c], w2v[c, rows, :])
            if i == 0:
                branch_two[:, rows] = part + biases[5:6, rows] + mid[:, rows]
            else:
                branch_two[:, rows] = branch_two[:, rows] + part

        loop(3, tile)

    def split():
        def one(i, rows):
            value = branch_two[rows, :].astype(BF)
            for r in range(4):
                put_block(land_x, r, i, value[:, r * 192 : r * 192 + 192])

        chunks(one)
        keep(land_x, out_h)

    def ready_b(p):
        gather.ready(p, 1)
        keep((wqv, wov, w1v, w2v)[p], (wq_h, wo_h, w1_h, w2_h)[p])

    steps = [start, pick_x, pick_g, norm_one, transpose_one, branch, norm_two, transpose_two, transpose_mixed, join]
    steps += [
        transpose_cot,
        split,
        lambda: exchange_start(at, sends, send_x, land_x, exs, exr),
        lambda: exchange_start(at, sends, send_g, land_g, egs, egr),
        lambda: exchange_wait(at, land_x, exr),
        lambda: exchange_wait(at, land_g, egr),
    ]
    for step in (project, lambda i: attend(at, groups[i], qkv, mixed, pbig, ptrio), expand, contract):
        steps += [functools.partial(step, i) for i in range(4)]
    for p in (WQ, WO, W1, W2):
        steps += [
            functools.partial(gather.own_across, p),
            functools.partial(gather.own_along, p),
            functools.partial(gather.corner, p),
            functools.partial(gather.ready, p, 0),
            functools.partial(ready_b, p),
        ]
        steps += [functools.partial(gather.along, p, j) for j in (1, 2, 3)]
        steps += [functools.partial(gather.cross, p, j) for j in range(4)]
    for number in FORWARD_ORDER:
        steps[number]()
    sends.drain()
    for copy in stores:
        copy.wait()


FORWARD_OUT = (
    ((4, 768, QW), BF), ((4, 1024, 192), BF), ((4, 768, 768), BF), ((4, 768, 768), BF),
    ((SLOTS, D), BF), ((SLOTS, D), F32), ((784, SLOTS), BF), ((784, SLOTS), BF), ((1024, SLOTS), BF),
    ((4, SLOTS, QW), BF), ((4, 3, 2, BIG_SLOTS, BIG_SLOTS), BF), ((4, 3, 3, TRIO_SLOTS, TRIO_SLOTS), BF),
    ((4, SLOTS, 768), BF), ((4, SLOTS, 768), BF), ((SLOTS, D), BF), ((D, SLOTS), BF), ((4, BLOCK, 128), BF),
    ((4, 1, SLOTS), jnp.int32),
)


def run_forward(*operands):
    sem = pltpu.SemaphoreType.DMA
    vmem = pltpu.VMEM
    return pl.pallas_call(
        forward_kernel,
        out_shape=[jax.ShapeDtypeStruct(s, t) for s, t in FORWARD_OUT],
        in_specs=[pl.BlockSpec(memory_space=vmem)] * len(operands),
        out_specs=[pl.BlockSpec(memory_space=pl.ANY)] * len(FORWARD_OUT),
        scratch_shapes=[
            vmem((4, 4, 2, 96, QW), BF), vmem((4, 4, 256, 192), BF), vmem((4, 4, 2, 96, 768), BF), vmem((4, 4, 192, 768), BF),
            vmem((2, 2 * TOK, 192), BF),
            vmem((4, BLOCK, 128), BF), vmem((4, BLOCK, 128), BF), vmem((4, BLOCK, 128), BF), vmem((4, BLOCK, 128), BF),
            vmem((SLOTS, D), BF), vmem((SLOTS, D), F32), vmem((4, SLOTS, 192), F32), vmem((SLOTS, D), BF),
            vmem((784, SLOTS), BF), vmem((784, SLOTS), BF), vmem((SLOTS, 1024), BF), vmem((1024, SLOTS), BF),
            vmem((4, SLOTS, QW), BF), vmem((4, 3, 2, BIG_SLOTS, BIG_SLOTS), BF), vmem((4, 3, 3, TRIO_SLOTS, TRIO_SLOTS), BF),
            vmem((4, SLOTS, 768), BF), vmem((4, SLOTS, 768), BF), vmem((SLOTS, D), BF), vmem((D, SLOTS), BF),
            vmem((2, D), F32), vmem((6, D), F32), vmem((4, 1, D), F32), vmem((4, 1, QW), F32), vmem((4, 8, 128), F32),
            vmem((4, SLOTS, 1), jnp.int32), vmem((4, 1, SLOTS), jnp.int32), vmem((SLOTS, D), F32),
            sem((4, 4)), sem((4, 4)), sem((4, 4)), sem((4, 4)), sem((4, 4)), sem((4, 4)), sem((4, 4)), sem((4, 4)),
            sem((4, 4)), sem((4, 4)), sem((3,)), sem((4,)), sem((3,)), sem((4,)), sem((3,)), sem((4,)), sem((len(FORWARD_OUT) + 6,)),
        ],
        compiler_params=pltpu.CompilerParams(collective_id=0, has_side_effects=True, vmem_limit_bytes=VMEM_LIMIT),
    )(*operands)


FORWARD_ORDER = (
    0, 33, 68, 44, 45, 32, 57, 1, 37, 49, 38, 52, 40, 39, 41, 12, 53, 50, 42, 61, 56, 54, 43, 51, 62, 2, 64, 35, 34,
    36, 55, 63, 69, 13, 65, 14, 76, 66, 46, 3, 17, 16, 47, 18, 67, 73, 19, 20, 21, 4, 48, 23, 58, 22, 74, 5, 6, 59,
    77, 60, 26, 78, 27, 75, 8, 24, 7, 25, 79, 28, 71, 29, 15, 9, 10, 70, 30, 72, 31, 11,
)
FORWARD_DIRECT = ()


def parts_of(ref, p, *lead, count=1):
    *outer, first = lead
    if p != W2:
        return ref.at[(*outer, first) if count == 1 else (*outer, pl.ds(first, count))]
    rows = pl.ds(pl.multiple_of(first * 192, 192), count * 192)
    return ref.at[(*outer[:-1], rows, pl.ds(pl.multiple_of(outer[-1] * 384, 128), 384))]


class Reduce:
    def __init__(self, at, sends, grads, pair, corner, cross, along, owned, squares, direct, sems):
        self.at, self.sends = at, sends
        self.grads, self.pair, self.corner, self.cross, self.along = grads, pair, corner, cross, along
        self.owned, self.squares, self.direct = owned, squares, direct
        self.ss, self.rs = sems

    def start(self, p, n, src, dst, peer, arrival=None, when=None):
        self.sends.start(src, dst, self.ss.at[p, n], self.rs.at[p, n if arrival is None else arrival], peer, when=when)

    def grad(self, p, c, y, s, count=1):
        return parts_of(self.grads[p], p, c, y, s, count=count)

    def half(self, ref, p, i, first):
        if p != W2:
            return ref.at[i, pl.ds(first, 2)]
        return ref.at[i, pl.ds(first * 192, 384)]

    def one(self, ref, p, i, s):
        return ref.at[i, s] if p != W2 else ref.at[i, pl.ds(pl.multiple_of(s * 192, 192), 192)]

    def far_and_near(self, i):
        return self.at.cx if i == 0 else self.at.c

    def pair_send(self, p, i):
        at = self.at
        c = 2 * ((1 - at.x) if i == 0 else at.x) + 1 - at.core
        self.start(p, i, self.grads[p].at[c], self.pair[p].at[i], at.cn)

    def add(self, count, pair):
        def one(s):
            mine, other = pair(s)
            mine[...] = mine[...] + other[...]

        loop(count, one)

    def add_pair(self, p, i, y):
        c = self.far_and_near(i)
        self.add(4, lambda s: (self.grad(p, c, y, s), parts_of(self.pair[p], p, i, y, s)))

    def far_sum(self, p):
        at = self.at
        arrived(self.pair[p].at[0], self.rs.at[p, 0], at.yn)
        self.add_pair(p, 0, 1 - at.y)
        self.start(p, 2, self.grad(p, at.cx, 1 - at.y, 0, 2), self.corner[p].at[0], at.xn)
        self.start(p, 3, self.grad(p, at.cx, 1 - at.y, 2, 2), self.corner[p].at[1], at.yn)
        self.add_pair(p, 0, at.y)
        self.start(p, 4, self.grad(p, at.cx, at.y, 0, 2), self.half(self.cross[p], p, 0, 0), at.xn)

    def near_sum(self, p):
        at = self.at
        arrived(self.pair[p].at[1], self.rs.at[p, 1], at.yn)
        self.add_pair(p, 1, 1 - at.y)
        self.start(p, 5, self.grad(p, at.c, 1 - at.y, 2, 2), self.half(self.cross[p], p, 1, 2), at.yn)
        self.add_pair(p, 1, at.y)

    def corner_a(self, p):
        at, corner = self.at, self.corner[p]
        arrived(corner.at[0], self.rs.at[p, 2], at.yn)
        self.add(2, lambda s: (self.grad(p, at.c, 1 - at.y, s), self.one(corner, p, 0, s)))
        self.start(p, 6, self.grad(p, at.c, 1 - at.y, 0, 2), self.half(self.cross[p], p, 1, 0), at.yn)

    def corner_b(self, p):
        at, corner = self.at, self.corner[p]
        arrived(corner.at[1], self.rs.at[p, 3], at.yn)
        self.add(2, lambda s: (self.grad(p, at.cx, at.y, s + 2), self.one(corner, p, 1, s)))
        self.start(p, 7, self.grad(p, at.cx, at.y, 2, 2), self.half(self.cross[p], p, 0, 2), at.xn)

    def cross_sum(self, p):
        at, cross = self.at, self.cross[p]
        for n, (i, first) in ((4, (0, 0)), (7, (0, 2)), (5, (1, 2)), (6, (1, 0))):
            arrived(self.half(cross, p, i, first), self.rs.at[p, n], at.yn)

        def one(s):
            mine = self.grad(p, at.c, at.y, s)
            mine[...] = mine[...] + self.one(cross, p, 0, s)[...] + self.one(cross, p, 1, s)[...]

        loop(4, one)
        line = self.along[p]

        def mine(s):
            return self.grad(p, at.c, at.y, s)

        if p in self.direct:
            for n in (1, 2, 3):
                s = at.other(n)
                self.start(p, 7 + n, mine(s), line.at[at.z], at.zth(s), arrival=8 + at.z)
            return
        end = jnp.logical_not(at.mid)
        near = jnp.where(at.mid, at.z - at.step, at.z + at.step)
        self.start(p, 8, mine(near), line.at[0], at.zth(near), arrival=8)
        for n in (2, 3):
            self.start(p, 7 + n, mine(at.other(n)), line.at[n], at.zth(near), arrival=8 + n, when=end)

    def line_sum(self, p):
        at, line = self.at, self.along[p]
        if p in self.direct:
            return

        @pl.when(at.mid)
        def _():
            for n in (2, 3):
                arrived(line.at[n], self.rs.at[p, 8 + n], at.yn)
                mine = self.grad(p, at.c, at.y, at.other(n - 1))
                mine[...] = mine[...] + line[n]

        for n in (2, 3):
            s = at.other(n - 1)
            self.start(p, 9 + n, self.grad(p, at.c, at.y, s), line.at[1], at.zth(s), arrival=9, when=at.mid)

    def along_sum(self, p):
        at, line = self.at, self.along[p]
        total = self.grad(p, at.c, at.y, at.z)[...].astype(F32)
        for n in (1, 2, 3) if p in self.direct else (0, 1):
            s = at.other(n) if p in self.direct else n
            arrived(line.at[s], self.rs.at[p, 8 + s], at.yn)
            total = total + line[s].astype(F32)
        self.owned[p][...] = total
        wide = total.shape[1]
        self.squares[:, 0:wide] = self.squares[:, 0:wide] + jnp.sum(total * total, axis=0, keepdims=True)


class Total:
    def __init__(self, at, sends, mine, line, plane, sems):
        self.at, self.sends, self.mine, self.line, self.plane = at, sends, mine, line, plane
        self.line_s, self.line_r, self.plane_s, self.plane_r, self.back_s, self.back_r = sems
        self.rows = line.shape[1]
        self.cut = mine.shape[0] != self.rows

    def part(self, ref, z):
        return ref.at[pl.ds(pl.multiple_of(z * self.rows, 8), self.rows)] if self.cut else ref

    def start(self):
        at = self.at
        self.line[at.z] = self.part(self.mine, at.z)[...]
        for k in (1, 2, 3):
            to = lax.rem(at.z + k, 4)
            self.sends.start(
                self.part(self.mine, to), self.line.at[at.z], self.line_s.at[k - 1], self.line_r.at[at.z], at.zth(to)
            )

    def spread(self):
        at = self.at
        for k in (1, 2, 3):
            s = lax.rem(at.z + k, 4)
            arrived(self.line.at[s], self.line_r.at[s], at.yn)
        me = at.y * 4 + at.c
        self.plane[me] = self.line[0] + self.line[1] + self.line[2] + self.line[3]
        for k in range(1, 8):
            to = lax.rem(me + k, 8)
            peer = (lax.div(to, 4), at.z, lax.rem(to, 4))
            self.sends.start(self.plane.at[me], self.plane.at[me], self.plane_s.at[k - 1], self.plane_r.at[me], peer)

    def collect(self):
        at = self.at
        me = at.y * 4 + at.c
        for k in range(1, 8):
            s = lax.rem(me + k, 8)
            arrived(self.plane.at[s], self.plane_r.at[s], at.yn)
        value = self.plane[0]
        for s in range(1, 8):
            value = value + self.plane[s]
        return value

    def share(self, whole):
        at = self.at
        mine = self.part(whole, at.z)
        mine[...] = self.collect()
        for k in (1, 2, 3):
            self.sends.start(mine, mine, self.back_s.at[k - 1], self.back_r.at[at.z], at.zth(lax.rem(at.z + k, 4)))

    def finish(self, whole):
        for k in (1, 2, 3):
            s = lax.rem(self.at.z + k, 4)
            arrived(self.part(whole, s), self.back_r.at[s], self.at.yn)


def fold(value):
    return value[0:8] + value[8:16] + value[16:24] + value[24:32]


def back_segment(c, slot, first, is_big, index, qkv, weights_big, weights_trio, mixed, grads):
    size = BIG_SLOTS if is_big else TRIO_SLOTS
    rows = pl.ds(first, size)
    q01 = qkv[c, rows, 0:128]
    k01 = qkv[c, rows, 128:256]
    v01 = qkv[c, rows, 256:384]
    kq2 = swap_halves(qkv[c, rows, 384:512])
    v2 = qkv[c, rows, 512:640]
    g01 = mixed[rows, pl.ds(pl.multiple_of(c * 256, 256), 128)]
    g2 = mixed[rows, pl.ds(pl.multiple_of(c * 256 + 128, 128), 128)]
    low = lane_low(size)
    none = jnp.zeros((size, 128), BF)
    dq, dk, dv = [], [], []
    for h, (g, gs, q, k, v) in enumerate((
        (g01, jnp.where(low, g01, none), q01, k01, v01),
        (g01, jnp.where(low, none, g01), q01, k01, v01),
        (g2, g2, kq2, kq2, v2),
    )):
        if is_big:
            weights = weights_big[slot, h, index]
        else:
            weights = weights_trio[slot, h, index]
        wide = weights.astype(F32)
        product = wide * mm_nt(v, gs)
        scores = (product - wide * jnp.sum(product, axis=0, keepdims=True)).astype(BF)
        dq.append(mm_tn(scores, k))
        dk.append(mm(scores, q))
        dv.append(mm(weights, g))
    scale = HEAD_DIM**-0.5
    grads[c, rows, 0:128] = (jnp.where(low, dq[0], dq[1]) * scale).astype(BF)
    grads[c, rows, 128:256] = (jnp.where(low, dk[0], dk[1]) * scale).astype(BF)
    grads[c, rows, 256:384] = jnp.where(low, dv[0], dv[1]).astype(BF)
    grads[c, rows, 384:512] = (jnp.where(low, dq[2], dk[2]) * scale).astype(BF)
    grads[c, rows, 512:640] = dv[2].astype(BF)


def backward_kernel(
    wq_h, wo_h, w1_h, w2_h, x_h, mid_h, a1t_h, a2t_h, mixt_h, qkv_h, pbig_h, ptrio_h, act_h, slope_h, cot_h, cott_h, out_h,
    gains_in,
    own_q, own_o, own_1, own_2, total, square_total, land_out, land_in,
    ring, wo, gq, go, g1, g2, pq, po, p1, p2, nq, no, n1, n2, rq, ro, r1, r2, lq, lo, l1, l2,
    act, slope, cot, cott, a2t, a1t, mixt, mid, x, pbig, ptrio, gmix, grad, half, send, gains, small, summed, squares, sums_of, line, plane, square_tile, square_line, square_plane,
    ss, rs, hs, ring_s, p_s, ex_s, ex_r, in_s, in_r, *total_sems,
):
    at = Place()
    sends = Sends()
    reduce = Reduce(
        at, sends, (gq, go, g1, g2), (pq, po, p1, p2), (nq, no, n1, n2), (rq, ro, r1, r2), (lq, lo, l1, l2),
        (own_q, own_o, own_1, own_2), squares, BACKWARD_DIRECT, (ss, rs),
    )
    loads = {}
    waited = []

    def load(name, src, dst):
        copy = pltpu.make_async_copy(src, dst, hs.at[len(loads) + len(waited)])
        copy.start()
        loads[name] = copy

    groups = (2 * (1 - at.x) + 1 - at.core, at.cx, at.cs, at.c)
    uses = [(ref, c) for ref in (w2_h, w1_h, wq_h) for c in groups]
    ring_copies = {}

    def ring_start(u):
        if u < len(uses):
            src, c = uses[u]
            wide = src.shape[2]
            copy = pltpu.make_async_copy(src.at[c], ring.at[u % 3, :, pl.ds(0, wide)], ring_s.at[u])
            copy.start()
            ring_copies[u] = copy

    def loaded(*names):
        for name in names:
            if name in loads:
                loads.pop(name).wait()
                waited.append(name)

    sums = Total(at, sends, small, line, plane, total_sems[:6])
    square_sum = Total(at, sends, square_tile, square_line, square_plane, total_sems[6:])
    keep_out = pltpu.make_async_copy(out_h.at[at.z], land_out.at[at.z], ex_s.at[3])
    keep_in = pltpu.make_async_copy(send.at[at.z], land_in.at[at.z], in_s.at[3])

    def start():
        load("cott", cott_h, cott)
        for i in range(4):
            load(f"act{i}", act_h.at[groups[i]], act.at[groups[i]])
        for u in range(3):
            ring_start(u)
        load("cot", cot_h, cot)
        for i in range(4):
            load(f"slope{i}", slope_h.at[groups[i]], slope.at[groups[i]])
        load("a2t", a2t_h, a2t)
        load("mid", mid_h, mid)
        load("mixt", mixt_h, mixt)
        load("wo", wo_h, wo)
        load("a1t", a1t_h, a1t)
        load("x", x_h, x)
        at_enter(at)
        squares[...] = jnp.zeros((1, D), F32)
        for n in (0, 1):
            gains[n : n + 1, :] = jnp.concatenate([gains_in[6 * n + i : 6 * n + i + 1, :] for i in range(6)], axis=1)

    def send_out():
        keep_out.start()
        exchange_start(at, sends, out_h, land_out, ex_s, ex_r)

    def grad_fc2(i):
        c = groups[i]
        loaded("cott", f"act{i}")

        def tile(n):
            lanes = pl.ds(pl.multiple_of(n * 256, 256), 256)
            g2[c, :, lanes] = mm(cott[...], act[c, :, lanes]).astype(BF)

        loop(3, tile)

    def grad_hidden(i):
        c = groups[i]
        loaded("cot", f"slope{i}")
        ring_copies[i].wait()

        def tile(n):
            lanes = pl.ds(pl.multiple_of(n * 256, 256), 256)
            slope[c, :, lanes] = (mm(cot[...], ring[i % 3, :, lanes]) * slope[c, :, lanes].astype(F32)).astype(BF)

        loop(3, tile)
        ring_start(i + 3)

    def rows_to_shards(dst, c, lanes, tile):
        for z in range(4):
            for y in range(2):
                first = (z * 2 + y) * 96
                dst[c, y, z, :, lanes] = tile[first : first + 96].astype(BF)

    def grad_fc1(i):
        c = groups[i]
        loaded("a2t")

        def tile(n):
            lanes = pl.ds(pl.multiple_of(n * 256, 256), 256)
            value = mm(a2t[...], slope[c, :, lanes])
            rows_to_shards(g1, c, lanes, value)
            sums_of[c, :, lanes] = value[768:769]

        loop(3, tile)

    def back_through(first_use, left, wide, i):
        u = first_use + i
        ring_copies[u].wait()

        part = mm_nt(left[groups[i], :, 0:wide], ring[u % 3, :, 0:wide])
        if i == 0:
            grad[...] = part
        else:
            grad[...] = grad[...] + part
        ring_start(u + 3)

    def put_row(first, value):
        for i in range(6):
            small[first + i : first + i + 1, :] = value[:, i * 128 : i * 128 + 128]

    def norm_two():
        loaded("mid")
        parts = [jnp.zeros((8, D), F32)] * 4

        def one(i, rows):
            normed, inverse = row_stats(mid[rows, :])
            upper = grad[rows, :]
            weighted = upper * gains[1:2, :]
            first = jnp.sum(weighted, axis=1, keepdims=True) * (1.0 / D)
            second = jnp.sum(weighted * normed, axis=1, keepdims=True) * (1.0 / D)
            straight = cot[rows, :].astype(F32)
            value = straight + inverse * (weighted - first - normed * second)
            mid[rows, :] = value
            branch = value.astype(BF)
            for r in range(4):
                half[r, rows, :] = branch[:, r * 192 : r * 192 + 192]
            for n, v in enumerate((upper * normed, upper, branch.astype(F32), straight)):
                parts[n] = parts[n] + fold(v)

        chunks(one)
        for first, value in zip((6, 18, 36, 42), parts):
            put_row(first, jnp.sum(value, axis=0, keepdims=True))

    def grad_out():
        loaded("mixt")

        def one(z):
            value = mm(mixt[...], half[z]).astype(BF)
            for c in range(4):
                for y in range(2):
                    go[c, y, z] = value[c * 256 + y * 96 : c * 256 + y * 96 + 96]

        loop(4, one)

    def grad_mixed():
        load("qkv", qkv_h, slope.at[:, :, pl.ds(0, QW)])
        loaded("wo")

        def one(c):
            rows = pl.ds(pl.multiple_of(c * 256, 256), 256)
            value = mm_nt(half[0], wo[0, rows, :])
            for z in (1, 2, 3):
                value = value + mm_nt(half[z], wo[z, rows, :])
            gmix[:, rows] = value.astype(BF)

        loop(4, one)
        for copy in fetch(0):
            copy.start()
        loaded("qkv")

    def fetch(i):
        c, slot = groups[i], i % 2
        return (
            pltpu.make_async_copy(pbig_h.at[c], pbig.at[slot], p_s.at[slot, 0]),
            pltpu.make_async_copy(ptrio_h.at[c], ptrio.at[slot], p_s.at[slot, 1]),
        )

    def attend_back(i):
        for copy in fetch(i):
            copy.wait()
        if i < 3:
            for copy in fetch(i + 1):
                copy.start()
        c = groups[i]
        act[c, SLOTS - 16 : SLOTS, 0:QW] = jnp.zeros((16, QW), BF)
        segments(
            at, lambda first, is_big, n: back_segment(c, i % 2, first, is_big, n, slope, pbig, ptrio, gmix, act)
        )

    def grad_q(i):
        c = groups[i]
        loaded("a1t")

        def tile(lanes):
            value = mm(a1t[...], act[c, :, lanes])
            rows_to_shards(gq, c, lanes, value)
            sums_of[4 + c, :, lanes] = value[768:769]

        loop(2, lambda n: tile(pl.ds(pl.multiple_of(n * 256, 256), 256)))
        tile(pl.ds(512, 128))

    def norm_one():
        loaded("x")
        parts = [jnp.zeros((8, D), F32)] * 2

        def one(i, rows):
            normed, inverse = row_stats(x[rows, :].astype(F32))
            upper = grad[rows, :]
            weighted = upper * gains[0:1, :]
            first = jnp.sum(weighted, axis=1, keepdims=True) * (1.0 / D)
            second = jnp.sum(weighted * normed, axis=1, keepdims=True) * (1.0 / D)
            value = (mid[rows, :] + inverse * (weighted - first - normed * second)).astype(BF)
            for r in range(4):
                put_block(send, r, i, value[:, r * 192 : r * 192 + 192])
            for n, v in enumerate((upper * normed, upper)):
                parts[n] = parts[n] + fold(v)

        chunks(one)
        for first, value in zip((0, 12), parts):
            put_row(first, jnp.sum(value, axis=0, keepdims=True))

    def send_in():
        exchange_start(at, sends, send, land_in, in_s, in_r)
        keep_in.start()

    def start_total():
        for c in range(4):
            put_row(48 + 6 * c, sums_of[c])
        packed = [sums_of[4 + c] for c in range(4)]
        for first, lanes in ((24, (0, 384)), (30, (256, 512))):
            parts = []
            for value in packed:
                parts += [value[:, lanes[0] : lanes[0] + 128], value[:, lanes[1] : lanes[1] + HALF]]
            put_row(first, jnp.concatenate(parts, axis=1))
        small[72:96, :] = jnp.zeros((24, 128), F32)
        sums.start()

    def finish_total():
        sums.finish(summed)
        total[...] = summed[...]

    def start_squares():
        value = squares[:, 0:128]
        for i in range(1, 6):
            value = value + squares[:, i * 128 : i * 128 + 128]
        square_tile[...] = jnp.zeros((8, 128), F32)
        square_tile[0:1, :] = value
        square_sum.start()

    def finish_squares():
        square_total[...] = square_sum.collect()

    def wait_exchanges():
        exchange_wait(at, land_out, ex_r)
        exchange_wait(at, land_in, in_r)
        keep_out.wait()
        keep_in.wait()

    steps = [start, send_out, norm_two, grad_out, grad_mixed, norm_one, send_in, start_total, sums.spread]
    steps += [lambda: sums.share(summed), finish_total, start_squares, square_sum.spread, finish_squares, wait_exchanges]
    through_fc1 = functools.partial(back_through, 4, slope, 768)
    through_q = functools.partial(back_through, 8, act, QW)
    for step in (grad_fc2, grad_hidden, grad_fc1, through_fc1, attend_back, grad_q, through_q):
        steps += [functools.partial(step, i) for i in range(4)]
    for p in (WQ, WO, W1, W2):
        steps += [functools.partial(reduce.pair_send, p, 0), functools.partial(reduce.pair_send, p, 1)]
        for step in (
            reduce.far_sum, reduce.near_sum, reduce.corner_a, reduce.corner_b, reduce.cross_sum, reduce.line_sum, reduce.along_sum
        ):
            steps.append(functools.partial(step, p))
    for number in BACKWARD_ORDER:
        steps[number]()
    sends.drain()


def at_enter(at):
    barrier = pltpu.get_barrier_semaphore()
    me = at.y * 4 + at.c
    peers = [at.zth(lax.rem(at.z + k, 4)) for k in (1, 2, 3)]
    for k in range(1, 8):
        to = lax.rem(me + k, 8)
        peers.append((lax.div(to, 4), at.z, lax.rem(to, 4)))
    for peer in peers:
        pl.semaphore_signal(barrier, inc=1, device_id=peer, device_id_type=MESH)
    pl.semaphore_wait(barrier, len(peers))


SHARDS = ((96, QW), (96, 192), (96, 768), (192, 384))


def run_backward(*operands):
    sem = pltpu.SemaphoreType.DMA
    vmem = pltpu.VMEM
    shape = jax.ShapeDtypeStruct
    stages = [(4, 2, 4), (2, 2, 4), (2, 2), (2, 4), (4,)]
    matrices = [(4, 768, 768), (2, 768, 768), (2, 384, 384), (2, 768, 384), (4, 192, 384)]
    return pl.pallas_call(
        backward_kernel,
        out_shape=[shape(s, F32) for s in SHARDS] + [shape((96, 128), F32), shape((8, 128), F32)] + [shape((4, BLOCK, 128), BF)] * 2,
        in_specs=[pl.BlockSpec(memory_space=pl.ANY)] * (len(operands) - 1) + [pl.BlockSpec(memory_space=vmem)],
        out_specs=[pl.BlockSpec(memory_space=vmem)] * 6 + [pl.BlockSpec(memory_space=pl.ANY)] * 2,
        scratch_shapes=[vmem((3, 768, 768), BF), vmem((4, 1024, 192), BF)]
        + [
            vmem(whole if s == SHARDS[W2] else lead + s, BF) for lead, whole in zip(stages, matrices) for s in SHARDS
        ]
        + [
            vmem((4, SLOTS, 768), BF), vmem((4, SLOTS, 768), BF), vmem((SLOTS, D), BF), vmem((D, SLOTS), BF),
            vmem((784, SLOTS), BF), vmem((784, SLOTS), BF), vmem((1024, SLOTS), BF), vmem((SLOTS, D), F32),
            vmem((SLOTS, D), BF), vmem((2, 3, 2, BIG_SLOTS, BIG_SLOTS), BF), vmem((2, 3, 3, TRIO_SLOTS, TRIO_SLOTS), BF),
            vmem((SLOTS, 1024), BF), vmem((SLOTS, D), F32), vmem((4, SLOTS, 192), BF), vmem((4, BLOCK, 128), BF),
            vmem((2, D), F32), vmem((96, 128), F32), vmem((96, 128), F32), vmem((1, D), F32), vmem((8, 1, D), F32),
            vmem((4, 24, 128), F32), vmem((8, 24, 128), F32), vmem((8, 128), F32), vmem((4, 8, 128), F32), vmem((8, 8, 128), F32),
            sem((4, 13)), sem((4, 13)), sem((18,)), sem((12,)), sem((2, 2)), sem((4,)), sem((4,)), sem((4,)), sem((4,)),
        ]
        + [sem((n,)) for n in (3, 4, 7, 8, 3, 4)] * 2,
        compiler_params=pltpu.CompilerParams(collective_id=1, has_side_effects=True, vmem_limit_bytes=VMEM_LIMIT),
    )(*operands)


BACKWARD_ORDER = (
    0, 19, 15, 1, 20, 18, 17, 70, 16, 21, 22, 72, 71, 23, 27, 26, 28, 29, 73, 30, 25, 61, 74, 75, 24, 2, 62, 4, 64,
    63, 31, 76, 77, 32, 33, 39, 40, 34, 41, 42, 5, 6, 66, 65, 35, 43, 36, 37, 44, 45, 38, 78, 46, 47, 3, 67, 53, 48,
    68, 52, 54, 55, 49, 50, 7, 56, 57, 58, 59, 51, 69, 8, 60, 11, 9, 12, 10, 13, 14,
)
BACKWARD_DIRECT = ()


RATES = (D**-0.5, (D // 24) ** -0.5, D**-0.5, FF**-0.5, 0.3, 0.3)
ROWS = 208


def update_kernel(
    own_q, own_o, own_1, own_2, total, square_total, land_out, land_in, where,
    wq, wo, w1, w2, wg, wb, mq, mo, m1, m2, mg, mb, vq, vo, v1, v2, vg, vb,
    out, grad_in, norm,
    nmq, nvq, nwq, hq, nmo, nvo, nwo, ho, nm1, nv1, nw1, h1, nm2, nv2, nw2, h2, nmg, nvg, nwg, hg, nmb, nvb, nwb, hb,
    blocks,
):
    gains = total[0:12, :]
    biases = total[12:72, :]
    squares = jnp.sum(jnp.sum(square_total[...], axis=0, keepdims=True), axis=1, keepdims=True)
    for part in (gains, biases):
        squares = squares + jnp.sum(jnp.sum(part * part, axis=0, keepdims=True), axis=1, keepdims=True)
    size = jnp.sqrt(squares)
    norm[...] = size
    factor = jnp.minimum(1.0, CLIP_NORM / size)

    def step(rate, grad, pick, refs):
        weight, first, second, new_first, new_second, new_weight, half = refs
        results = adam_step(weight[pick], grad, first[pick], second[pick], rate, factor)
        for ref, value in zip((new_first, new_second, new_weight, half), results):
            ref[pick] = value

    everything = (slice(None), slice(None))
    packed = own_q[...]
    for n in range(3):
        grad = jnp.concatenate([packed[:, 128 * n : 128 * n + 128], packed[:, 384 + HALF * n : 448 + HALF * n]], axis=1)
        step(RATES[0], grad, n, (wq, mq, vq, nmq, nvq, nwq, hq))
    step(RATES[1], own_o[...], everything, (wo, mo, vo, nmo, nvo, nwo, ho))
    step(RATES[2], own_1[...], everything, (w1, m1, v1, nm1, nv1, nw1, h1))
    step(RATES[3], own_2[...], everything, (w2, m2, v2, nm2, nv2, nw2, h2))
    step(RATES[4], gains, everything, (wg, mg, vg, nmg, nvg, nwg, hg))
    step(RATES[5], biases, everything, (wb, mb, vb, nmb, nvb, nwb, hb))

    pairs = out.shape[0]
    for n, land in enumerate((land_out, land_in)):
        for r in range(4):
            for i in range(SLOTS // CHUNK):
                rows = slice(r * SLOTS + i * CHUNK, r * SLOTS + i * CHUNK + CHUNK)
                rest = land[r, SLOTS + i * 16 : SLOTS + i * 16 + 16, :]
                blocks[rows, n * 192 : n * 192 + 128] = land[r, i * CHUNK : i * CHUNK + CHUNK, :]
                blocks[rows, n * 192 + 128 : n * 192 + 192] = jnp.concatenate([rest[:, 0:HALF], rest[:, HALF:]], axis=0)
    for first in range(0, pairs, ROWS):
        count = min(ROWS, pairs - first)
        halves = []
        for half in (0, 1):
            token = half * TOK + first + lax.broadcasted_iota(jnp.int32, (ROWS, SLOTS), 0)
            one = jnp.concatenate([(token == where[r]).astype(F32).astype(BF) for r in range(4)], axis=1)
            halves.append(mm(one, blocks[...])[0:count])
        for ref, lanes in ((out, 0), (grad_in, 192)):
            even, odd = (value[:, lanes : lanes + 192] for value in halves)
            ref[first : first + count, 0, :] = jnp.concatenate([even, odd], axis=1)


def run_update(pairs, *operands):
    shape = jax.ShapeDtypeStruct
    shapes = [shape((pairs, 1, 384), F32)] * 2 + [shape((1, 1), F32)]
    for weight in operands[9:15]:
        shapes += [shape(weight.shape, F32)] * 3 + [shape(weight.shape, BF)]
    return pl.pallas_call(
        update_kernel,
        out_shape=shapes,
        in_specs=[pl.BlockSpec(memory_space=pltpu.VMEM)] * len(operands),
        out_specs=[pl.BlockSpec(memory_space=pltpu.VMEM)] * len(shapes),
        scratch_shapes=[pltpu.VMEM((4 * SLOTS, 384), BF)],
        compiler_params=pltpu.CompilerParams(vmem_limit_bytes=VMEM_LIMIT),
    )(*operands)


def prepare(layer_in, grad_out, crop_ids, w_qkv, w_out, w_fc1, w_fc2, norm_gains, all_biases):
    pairs = layer_in.shape[0]
    return (
        layer_in.reshape(pairs, 384), grad_out.reshape(pairs, 384), crop_ids.reshape(-1, IMAGE_LEN),
        w_qkv.transpose(1, 0, 2), w_out, w_fc1, w_fc2.T, norm_gains.reshape(12, 128), all_biases.reshape(60, 128),
    )


def local_fast(
    layer_in, grad_out, crop_ids, w_qkv, w_out, w_fc1, w_fc2, norm_gains, all_biases,
    first_qkv, second_qkv, first_out, second_out, first_fc1, second_fc1, first_fc2, second_fc2,
    first_gains, second_gains, first_biases, second_biases,
):
    pairs = layer_in.shape[0]
    operands = prepare(layer_in, grad_out, crop_ids, w_qkv, w_out, w_fc1, w_fc2, norm_gains, all_biases)
    *kept, where = run_forward(*operands)
    reduced = run_backward(*kept, operands[7])
    masters = operands[3:9]
    results = run_update(
        pairs, *reduced, where, *masters,
        first_qkv.transpose(1, 0, 2), first_out, first_fc1, first_fc2.T,
        first_gains.reshape(12, 128), first_biases.reshape(60, 128),
        second_qkv.transpose(1, 0, 2), second_out, second_fc1, second_fc2.T,
        second_gains.reshape(12, 128), second_biases.reshape(60, 128),
    )
    return (
        results[0], results[1], results[2].reshape(()),
        *[v.transpose(1, 0, 2) for v in results[3:7]], *results[7:15], *[v.T for v in results[15:19]],
        *[v.reshape(-1) for v in results[19:27]],
    )


def dot(a, b):
    return jnp.dot(a, b, preferred_element_type=F32)


def dot_nt(a, b):
    return lax.dot_general(a, b, (((1,), (1,)), ((), ())), preferred_element_type=F32)


def dot_tn(a, b):
    return lax.dot_general(a, b, (((0,), (0,)), ((), ())), preferred_element_type=F32)


def norm_stats(value):
    centre = jnp.mean(value, axis=1, keepdims=True)
    centred = value - centre
    spread = jnp.mean(centred * centred, axis=1, keepdims=True)
    inverse = lax.rsqrt(spread + NORM_EPS)
    return centred * inverse, inverse


def norm_back(grad, normed, inverse, gain):
    weighted = grad * gain
    first = jnp.mean(weighted, axis=1, keepdims=True)
    second = jnp.mean(weighted * normed, axis=1, keepdims=True)
    return inverse * (weighted - first - normed * second)


def layer(x, cot, crops, w_qkv, w_out, w_fc1, w_fc2, gains, biases):
    inputs = x.astype(F32)
    cotf = cot.astype(F32)
    normed_one, inverse_one = norm_stats(inputs)
    act_one = (normed_one * gains[:D] + biases[:D]).astype(BF)
    qkv_bias = jnp.concatenate([biases[2 * D : 3 * D], jnp.zeros((D,), F32), biases[3 * D : 4 * D]])
    qkv = (dot(act_one, w_qkv) + qkv_bias).astype(BF)
    heads = qkv.reshape(SLOTS, 3, HEADS, HEAD_DIM)
    q, k, v = heads[:, 0], heads[:, 1], heads[:, 2]
    scores = jnp.einsum("qhd,khd->hqk", q, k, preferred_element_type=F32) * HEAD_DIM ** (-0.5)
    scores = jnp.where((crops[:, None] == crops[None, :])[None], scores, MASKED)
    probs = jax.nn.softmax(scores, axis=2)
    half_probs = probs.astype(BF)
    mixed = jnp.einsum("hqk,khd->qhd", half_probs, v, preferred_element_type=F32)
    mixed = mixed.reshape(SLOTS, D).astype(BF)
    middle = inputs + dot(mixed, w_out) + biases[4 * D : 5 * D]
    normed_two, inverse_two = norm_stats(middle)
    act_two = (normed_two * gains[D:] + biases[D : 2 * D]).astype(BF)
    hidden = dot(act_two, w_fc1) + biases[6 * D :]
    active, gelu_pull = jax.vjp(lambda h: jax.nn.gelu(h, approximate=False), hidden)
    active = active.astype(BF)
    out = middle + dot(active, w_fc2) + biases[5 * D : 6 * D]

    g_fc2 = dot_tn(active, cot)
    grad_hidden = gelu_pull(dot_nt(cot, w_fc2))[0].astype(BF)
    g_fc1 = dot_tn(act_two, grad_hidden)
    grad_two = dot_nt(grad_hidden, w_fc1)
    grad_middle = cotf + norm_back(grad_two, normed_two, inverse_two, gains[D:])
    branch = grad_middle.astype(BF)
    g_out = dot_tn(mixed, branch)
    grad_mixed = dot_nt(branch, w_out).astype(BF).reshape(SLOTS, HEADS, HEAD_DIM)
    grad_probs = jnp.einsum("qhd,khd->hqk", grad_mixed, v, preferred_element_type=F32)
    grad_scores = (probs * (grad_probs - jnp.sum(probs * grad_probs, axis=2, keepdims=True))).astype(BF)
    scale = HEAD_DIM ** (-0.5)
    grad_q = jnp.einsum("hqk,khd->qhd", grad_scores, k, preferred_element_type=F32) * scale
    grad_k = jnp.einsum("hqk,qhd->khd", grad_scores, q, preferred_element_type=F32) * scale
    grad_v = jnp.einsum("hqk,qhd->khd", half_probs, grad_mixed, preferred_element_type=F32)
    grad_qkv = jnp.stack([grad_q, grad_k, grad_v], axis=1).astype(BF).reshape(SLOTS, 3 * D)
    g_qkv = dot_tn(act_one, grad_qkv)
    grad_one = dot_nt(grad_qkv, w_qkv)
    grad_in = grad_middle + norm_back(grad_one, normed_one, inverse_one, gains[:D])

    g_gains = jnp.concatenate([jnp.sum(grad_one * normed_one, axis=0), jnp.sum(grad_two * normed_two, axis=0)])
    qkv_sums = jnp.sum(grad_qkv.astype(F32), axis=0)
    g_biases = jnp.concatenate([
        jnp.sum(grad_one, axis=0),
        jnp.sum(grad_two, axis=0),
        qkv_sums[:D],
        qkv_sums[2 * D :],
        jnp.sum(branch.astype(F32), axis=0),
        jnp.sum(cotf, axis=0),
        jnp.sum(grad_hidden.astype(F32), axis=0),
    ])
    return out, grad_in, g_qkv, g_out, g_fc1, g_fc2, g_gains, g_biases


def adam_step(weight, grad, first, second, rate, factor):
    clipped = grad * factor
    new_first = BETA_ONE * first + (1.0 - BETA_ONE) * clipped
    new_second = BETA_TWO * second + (1.0 - BETA_TWO) * clipped * clipped
    unbiased_first = new_first / (1.0 - BETA_ONE**STEP)
    unbiased_second = new_second / (1.0 - BETA_TWO**STEP)
    new_weight = weight - rate * (
        unbiased_first / (jnp.sqrt(unbiased_second) + ADAM_EPS) + DECAY * weight
    )
    return (new_first, new_second, new_weight, new_weight.astype(BF))


def gather(value, axes):
    for name, dim in axes:
        value = lax.all_gather(value, name, axis=dim, tiled=True)
    return value


def scatter(value, axes):
    for name, dim in axes:
        value = lax.psum_scatter(value, name, scatter_dimension=dim, tiled=True)
    return value.astype(F32)


def local_plain(
    layer_in, grad_out, crop_ids, w_qkv, w_out, w_fc1, w_fc2, norm_gains, all_biases,
    first_qkv, second_qkv, first_out, second_out, first_fc1, second_fc1, first_fc2, second_fc2,
    first_gains, second_gains, first_biases, second_biases,
):
    row = lax.axis_index("row")
    n_row, n_col = lax.axis_size("row"), lax.axis_size("col")
    feat = D // n_row
    pairs = layer_in.shape[0]
    labels = lax.ppermute(
        crop_ids, ("row", "col"), [(r * n_col + c, c * n_row + r) for r in range(n_row) for c in range(n_col)]
    )
    sources = slot_sources(labels).reshape(-1)
    place = jnp.where(sources < 0, -1, (sources % 2) * pairs + sources // 2)
    pick = (place[:, None] == jnp.arange(2 * pairs, dtype=jnp.int32)[None, :]).astype(BF)

    def to_slots(value):
        halves = jnp.concatenate([value[:, 0, :feat], value[:, 0, feat:]], axis=0)
        sent = dot(pick, halves).astype(BF)
        got = lax.all_to_all(sent, "row", 0, 0, tiled=True)
        return got.reshape(n_row, SLOTS, feat).transpose(1, 0, 2).reshape(SLOTS, D)

    def to_tokens(value):
        sent = value.astype(BF).reshape(SLOTS, n_row, feat).transpose(1, 0, 2).reshape(n_row * SLOTS, feat)
        got = lax.all_to_all(sent, "row", 0, 0, tiled=True)
        halves = dot_tn(pick, got)
        return jnp.concatenate([halves[:pairs], halves[pairs:]], axis=1).reshape(pairs, 1, 2 * feat)

    full_qkv = gather(w_qkv.astype(BF), (("dp", 0), ("row", 0), ("col", 2))).reshape(D, 3 * D)
    full_out = gather(w_out.astype(BF), (("dp", 0), ("col", 0), ("row", 1)))
    full_fc1 = gather(w_fc1.astype(BF), (("dp", 0), ("row", 0), ("col", 1)))
    full_fc2 = gather(w_fc2.astype(BF), (("dp", 0), ("col", 0), ("row", 1)))
    crops = jnp.where(row < 2, slot_crops(0), slot_crops(1))
    out, grad_in, g_qkv, g_out, g_fc1, g_fc2, g_gains, g_biases = layer(
        to_slots(layer_in), to_slots(grad_out), crops, full_qkv, full_out, full_fc1, full_fc2, norm_gains, all_biases
    )
    owned_qkv = scatter(g_qkv.astype(BF).reshape(D, 3, D), (("col", 2), ("row", 0), ("dp", 0)))
    owned_out = scatter(g_out.astype(BF), (("row", 1), ("col", 0), ("dp", 0)))
    owned_fc1 = scatter(g_fc1.astype(BF), (("col", 1), ("row", 0), ("dp", 0)))
    owned_fc2 = scatter(g_fc2.astype(BF), (("row", 1), ("col", 0), ("dp", 0)))
    local_squares = (
        jnp.sum(owned_qkv * owned_qkv)
        + jnp.sum(owned_out * owned_out)
        + jnp.sum(owned_fc1 * owned_fc1)
        + jnp.sum(owned_fc2 * owned_fc2)
    )
    grad_gains, grad_biases, weight_squares = lax.psum((g_gains, g_biases, local_squares), ("dp", "row", "col"))
    grad_norm = jnp.sqrt(weight_squares + jnp.sum(grad_gains * grad_gains) + jnp.sum(grad_biases * grad_biases))
    factor = jnp.minimum(1.0, CLIP_NORM / grad_norm)
    upd_qkv = adam_step(w_qkv, owned_qkv, first_qkv, second_qkv, D ** (-0.5), factor)
    upd_out = adam_step(w_out, owned_out, first_out, second_out, (D // 24) ** (-0.5), factor)
    upd_fc1 = adam_step(w_fc1, owned_fc1, first_fc1, second_fc1, D ** (-0.5), factor)
    upd_fc2 = adam_step(w_fc2, owned_fc2, first_fc2, second_fc2, FF ** (-0.5), factor)
    upd_gains = adam_step(norm_gains, grad_gains, first_gains, second_gains, 0.3, factor)
    upd_biases = adam_step(all_biases, grad_biases, first_biases, second_biases, 0.3, factor)
    return (
        to_tokens(out), to_tokens(grad_in), grad_norm,
        *upd_qkv, *upd_out, *upd_fc1, *upd_fc2, *upd_gains, *upd_biases,
    )


def solution(mesh):
    tokens = P(("dp", "col"), "row", None)
    qkv = P(("row", "dp"), None, "col")
    out = P(("col", "dp"), "row")
    fc1 = P(("row", "dp"), "col")
    whole = P()
    return jax.shard_map(
        local_fast if mesh.shape["dp"] == 2 else local_plain,
        mesh=mesh,
        in_specs=(
            tokens, tokens, P(("dp", "row")), qkv, out, fc1, out, whole, whole,
            qkv, qkv, out, out, fc1, fc1, out, out, whole, whole, whole, whole,
        ),
        out_specs=(tokens, tokens, whole) + (qkv,) * 4 + (out,) * 4 + (fc1,) * 4 + (out,) * 4 + (whole,) * 8,
        check_vma=False,
    )
```
